32 devices in a mesh: grp: 4 (over y, x), row: 8 (over z, core).
Axes of the slice: x: 2, y: 2, z: 4, core: 2. Of those that a mesh axis runs over, the one named last changes fastest.
Arguments:
- snapshots: bfloat16 [8192, 32768], P(None, ('grp', 'row')), may hold values from -8 to 8
- weights: float32 [32768], P(('grp', 'row')), may hold values from 0.25 to 4
- reference_field: float32 [32768], P(('grp', 'row')), may hold values from -6 to 6
- start_basis: float32 [64, 2, 63, 8], replicated, may hold values from -6 to 6
Outputs:
- spod_modes: float32 [64, 16, 32768], P(None, None, ('grp', 'row'))
- energies: float32 [64, 8], replicated
The draws below stay inside these ranges and needn't reach their ends.
All inputs are finite; a program needn't handle non-finite values.
Results may differ from the reference program's by a relative error of at most 0.012.
The reference program's roundings to bfloat16 on the way count: a program that leaves them out, or rounds other values in their place, can miss the bound.
Values may be sent and summed in bfloat16 or wider, within the bound.
No kernel may reach another device: no remote copies, remote signals or barrier semaphores. Data moves between devices by JAX's collectives and lax.ppermute only.
A program may use at most 192 MiB of HBM per device.

```python
import math
import jax
import jax.numpy as jnp
from jax import lax

NFFT = 256
NBLK = 63
NF = 64
NM = 8
ITERS = 12
ROW_DEV = 1024
NT = 8192
NROWS = 32768


def draw_snapshots(key, part):
    shape_count = 32
    key_time, key_shape, key_noise = jax.random.split(jax.random.fold_in(key, 7), 3)
    energy_levels = jnp.sqrt(0.15 * 0.85 ** jnp.arange(shape_count, dtype=jnp.float32))
    position = jnp.arange(NROWS, dtype=jnp.float32) / NROWS
    envelope = 0.6 + 1.2 * position
    temporal = jax.random.normal(key_time, (NT, shape_count), jnp.float32) * energy_levels
    spatial = jax.random.normal(key_shape, (shape_count, NROWS), jnp.float32)
    noise = 0.6 * jax.random.normal(key_noise, (NT, NROWS), jnp.float32)
    field = jnp.dot(temporal, spatial * envelope) + noise
    return jnp.clip(field, -8.0, 8.0).astype(jnp.bfloat16)


def block_levels(stream_key, shape, shards, low, top_value):
    def one(dim, parts):
        steps = jax.random.uniform(jax.random.fold_in(jax.random.fold_in(stream_key, 6), dim), (parts,), jnp.float32, low / len(shards), top_value / len(shards))
        return jnp.repeat(jnp.exp(steps), shape[dim] // parts).reshape((-1,) + (1,) * (len(shape) - dim - 1))

    loudness = one(*shards[0])
    for cut in shards[1:]:
        loudness = loudness * one(*cut)
    return loudness


def bell_draw(key, extent, spread, reach, pieces=(), kind=jnp.bfloat16):
    drawn = spread * jax.random.normal(key, extent, jnp.float32)
    if pieces:
        drawn = drawn * block_levels(key, extent, pieces, -0.22, 0.18)
    return jnp.clip(drawn, -reach, reach).astype(kind)


def setup_inputs(seed: int = 0) -> dict:
    key_list = jax.random.split(jax.random.key(seed), 5)
    snapshots = draw_snapshots(jax.random.fold_in(key_list[4], 71), 0)
    weights = jnp.clip(jnp.exp(math.log(4.0) - 2.7725887 * jax.random.uniform(key_list[1], (NROWS,), jnp.float32) ** block_levels(key_list[1], (NROWS,), ((0, 32),), -0.2, 0.2)), 0.25, 4.0)
    reference_field = bell_draw(key_list[2], (NROWS,), 1.0, 6.0, ((0, 32),), jnp.float32)
    start_basis = bell_draw(key_list[3], (NF, 2, NBLK, NM), 1.0, 6.0, (), jnp.float32)
    return dict(snapshots=snapshots, weights=weights, reference_field=reference_field, start_basis=start_basis)


highest = lax.Precision.HIGHEST

def dft_table():
    time_steps = jnp.arange(NFFT, dtype=jnp.int32)
    freq_bins = jnp.arange(1, NF + 1, dtype=jnp.int32)
    wrapped = freq_bins[:, None] * time_steps[None, :] % NFFT
    angles = 2.0 * math.pi / NFFT * wrapped.astype(jnp.float32)
    window_taper = 0.5 - 0.5 * jnp.cos(2.0 * math.pi / NFFT * time_steps.astype(jnp.float32))
    scaled_taper = window_taper / jnp.sqrt(jnp.sum(window_taper * window_taper))
    stacked = jnp.stack([jnp.cos(angles), -jnp.sin(angles)]) * scaled_taper[None, None, :]
    return stacked.astype(jnp.bfloat16)

def transform(rows_block, root_weight, dft_rows):
    half_len = NFFT // 2
    hop_rows = rows_block.reshape(NBLK + 1, half_len, rows_block.shape[1]).astype(jnp.float32)
    table_wide = dft_rows.astype(jnp.float32)
    leading = jnp.einsum('pft,htx->fphx', table_wide[:, :, :half_len], hop_rows[:NBLK], precision=highest)
    trailing = jnp.einsum('pft,htx->fphx', table_wide[:, :, half_len:], hop_rows[1:], precision=highest)
    return ((leading + trailing) * root_weight).astype(jnp.bfloat16)

def apply_gram(gram_real, gram_imag, basis_real, basis_imag):
    image_real = jnp.einsum('fbc,fck->fbk', gram_real, basis_real, precision=highest) - jnp.einsum('fbc,fck->fbk', gram_imag, basis_imag, precision=highest)
    image_imag = jnp.einsum('fbc,fck->fbk', gram_real, basis_imag, precision=highest) + jnp.einsum('fbc,fck->fbk', gram_imag, basis_real, precision=highest)
    return (image_real, image_imag)

def orthonormalize(image_real, image_imag):
    cols_real = []
    cols_imag = []
    for column in range(image_real.shape[2]):
        target_real = image_real[:, :, column]
        target_imag = image_imag[:, :, column]
        for earlier in range(column):
            prior_real = cols_real[earlier]
            prior_imag = cols_imag[earlier]
            inner_real = lax.optimization_barrier(jnp.sum(prior_real * target_real + prior_imag * target_imag, axis=1, keepdims=True))
            inner_imag = lax.optimization_barrier(jnp.sum(prior_real * target_imag - prior_imag * target_real, axis=1, keepdims=True))
            target_real, target_imag = (target_real - (inner_real * prior_real - inner_imag * prior_imag), target_imag - (inner_real * prior_imag + inner_imag * prior_real))
        length = jnp.sqrt(lax.optimization_barrier(jnp.sum(target_real * target_real + target_imag * target_imag, axis=1, keepdims=True)) + 1e-06)
        cols_real.append(target_real / length)
        cols_imag.append(target_imag / length)
    return (jnp.stack(cols_real, axis=2), jnp.stack(cols_imag, axis=2))

def subspace_solve(gram_real, gram_imag, start_basis):

    def sweep_once(sweep_index, current):
        image_real, image_imag = apply_gram(gram_real, gram_imag, current[0], current[1])
        return orthonormalize(image_real, image_imag)
    basis_real, basis_imag = lax.fori_loop(0, ITERS, sweep_once, (start_basis[:, 0], start_basis[:, 1]))
    image_real, image_imag = apply_gram(gram_real, gram_imag, basis_real, basis_imag)
    energy = lax.optimization_barrier(jnp.sum(basis_real * image_real + basis_imag * image_imag, axis=1))
    return (basis_real, basis_imag, energy)

def coefficient_matrix(basis_real, basis_imag):
    round_real = basis_real.astype(jnp.bfloat16)
    round_imag = basis_imag.astype(jnp.bfloat16)
    upper_half = jnp.concatenate([round_real, round_imag], axis=2)
    lower_half = jnp.concatenate([-round_imag, round_real], axis=2)
    return jnp.stack([upper_half, lower_half], axis=1)

def phase_turn(correlation, energy):
    gain_scale = 1.0 / jnp.sqrt(energy + 1e-06)
    tilt_real = gain_scale * correlation[:, :NM]
    tilt_imag = gain_scale * correlation[:, NM:]
    tilt_size = jnp.sqrt(jnp.maximum(tilt_real * tilt_real + tilt_imag * tilt_imag, 0.25))
    return (gain_scale * tilt_real / tilt_size, -gain_scale * tilt_imag / tilt_size)

def finish(projected, factor_real, factor_imag, root_weight):
    part_real = projected[:, :NM]
    part_imag = projected[:, NM:]
    inverse_root = 1.0 / root_weight
    out_real = (part_real * factor_real[:, :, None] - part_imag * factor_imag[:, :, None]) * inverse_root
    out_imag = (part_real * factor_imag[:, :, None] + part_imag * factor_real[:, :, None]) * inverse_root
    return jnp.concatenate([out_real, out_imag], axis=1)

def reference(snapshots, weights, reference_field, start_basis):
    dft_rows = dft_table()
    block_count = NROWS // ROW_DEV
    root_all = jnp.sqrt(weights)
    probe_all = (root_all * reference_field).astype(jnp.bfloat16)
    indices = jnp.arange(block_count, dtype=jnp.int32)

    def block_coeffs(block_index):
        first_row = block_index * ROW_DEV
        rows_block = lax.dynamic_slice_in_dim(snapshots, first_row, ROW_DEV, 1)
        root_block = lax.dynamic_slice_in_dim(root_all, first_row, ROW_DEV, 0)
        probe_block = lax.dynamic_slice_in_dim(probe_all, first_row, ROW_DEV, 0)
        return (transform(rows_block, root_block, dft_rows), root_block, probe_block)

    def gram_step(current, block_index):
        coeffs, root_block, probe_block = block_coeffs(block_index)
        coeffs_wide = coeffs.astype(jnp.float32)
        real_part = jnp.einsum('fpbx,fpcx->fbc', coeffs_wide, coeffs_wide, precision=highest)
        cross_part = jnp.einsum('fbx,fcx->fbc', coeffs_wide[:, 0], coeffs_wide[:, 1], precision=highest)
        gram_real = current[0] + real_part
        gram_imag = current[1] + (cross_part - jnp.swapaxes(cross_part, 1, 2))
        correlation = current[2] + jnp.einsum('fpbx,x->fpb', coeffs_wide, probe_block.astype(jnp.float32), precision=highest)
        return ((gram_real, gram_imag, correlation), None)
    zeros_gram = jnp.zeros((NF, NBLK, NBLK), jnp.float32)
    totals, leftover = lax.scan(gram_step, (zeros_gram, zeros_gram, jnp.zeros((NF, 2, NBLK), jnp.float32)), indices)
    gram_real = totals[0] / NROWS
    gram_imag = totals[1] / NROWS
    projection = totals[2] / math.sqrt(NROWS)
    basis_real, basis_imag, energy = subspace_solve(gram_real, gram_imag, start_basis)
    coef_matrix = coefficient_matrix(basis_real, basis_imag)
    coef_wide = coef_matrix.astype(jnp.float32)
    correlation = jnp.einsum('fpb,fpbk->fk', projection, coef_wide, precision=highest)
    factor_real, factor_imag = phase_turn(correlation, energy)

    def mode_block(block_index):
        coeffs, root_block, probe_block = block_coeffs(block_index)
        projected = jnp.einsum('fpbk,fpbx->fkx', coef_wide, coeffs.astype(jnp.float32), precision=highest)
        return finish(projected, factor_real, factor_imag, root_block)
    mode_blocks = lax.map(mode_block, indices)
    spod_modes = jnp.transpose(mode_blocks, (1, 2, 0, 3)).reshape(NF, 2 * NM, NROWS)
    return (spod_modes, energy)
```

```python
import functools
import math

import jax
import jax.numpy as jnp
import numpy as np
from jax import lax
from jax.experimental import pallas as pl
from jax.experimental.pallas import tpu as pltpu
from jax.sharding import PartitionSpec as P

NFFT = 256
HALF = NFFT // 2
NBLK = 63
NB = 64
NF = 64
NM = 8
ITERS = 12
EPS = 1e-06
LANES = 128
VMEM_LIMIT = 56 * 1024 * 1024

highest = lax.Precision.HIGHEST


def dft_table():
    time_steps = np.arange(NFFT, dtype=np.int32)
    freq_bins = np.arange(1, NF + 1, dtype=np.int32)
    wrapped = freq_bins[:, None] * time_steps[None, :] % NFFT
    angles = np.float32(2.0 * math.pi / NFFT) * wrapped.astype(np.float32)
    taper = np.float32(0.5) - np.float32(0.5) * np.cos(
        np.float32(2.0 * math.pi / NFFT) * time_steps.astype(np.float32)
    )
    taper = taper / np.sqrt(np.sum(taper * taper))
    stacked = np.concatenate([np.cos(angles), -np.sin(angles)]) * taper[None, :]
    return jnp.asarray(stacked, dtype=jnp.float32).astype(jnp.bfloat16)


class Plan:
    def __init__(self, grp, row):
        self.grp, self.row, self.deep = grp, row, row // 2
        self.split_grp = NF % (grp * row) == 0
        self.g_slots = grp if self.split_grp else 1
        self.owners = row * self.g_slots
        self.per = NF // self.owners

    def first_freq(self, core_slot, grp_slot, z_slot):
        row_index = lax.axis_index("row")
        core = (row_index & 1) ^ core_slot
        deep = (row_index >> 1) ^ z_slot
        owner = deep * 2 + core
        if self.split_grp:
            owner = (lax.axis_index("grp") ^ grp_slot) * self.row + owner
        return owner * self.per


def lane_index(shape):
    return lax.broadcasted_iota(jnp.int32, shape, 1)


def row_index_of(shape):
    return lax.broadcasted_iota(jnp.int32, shape, 0)


def transform_kernel(plan, snap_ref, root_ref, probe_ref, table_ref, coef_ref, keep_ref, send_ref, flip, gram):
    step = pl.program_id(0)
    tile = snap_ref.shape[1]
    pieces = tile // LANES
    table = table_ref[...]
    root = root_ref[...]

    def one_block(b, carry):
        rows = snap_ref[pl.ds(pl.multiple_of(b * HALF, HALF), NFFT), :]
        out = jnp.dot(table, rows, preferred_element_type=jnp.float32) * root
        for part in range(2):
            for piece in range(pieces):
                flip[piece, pl.ds(part * NB + b, NF, stride=2 * NB), :] = out[
                    part * NF : (part + 1) * NF, piece * LANES : (piece + 1) * LANES
                ]
        return carry

    lax.fori_loop(0, NBLK, one_block, 0, unroll=3)
    for piece in range(pieces):
        probe = probe_ref[:, piece * LANES : (piece + 1) * LANES]
        flip[piece, pl.ds(NB - 1, NF, stride=2 * NB), :] = jnp.broadcast_to(probe, (NF, LANES))
        flip[piece, pl.ds(2 * NB - 1, NF, stride=2 * NB), :] = jnp.zeros((NF, LANES), jnp.float32)

    @pl.when(step == 0)
    def _():
        gram[...] = jnp.zeros_like(gram)

    def one_freq(f, carry):
        base = pl.multiple_of(f * 2 * NB, 2 * NB)
        wide = jnp.concatenate([flip[piece, pl.ds(base, 2 * NB), :] for piece in range(pieces)], axis=1)
        coefs = wide.astype(jnp.bfloat16)
        coef_ref[f] = coefs
        gram[f] += lax.dot_general(
            coefs, coefs, (((1,), (1,)), ((), ())), preferred_element_type=jnp.float32
        )
        return carry

    lax.fori_loop(0, NF, one_freq, 0, unroll=4)

    @pl.when(step == pl.num_programs(0) - 1)
    def _():
        upper = row_index_of((NB, LANES)) < lane_index((NB, LANES))
        left = lane_index((NB // 2, LANES)) < NB

        def pack(f):
            top = gram[f, :NB, :]
            low = gram[f, NB:, :]
            real = top + pltpu.roll(low, NB, 1)
            imag = pltpu.roll(top, NB, 1) - low
            packed = jnp.where(upper, imag, real)
            return jnp.where(left, packed[: NB // 2], pltpu.roll(packed[NB // 2 :], NB, 1))

        for core_slot, out_ref in ((0, keep_ref), (1, send_ref)):

            def one_slot(slot, carry):
                first = plan.first_freq(core_slot, slot // plan.deep, slot % plan.deep)
                for j in range(plan.per):
                    out_ref[slot * plan.per + j] = pack(first + j)
                return carry

            lax.fori_loop(0, plan.g_slots * plan.deep, one_slot, 0)


def transform(plan, snapshots, root_weight, probe):
    rows_here = snapshots.shape[1]
    tile = min(256, rows_here)
    half_freqs = NF // 2
    packed = jax.ShapeDtypeStruct((half_freqs, NB // 2, LANES), jnp.float32)
    packed_spec = pl.BlockSpec((half_freqs, NB // 2, LANES), lambda i: (0, 0, 0))
    return pl.pallas_call(
        functools.partial(transform_kernel, plan),
        grid=(rows_here // tile,),
        in_specs=[
            pl.BlockSpec((snapshots.shape[0], tile), lambda i: (0, i)),
            pl.BlockSpec((1, tile), lambda i: (0, i)),
            pl.BlockSpec((1, tile), lambda i: (0, i)),
            pl.BlockSpec((2 * NF, NFFT), lambda i: (0, 0)),
        ],
        out_specs=[
            pl.BlockSpec((NF, 2 * NB, tile), lambda i: (0, 0, i)),
            packed_spec,
            packed_spec,
        ],
        out_shape=[
            jax.ShapeDtypeStruct((NF, 2 * NB, rows_here), jnp.bfloat16),
            packed,
            packed,
        ],
        scratch_shapes=[
            pltpu.VMEM((tile // LANES, NF * 2 * NB, LANES), jnp.float32),
            pltpu.VMEM((NF, 2 * NB, LANES), jnp.float32),
        ],
        compiler_params=pltpu.CompilerParams(vmem_limit_bytes=VMEM_LIMIT),
        name="transform",
    )(snapshots, root_weight[None], probe[None], dft_table())


def solve_kernel(plan, total_rows, packed_ref, start_ref, out_ref):
    lane = lane_index((NB, LANES))
    row = row_index_of((NB, LANES))
    col = lane & (NB - 1)
    left = lane < NB
    inside = (row < NBLK) & (col < NBLK)
    lane8 = lane_index((NM, LANES))
    row8 = row_index_of((NM, LANES))
    left8 = lane8 < NB

    systems, probes, basis = [], [], []
    for i in range(plan.per):
        folded = packed_ref[i]
        turned = pltpu.roll(folded, NB, 1)
        wide = jnp.concatenate([folded, turned], axis=0)
        twice = jnp.where(left, wide, pltpu.roll(wide, NB, 1))
        flipped = jnp.transpose(jnp.concatenate([twice, twice], axis=0))[:NB]
        real = jnp.where(inside, jnp.where(row >= col, twice, flipped), 0.0) / total_rows
        imag = jnp.where(row < col, twice, jnp.where(row > col, -flipped, 0.0))
        imag = jnp.where(inside, imag, 0.0) / total_rows
        systems.append(
            jnp.concatenate([jnp.where(left, real, -imag), jnp.where(left, imag, real)], axis=0)
        )
        along = twice[NB - 1 :]
        across = flipped[NB - 1 :]
        left1 = lane_index((1, LANES)) < NB
        probes.append((jnp.where(left1, along, across), jnp.where(left1, -across, along)))
        basis.append(start_ref[i])

    def image_of(i, v):
        return jnp.dot(v, systems[i], precision=highest, preferred_element_type=jnp.float32)

    def lane_sum(x):
        return jnp.sum(x, axis=1, keepdims=True)

    def orthonormalize(y):
        swapped = pltpu.roll(y, NB, 1)
        turned = jnp.where(left8, -swapped, swapped)
        v = jnp.zeros_like(y)
        for j in range(NM):
            pivot = jnp.broadcast_to(y[j : j + 1], y.shape)
            pivot_turned = jnp.broadcast_to(turned[j : j + 1], y.shape)
            size = lane_sum(pivot * pivot) + EPS
            v = jnp.where(row8 == j, pivot * lax.rsqrt(size), v)
            if j < NM - 1:
                inner_real = lane_sum(pivot * y)
                inner_imag = lane_sum(pivot_turned * y)
                inverse = 1.0 / size
                later = row8 > j
                a = jnp.where(later, inner_real * inverse, 0.0)
                c = jnp.where(later, inner_imag * inverse, 0.0)
                y, turned = (
                    y - (a * pivot + c * pivot_turned),
                    turned - (a * pivot_turned - c * pivot),
                )
        return v

    def sweep(index, current):
        images = [image_of(i, v) for i, v in enumerate(current)]
        return tuple(orthonormalize(y) for y in images)

    basis = lax.fori_loop(0, ITERS, sweep, tuple(basis))
    extras = jnp.zeros((NM, LANES), jnp.float32)
    scale = 1.0 / math.sqrt(total_rows)
    for i, v in enumerate(basis):
        energy = lane_sum(v * image_of(i, v))
        coef = v.astype(jnp.bfloat16).astype(jnp.float32)
        out_ref[i * NM : (i + 1) * NM] = coef
        gain = 1.0 / jnp.sqrt(energy + EPS)
        tilt_real = gain * (lane_sum(coef * probes[i][0]) * scale)
        tilt_imag = gain * (lane_sum(coef * probes[i][1]) * scale)
        size = jnp.sqrt(jnp.maximum(tilt_real * tilt_real + tilt_imag * tilt_imag, 0.25))
        extras = jnp.where(lane8 == 3 * i, gain * tilt_real / size, extras)
        extras = jnp.where(lane8 == 3 * i + 1, -gain * tilt_imag / size, extras)
        extras = jnp.where(lane8 == 3 * i + 2, energy, extras)
    out_ref[plan.per * NM :] = extras


def solve(plan, total_rows, packed, start):
    return pl.pallas_call(
        functools.partial(solve_kernel, plan, total_rows),
        out_shape=jax.ShapeDtypeStruct(((plan.per + 1) * NM, LANES), jnp.float32),
        compiler_params=pltpu.CompilerParams(vmem_limit_bytes=VMEM_LIMIT),
        name="solve",
    )(packed, start)


def modes_kernel(plan, coef_ref, pay_ref, root_ref, out_ref, energy_ref):
    inverse_root = 1.0 / root_ref[...]
    left = lane_index((NM, LANES)) < NB
    lane8 = lane_index((NM, LANES))
    slots = plan.owners

    def one_slot(slot, energies):
        core_slot = slot // (plan.g_slots * plan.deep)
        rest = slot % (plan.g_slots * plan.deep)
        first = plan.first_freq(core_slot, rest // plan.deep, rest % plan.deep)
        for j in range(plan.per):
            f = first + j
            c = pay_ref[slot, j * NM : (j + 1) * NM, :]
            matrix = jnp.concatenate([jnp.where(left, c, -c), pltpu.roll(c, NB, 1)], axis=0)
            extras = pay_ref[slot, plan.per * NM :, :]
            factor_real = extras[:, 3 * j : 3 * j + 1]
            factor_imag = extras[:, 3 * j + 1 : 3 * j + 2]
            projected = jnp.dot(
                matrix.astype(jnp.bfloat16), coef_ref[f], preferred_element_type=jnp.float32
            )
            real = projected[:NM]
            imag = projected[NM:]
            out_ref[f, :NM, :] = (real * factor_real - imag * factor_imag) * inverse_root
            out_ref[f, NM:, :] = (real * factor_imag + imag * factor_real) * inverse_root
            energies = jnp.where(lane8 == f, extras[:, 3 * j + 2 : 3 * j + 3], energies)
        return energies

    energies = lax.fori_loop(0, slots, one_slot, jnp.zeros((NM, LANES), jnp.float32), unroll=2)
    square = jnp.concatenate([energies] + [jnp.zeros_like(energies)] * (LANES // NM - 1), axis=0)
    energy_ref[...] = jnp.transpose(square)[:NF, :NM]


def modes(plan, coeffs, payload, root_weight):
    rows_here = coeffs.shape[2]
    tile = min(256, rows_here)
    return pl.pallas_call(
        functools.partial(modes_kernel, plan),
        grid=(rows_here // tile,),
        in_specs=[
            pl.BlockSpec((NF, 2 * NB, tile), lambda i: (0, 0, i)),
            pl.BlockSpec(payload.shape, lambda i: (0, 0, 0)),
            pl.BlockSpec((1, tile), lambda i: (0, i)),
        ],
        out_specs=[
            pl.BlockSpec((NF, 2 * NM, tile), lambda i: (0, 0, i)),
            pl.BlockSpec((NF, NM), lambda i: (0, 0)),
        ],
        out_shape=[
            jax.ShapeDtypeStruct((NF, 2 * NM, rows_here), jnp.float32),
            jax.ShapeDtypeStruct((NF, NM), jnp.float32),
        ],
        compiler_params=pltpu.CompilerParams(vmem_limit_bytes=VMEM_LIMIT),
        name="modes",
    )(coeffs, payload, root_weight[None])


def swap(x, axis, size, offset):
    return lax.ppermute(x, axis, [(i, i ^ offset) for i in range(size)])


def shards(plan, snapshots, weights, reference_field, start_basis):
    total_rows = snapshots.shape[1] * plan.grp * plan.row
    root_weight = jnp.sqrt(weights)
    probe = (root_weight * reference_field).astype(jnp.bfloat16).astype(jnp.float32)
    start = lax.dynamic_slice_in_dim(start_basis, plan.first_freq(0, 0, 0), plan.per, 0)
    start = jnp.pad(start, ((0, 0), (0, 0), (0, NB - NBLK), (0, 0)))
    start = jnp.transpose(start, (0, 3, 1, 2)).reshape(plan.per, NM, 2 * NB)

    coeffs, keep, send = transform(plan, snapshots, root_weight, probe)

    held = keep + swap(send, "row", plan.row, 1)
    if plan.split_grp:
        held = held.reshape((plan.grp, plan.deep * plan.per) + held.shape[1:])
        arrived = [swap(held[d], "grp", plan.grp, d) for d in range(1, plan.grp)]
        held = functools.reduce(jnp.add, arrived, held[0])
    held = held.reshape((plan.deep, plan.per) + held.shape[1:])
    arrived = [swap(held[d], "row", plan.row, 2 * d) for d in range(1, plan.deep)]
    held = functools.reduce(jnp.add, arrived, held[0])
    if not plan.split_grp:
        held = lax.psum(held, "grp")

    payload = solve(plan, total_rows, held, start)

    payload = jnp.stack(
        [payload] + [swap(payload, "row", plan.row, 2 * d) for d in range(1, plan.deep)]
    )
    if plan.split_grp:
        payload = jnp.concatenate(
            [payload] + [swap(payload, "grp", plan.grp, d) for d in range(1, plan.grp)]
        )
    payload = jnp.concatenate([payload, swap(payload, "row", plan.row, 1)])
    return tuple(modes(plan, coeffs, payload, root_weight))


def solution(mesh):
    plan = Plan(mesh.shape["grp"], mesh.shape["row"])
    in_specs = (P(None, ("grp", "row")), P(("grp", "row")), P(("grp", "row")), P())
    out_specs = (P(None, None, ("grp", "row")), P())
    return jax.shard_map(
        functools.partial(shards, plan),
        mesh=mesh,
        in_specs=in_specs,
        out_specs=out_specs,
        check_vma=False,
    )
```

```python
import functools
import math

import jax
import jax.numpy as jnp
import numpy as np
from jax import lax
from jax.experimental import pallas as pl
from jax.experimental.pallas import tpu as pltpu
from jax.sharding import PartitionSpec as P

NFFT = 256
HALF = NFFT // 2
NBLK = 63
NB = 64
NF = 64
NM = 8
ITERS = 12
EPS = 1e-06
LANES = 128
PITCH = 2 * NB + 1
VMEM_LIMIT = 56 * 1024 * 1024


def dft_table():
    time_steps = np.arange(NFFT, dtype=np.int32)
    freq_bins = np.arange(1, NF + 1, dtype=np.int32)
    wrapped = freq_bins[:, None] * time_steps[None, :] % NFFT
    angles = np.float32(2.0 * math.pi / NFFT) * wrapped.astype(np.float32)
    taper = np.float32(0.5) - np.float32(0.5) * np.cos(
        np.float32(2.0 * math.pi / NFFT) * time_steps.astype(np.float32)
    )
    taper = taper / np.sqrt(np.sum(taper * taper))
    stacked = np.concatenate([np.cos(angles), -np.sin(angles)]) * taper[None, :]
    return jnp.asarray(stacked, dtype=jnp.float32).astype(jnp.bfloat16)


class Plan:
    def __init__(self, grp, row):
        self.grp, self.row, self.deep = grp, row, row // 2
        self.split_grp = NF % (grp * row) == 0
        self.g_slots = grp if self.split_grp else 1
        self.owners = row * self.g_slots
        self.per = NF // self.owners

    def first_freq(self, core_slot, grp_slot, z_slot):
        row_index = lax.axis_index("row")
        core = (row_index & 1) ^ core_slot
        deep = (row_index >> 1) ^ z_slot
        owner = deep * 2 + core
        if self.split_grp:
            owner = (lax.axis_index("grp") ^ grp_slot) * self.row + owner
        return owner * self.per


def lane_index(shape):
    return lax.broadcasted_iota(jnp.int32, shape, 1)


def row_index_of(shape):
    return lax.broadcasted_iota(jnp.int32, shape, 0)


def transform_kernel(plan, snap_ref, root_ref, probe_ref, table_ref, coef_ref, keep_ref, send_ref, flip, gram):
    step = pl.program_id(0)
    tile = snap_ref.shape[1]
    pieces = tile // LANES
    table = table_ref[...]
    root = root_ref[...]

    def one_block(b, carry):
        rows = snap_ref[pl.ds(pl.multiple_of(b * HALF, HALF), NFFT), :]
        out = jnp.dot(table, rows, preferred_element_type=jnp.float32) * root
        for part in range(2):
            for piece in range(pieces):
                flip[piece, pl.ds(part * NB + b, NF, stride=PITCH), :] = out[
                    part * NF : (part + 1) * NF, piece * LANES : (piece + 1) * LANES
                ]
        return carry

    lax.fori_loop(0, NBLK, one_block, 0, unroll=21)
    for piece in range(pieces):
        probe = probe_ref[:, piece * LANES : (piece + 1) * LANES]
        flip[piece, pl.ds(NB - 1, NF, stride=PITCH), :] = jnp.broadcast_to(probe, (NF, LANES))
        flip[piece, pl.ds(2 * NB - 1, NF, stride=PITCH), :] = jnp.zeros((NF, LANES), jnp.float32)

    @pl.when(step == 0)
    def _():
        gram[...] = jnp.zeros_like(gram)

    def one_freq(f, carry):
        wide = jnp.concatenate(
            [flip[piece, pl.ds(f * PITCH, 2 * NB), :] for piece in range(pieces)], axis=1
        )
        coefs = wide.astype(jnp.bfloat16)
        coef_ref[f] = coefs
        gram[f] += lax.dot_general(
            coefs, coefs, (((1,), (1,)), ((), ())), preferred_element_type=jnp.float32
        )
        return carry

    lax.fori_loop(0, NF, one_freq, 0, unroll=16)

    @pl.when(step == pl.num_programs(0) - 1)
    def _():
        upper = row_index_of((NB, LANES)) < lane_index((NB, LANES))
        left = lane_index((NB // 2, LANES)) < NB

        def pack(f):
            top = gram[f, :NB, :]
            low = gram[f, NB:, :]
            real = top + pltpu.roll(low, NB, 1)
            imag = pltpu.roll(top, NB, 1) - low
            packed = jnp.where(upper, imag, real)
            return jnp.where(left, packed[: NB // 2], pltpu.roll(packed[NB // 2 :], NB, 1))

        for core_slot, out_ref in ((0, keep_ref), (1, send_ref)):

            def one_slot(slot, carry):
                first = plan.first_freq(core_slot, slot // plan.deep, slot % plan.deep)
                for j in range(plan.per):
                    out_ref[slot * plan.per + j] = pack(first + j)
                return carry

            lax.fori_loop(0, plan.g_slots * plan.deep, one_slot, 0, unroll=4)


def transform(plan, snapshots, root_weight, probe):
    rows_here = snapshots.shape[1]
    tile = min(256, rows_here)
    half_freqs = NF // 2
    packed = jax.ShapeDtypeStruct((half_freqs, NB // 2, LANES), jnp.float32)
    packed_spec = pl.BlockSpec((half_freqs, NB // 2, LANES), lambda i: (0, 0, 0))
    return pl.pallas_call(
        functools.partial(transform_kernel, plan),
        grid=(rows_here // tile,),
        in_specs=[
            pl.BlockSpec((snapshots.shape[0], tile), lambda i: (0, i)),
            pl.BlockSpec((1, tile), lambda i: (0, i)),
            pl.BlockSpec((1, tile), lambda i: (0, i)),
            pl.BlockSpec((2 * NF, NFFT), lambda i: (0, 0)),
        ],
        out_specs=[
            pl.BlockSpec((NF, 2 * NB, tile), lambda i: (0, 0, i)),
            packed_spec,
            packed_spec,
        ],
        out_shape=[
            jax.ShapeDtypeStruct((NF, 2 * NB, rows_here), jnp.bfloat16),
            packed,
            packed,
        ],
        scratch_shapes=[
            pltpu.VMEM((tile // LANES, NF * PITCH, LANES), jnp.float32),
            pltpu.VMEM((NF, 2 * NB, LANES), jnp.float32),
        ],
        compiler_params=pltpu.CompilerParams(vmem_limit_bytes=VMEM_LIMIT),
        name="transform",
    )(snapshots, root_weight[None], probe[None], dft_table())


def split_three(x):
    high = x.astype(jnp.bfloat16)
    rest = x - high.astype(jnp.float32)
    middle = rest.astype(jnp.bfloat16)
    low = (rest - middle.astype(jnp.float32)).astype(jnp.bfloat16)
    return high, middle, low


def solve_kernel(plan, total_rows, packed_ref, start_ref, out_ref):
    lane = lane_index((NB, LANES))
    row = row_index_of((NB, LANES))
    col = lane & (NB - 1)
    left = lane < NB
    inside = (row < NBLK) & (col < NBLK)
    lane8 = lane_index((NM, LANES))
    row8 = row_index_of((NM, LANES))
    left8 = lane8 < NB

    systems, probes, basis = [], [], []
    for i in range(plan.per):
        folded = packed_ref[i]
        turned = pltpu.roll(folded, NB, 1)
        wide = jnp.concatenate([folded, turned], axis=0)
        twice = jnp.where(left, wide, pltpu.roll(wide, NB, 1))
        flipped = jnp.transpose(jnp.concatenate([twice, twice], axis=0))[:NB]
        real = jnp.where(inside, jnp.where(row >= col, twice, flipped), 0.0) / total_rows
        imag = jnp.where(row < col, twice, jnp.where(row > col, -flipped, 0.0))
        imag = jnp.where(inside, imag, 0.0) / total_rows
        system = jnp.concatenate([jnp.where(left, real, -imag), jnp.where(left, imag, real)], axis=0)
        high, middle, low = split_three(system)
        systems.append(
            jnp.concatenate(
                [
                    jnp.concatenate([high, low], axis=1),
                    jnp.concatenate([middle, jnp.zeros_like(low)], axis=1),
                ],
                axis=0,
            )
        )
        along = twice[NB - 1 :]
        across = flipped[NB - 1 :]
        left1 = lane_index((1, LANES)) < NB
        probes.append((jnp.where(left1, along, across), jnp.where(left1, -across, along)))
        basis.append(start_ref[i])

    def image_of(i, v):
        high, middle, low = split_three(v)
        zeros = jnp.zeros_like(high)
        parts = jnp.concatenate(
            [
                jnp.concatenate([high, high], axis=1),
                jnp.concatenate([middle, middle], axis=1),
                jnp.concatenate([low, zeros], axis=1),
                jnp.concatenate([zeros, zeros], axis=1),
            ],
            axis=0,
        )
        out = jnp.dot(parts, systems[i], preferred_element_type=jnp.float32)
        small = out[:NM, LANES:] + out[2 * NM : 3 * NM, :LANES]
        return out[:NM, :LANES] + (out[NM : 2 * NM, :LANES] + small)

    def lane_sum(x):
        return jnp.sum(x, axis=1, keepdims=True)

    def orthonormalize(y):
        swapped = pltpu.roll(y, NB, 1)
        turned = jnp.where(left8, -swapped, swapped)
        v = jnp.zeros_like(y)
        for j in range(NM):
            pivot = jnp.broadcast_to(y[j : j + 1], y.shape)
            pivot_turned = jnp.broadcast_to(turned[j : j + 1], y.shape)
            size = lane_sum(pivot * pivot) + EPS
            v = jnp.where(row8 == j, pivot * lax.rsqrt(size), v)
            if j < NM - 1:
                inner_real = lane_sum(pivot * y)
                inner_imag = lane_sum(pivot_turned * y)
                inverse = 1.0 / size
                later = row8 > j
                a = jnp.where(later, inner_real * inverse, 0.0)
                c = jnp.where(later, inner_imag * inverse, 0.0)
                y, turned = (
                    y - (a * pivot + c * pivot_turned),
                    turned - (a * pivot_turned - c * pivot),
                )
        return v

    def sweep(index, current):
        images = [image_of(i, v) for i, v in enumerate(current)]
        return tuple(orthonormalize(y) for y in images)

    basis = lax.fori_loop(0, ITERS, sweep, tuple(basis))
    extras = jnp.zeros((NM, LANES), jnp.float32)
    scale = 1.0 / math.sqrt(total_rows)
    for i, v in enumerate(basis):
        energy = lane_sum(v * image_of(i, v))
        coef = v.astype(jnp.bfloat16).astype(jnp.float32)
        out_ref[i * NM : (i + 1) * NM] = coef
        gain = 1.0 / jnp.sqrt(energy + EPS)
        tilt_real = gain * (lane_sum(coef * probes[i][0]) * scale)
        tilt_imag = gain * (lane_sum(coef * probes[i][1]) * scale)
        size = jnp.sqrt(jnp.maximum(tilt_real * tilt_real + tilt_imag * tilt_imag, 0.25))
        extras = jnp.where(lane8 == 3 * i, gain * tilt_real / size, extras)
        extras = jnp.where(lane8 == 3 * i + 1, -gain * tilt_imag / size, extras)
        extras = jnp.where(lane8 == 3 * i + 2, energy, extras)
    out_ref[plan.per * NM :] = extras


def solve(plan, total_rows, packed, start):
    return pl.pallas_call(
        functools.partial(solve_kernel, plan, total_rows),
        out_shape=jax.ShapeDtypeStruct(((plan.per + 1) * NM, LANES), jnp.float32),
        compiler_params=pltpu.CompilerParams(vmem_limit_bytes=VMEM_LIMIT),
        name="solve",
    )(packed, start)


def modes_kernel(plan, coef_ref, near_ref, far_ref, root_ref, out_ref, energy_ref):
    inverse_root = 1.0 / root_ref[...]
    left = lane_index((NM, LANES)) < NB
    lane8 = lane_index((NM, LANES))

    def one_slot(core_slot, pay_ref, slot, energies):
        first = plan.first_freq(core_slot, slot // plan.deep, slot % plan.deep)
        for j in range(plan.per):
            f = first + j
            c = pay_ref[slot, j * NM : (j + 1) * NM, :]
            matrix = jnp.concatenate([jnp.where(left, c, -c), pltpu.roll(c, NB, 1)], axis=0)
            extras = pay_ref[slot, plan.per * NM :, :]
            factor_real = extras[:, 3 * j : 3 * j + 1]
            factor_imag = extras[:, 3 * j + 1 : 3 * j + 2]
            projected = jnp.dot(
                matrix.astype(jnp.bfloat16), coef_ref[f], preferred_element_type=jnp.float32
            )
            real = projected[:NM]
            imag = projected[NM:]
            out_ref[f, :NM, :] = (real * factor_real - imag * factor_imag) * inverse_root
            out_ref[f, NM:, :] = (real * factor_imag + imag * factor_real) * inverse_root
            energies = jnp.where(lane8 == f, extras[:, 3 * j + 2 : 3 * j + 3], energies)
        return energies

    energies = jnp.zeros((NM, LANES), jnp.float32)
    for core_slot, pay_ref in ((0, near_ref), (1, far_ref)):
        energies = lax.fori_loop(
            0,
            plan.g_slots * plan.deep,
            functools.partial(one_slot, core_slot, pay_ref),
            energies,
            unroll=8,
        )
    square = jnp.concatenate([energies] + [jnp.zeros_like(energies)] * (LANES // NM - 1), axis=0)
    energy_ref[...] = jnp.transpose(square)[:NF, :NM]


def modes(plan, coeffs, near, far, root_weight):
    rows_here = coeffs.shape[2]
    tile = min(256, rows_here)
    return pl.pallas_call(
        functools.partial(modes_kernel, plan),
        grid=(rows_here // tile,),
        in_specs=[
            pl.BlockSpec((NF, 2 * NB, tile), lambda i: (0, 0, i)),
            pl.BlockSpec(near.shape, lambda i: (0, 0, 0)),
            pl.BlockSpec(far.shape, lambda i: (0, 0, 0)),
            pl.BlockSpec((1, tile), lambda i: (0, i)),
        ],
        out_specs=[
            pl.BlockSpec((NF, 2 * NM, tile), lambda i: (0, 0, i)),
            pl.BlockSpec((NF, NM), lambda i: (0, 0)),
        ],
        out_shape=[
            jax.ShapeDtypeStruct((NF, 2 * NM, rows_here), jnp.float32),
            jax.ShapeDtypeStruct((NF, NM), jnp.float32),
        ],
        compiler_params=pltpu.CompilerParams(vmem_limit_bytes=VMEM_LIMIT),
        name="modes",
    )(coeffs, near, far, root_weight[None])


def swap(x, axis, size, offset):
    return lax.ppermute(x, axis, [(i, i ^ offset) for i in range(size)])


def shards(plan, snapshots, weights, reference_field, start_basis):
    total_rows = snapshots.shape[1] * plan.grp * plan.row
    root_weight = jnp.sqrt(weights)
    probe = (root_weight * reference_field).astype(jnp.bfloat16).astype(jnp.float32)
    start = lax.dynamic_slice_in_dim(start_basis, plan.first_freq(0, 0, 0), plan.per, 0)
    start = jnp.pad(start, ((0, 0), (0, 0), (0, NB - NBLK), (0, 0)))
    start = jnp.transpose(start, (0, 3, 1, 2)).reshape(plan.per, NM, 2 * NB)

    coeffs, keep, send = transform(plan, snapshots, root_weight, probe)

    held = keep + swap(send, "row", plan.row, 1)
    if plan.split_grp:
        held = held.reshape((plan.grp, plan.deep * plan.per) + held.shape[1:])
        arrived = [swap(held[d], "grp", plan.grp, d) for d in range(1, plan.grp)]
        held = functools.reduce(jnp.add, arrived, held[0])
    held = held.reshape((plan.deep, plan.per) + held.shape[1:])
    arrived = [swap(held[d], "row", plan.row, 2 * d) for d in range(1, plan.deep)]
    held = functools.reduce(jnp.add, arrived, held[0])
    if not plan.split_grp:
        held = lax.psum(held, "grp")

    payload = solve(plan, total_rows, held, start)

    payload = jnp.stack(
        [payload] + [swap(payload, "row", plan.row, 2 * d) for d in range(1, plan.deep)]
    )
    if plan.split_grp:
        payload = jnp.concatenate(
            [payload] + [swap(payload, "grp", plan.grp, d) for d in range(1, plan.grp)]
        )
    return tuple(modes(plan, coeffs, payload, swap(payload, "row", plan.row, 1), root_weight))


def solution(mesh):
    plan = Plan(mesh.shape["grp"], mesh.shape["row"])
    in_specs = (P(None, ("grp", "row")), P(("grp", "row")), P(("grp", "row")), P())
    out_specs = (P(None, None, ("grp", "row")), P())
    return jax.shard_map(
        functools.partial(shards, plan),
        mesh=mesh,
        in_specs=in_specs,
        out_specs=out_specs,
        check_vma=False,
    )
```

```python
import functools
import math

import jax
import jax.numpy as jnp
import numpy as np
from jax import lax
from jax.experimental import pallas as pl
from jax.experimental.pallas import tpu as pltpu
from jax.sharding import PartitionSpec as P

NFFT = 256
HALF = NFFT // 2
NBLK = 63
NB = 64
NF = 64
NM = 8
ITERS = 12
EPS = 1e-06
LANES = 128
PITCH = 2 * NB + 1
MIB = 1024 * 1024
TRANSFORM_MIB, SOLVE_MIB, MODES_MIB = 28, 8, 8


def dft_table():
    time_steps = np.arange(NFFT, dtype=np.int32)
    freq_bins = np.arange(1, NF + 1, dtype=np.int32)
    wrapped = freq_bins[:, None] * time_steps[None, :] % NFFT
    angles = np.float32(2.0 * math.pi / NFFT) * wrapped.astype(np.float32)
    taper = np.float32(0.5) - np.float32(0.5) * np.cos(
        np.float32(2.0 * math.pi / NFFT) * time_steps.astype(np.float32)
    )
    taper = taper / np.sqrt(np.sum(taper * taper))
    stacked = np.concatenate([np.cos(angles), -np.sin(angles)]) * taper[None, :]
    return jnp.asarray(stacked, dtype=jnp.float32).astype(jnp.bfloat16)


class Plan:
    def __init__(self, grp, row):
        self.grp, self.row, self.deep = grp, row, row // 2
        self.split_grp = NF % (grp * row) == 0
        self.g_slots = grp if self.split_grp else 1
        self.owners = row * self.g_slots
        self.per = NF // self.owners

    def first_freq(self, core_slot, grp_slot, z_slot):
        row_index = lax.axis_index("row")
        core = (row_index & 1) ^ core_slot
        deep = (row_index >> 1) ^ z_slot
        owner = deep * 2 + core
        if self.split_grp:
            owner = (lax.axis_index("grp") ^ grp_slot) * self.row + owner
        return owner * self.per


def lane_index(shape):
    return lax.broadcasted_iota(jnp.int32, shape, 1)


def row_index_of(shape):
    return lax.broadcasted_iota(jnp.int32, shape, 0)


def transform_kernel(plan, snap_ref, weight_ref, field_ref, table_ref, coef_ref, keep_ref, send_ref, flip, gram):
    step = pl.program_id(0)
    tile = snap_ref.shape[1]
    pieces = tile // LANES
    table = table_ref[...]
    root = jnp.sqrt(weight_ref[...])
    probe_row = (root * field_ref[...]).astype(jnp.bfloat16).astype(jnp.float32)
    here = pl.ds(pl.multiple_of(step * tile, tile), tile)

    def one_block(b, carry):
        rows = snap_ref[pl.ds(pl.multiple_of(b * HALF, HALF), NFFT), :]
        out = jnp.dot(table, rows, preferred_element_type=jnp.float32) * root
        for part in range(2):
            for piece in range(pieces):
                flip[piece, pl.ds(part * NB + b, NF, stride=PITCH), :] = out[
                    part * NF : (part + 1) * NF, piece * LANES : (piece + 1) * LANES
                ]
        return carry

    lax.fori_loop(0, NBLK, one_block, 0, unroll=21)
    for piece in range(pieces):
        probe = probe_row[:, piece * LANES : (piece + 1) * LANES]
        flip[piece, pl.ds(NB - 1, NF, stride=PITCH), :] = jnp.broadcast_to(probe, (NF, LANES))
        flip[piece, pl.ds(2 * NB - 1, NF, stride=PITCH), :] = jnp.zeros((NF, LANES), jnp.float32)

    @pl.when(step == 0)
    def _():
        gram[...] = jnp.zeros_like(gram)

    def one_freq(f, carry):
        wide = jnp.concatenate(
            [flip[piece, pl.ds(f * PITCH, 2 * NB), :] for piece in range(pieces)], axis=1
        )
        coefs = wide.astype(jnp.bfloat16)
        coef_ref[f, :, here] = coefs
        gram[f] += lax.dot_general(
            coefs, coefs, (((1,), (1,)), ((), ())), preferred_element_type=jnp.float32
        )
        return carry

    lax.fori_loop(0, NF, one_freq, 0, unroll=16)

    @pl.when(step == pl.num_programs(0) - 1)
    def _():
        upper = row_index_of((NB, LANES)) < lane_index((NB, LANES))
        left = lane_index((NB // 2, LANES)) < NB

        def pack(f):
            top = gram[f, :NB, :]
            low = gram[f, NB:, :]
            real = top + pltpu.roll(low, NB, 1)
            imag = pltpu.roll(top, NB, 1) - low
            packed = jnp.where(upper, imag, real)
            return jnp.where(left, packed[: NB // 2], pltpu.roll(packed[NB // 2 :], NB, 1))

        for core_slot, out_ref in ((0, keep_ref), (1, send_ref)):

            def one_slot(slot, carry):
                first = plan.first_freq(core_slot, slot // plan.deep, slot % plan.deep)
                for j in range(plan.per):
                    out_ref[slot * plan.per + j] = pack(first + j)
                return carry

            lax.fori_loop(0, plan.g_slots * plan.deep, one_slot, 0, unroll=4)


def transform(plan, snapshots, weights, reference_field):
    rows_here = snapshots.shape[1]
    tile = min(256, rows_here)
    half_freqs = NF // 2
    packed = jax.ShapeDtypeStruct((half_freqs, NB // 2, LANES), jnp.float32)
    packed_spec = pl.BlockSpec((half_freqs, NB // 2, LANES), lambda i: (0, 0, 0))
    return pl.pallas_call(
        functools.partial(transform_kernel, plan),
        grid=(rows_here // tile,),
        in_specs=[
            pl.BlockSpec((snapshots.shape[0], tile), lambda i: (0, i)),
            pl.BlockSpec((1, tile), lambda i: (0, i)),
            pl.BlockSpec((1, tile), lambda i: (0, i)),
            pl.BlockSpec((2 * NF, NFFT), lambda i: (0, 0)),
        ],
        out_specs=[
            pl.BlockSpec(memory_space=pltpu.VMEM),
            packed_spec,
            packed_spec,
        ],
        out_shape=[
            jax.ShapeDtypeStruct((NF, 2 * NB, rows_here), jnp.bfloat16),
            packed,
            packed,
        ],
        scratch_shapes=[
            pltpu.VMEM((tile // LANES, NF * PITCH, LANES), jnp.float32),
            pltpu.VMEM((NF, 2 * NB, LANES), jnp.float32),
        ],
        compiler_params=pltpu.CompilerParams(vmem_limit_bytes=TRANSFORM_MIB * MIB),
        name="transform",
    )(snapshots, weights[None], reference_field[None], dft_table())


def split_three(x):
    high = x.astype(jnp.bfloat16)
    rest = x - high.astype(jnp.float32)
    middle = rest.astype(jnp.bfloat16)
    low = (rest - middle.astype(jnp.float32)).astype(jnp.bfloat16)
    return high, middle, low


def solve_kernel(plan, total_rows, packed_ref, start_ref, out_ref):
    lane = lane_index((NB, LANES))
    row = row_index_of((NB, LANES))
    col = lane & (NB - 1)
    left = lane < NB
    inside = (row < NBLK) & (col < NBLK)
    lane8 = lane_index((NM, LANES))
    row8 = row_index_of((NM, LANES))
    left8 = lane8 < NB

    systems, probes, basis = [], [], []
    for i in range(plan.per):
        folded = packed_ref[i]
        turned = pltpu.roll(folded, NB, 1)
        wide = jnp.concatenate([folded, turned], axis=0)
        twice = jnp.where(left, wide, pltpu.roll(wide, NB, 1))
        flipped = jnp.transpose(jnp.concatenate([twice, twice], axis=0))[:NB]
        real = jnp.where(inside, jnp.where(row >= col, twice, flipped), 0.0) / total_rows
        imag = jnp.where(row < col, twice, jnp.where(row > col, -flipped, 0.0))
        imag = jnp.where(inside, imag, 0.0) / total_rows
        system = jnp.concatenate([jnp.where(left, real, -imag), jnp.where(left, imag, real)], axis=0)
        high, middle, low = split_three(system)
        systems.append(
            jnp.concatenate(
                [
                    jnp.concatenate([high, low], axis=1),
                    jnp.concatenate([middle, jnp.zeros_like(low)], axis=1),
                ],
                axis=0,
            )
        )
        along = twice[NB - 1 :]
        across = flipped[NB - 1 :]
        left1 = lane_index((1, LANES)) < NB
        probes.append((jnp.where(left1, along, across), jnp.where(left1, -across, along)))
        basis.append(start_ref[i])

    def image_of(i, v):
        high, middle, low = split_three(v)
        zeros = jnp.zeros_like(high)
        parts = jnp.concatenate(
            [
                jnp.concatenate([high, high], axis=1),
                jnp.concatenate([middle, middle], axis=1),
                jnp.concatenate([low, zeros], axis=1),
                jnp.concatenate([zeros, zeros], axis=1),
            ],
            axis=0,
        )
        out = jnp.dot(parts, systems[i], preferred_element_type=jnp.float32)
        small = out[:NM, LANES:] + out[2 * NM : 3 * NM, :LANES]
        return out[:NM, :LANES] + (out[NM : 2 * NM, :LANES] + small)

    def lane_sum(x):
        return jnp.sum(x, axis=1, keepdims=True)

    def orthonormalize(y):
        swapped = pltpu.roll(y, NB, 1)
        turned = jnp.where(left8, -swapped, swapped)
        v = jnp.zeros_like(y)
        for j in range(NM):
            pivot = jnp.broadcast_to(y[j : j + 1], y.shape)
            pivot_turned = jnp.broadcast_to(turned[j : j + 1], y.shape)
            size = lane_sum(pivot * pivot) + EPS
            v = jnp.where(row8 == j, pivot * lax.rsqrt(size), v)
            if j < NM - 1:
                inner_real = lane_sum(pivot * y)
                inner_imag = lane_sum(pivot_turned * y)
                inverse = 1.0 / size
                later = row8 > j
                a = jnp.where(later, inner_real * inverse, 0.0)
                c = jnp.where(later, inner_imag * inverse, 0.0)
                y, turned = (
                    y - (a * pivot + c * pivot_turned),
                    turned - (a * pivot_turned - c * pivot),
                )
        return v

    def sweep(index, current):
        images = [image_of(i, v) for i, v in enumerate(current)]
        return tuple(orthonormalize(y) for y in images)

    basis = lax.fori_loop(0, ITERS, sweep, tuple(basis))
    extras = jnp.zeros((NM, LANES), jnp.float32)
    scale = 1.0 / math.sqrt(total_rows)
    for i, v in enumerate(basis):
        energy = lane_sum(v * image_of(i, v))
        coef = v.astype(jnp.bfloat16).astype(jnp.float32)
        out_ref[i * NM : (i + 1) * NM] = coef
        gain = 1.0 / jnp.sqrt(energy + EPS)
        tilt_real = gain * (lane_sum(coef * probes[i][0]) * scale)
        tilt_imag = gain * (lane_sum(coef * probes[i][1]) * scale)
        size = jnp.sqrt(jnp.maximum(tilt_real * tilt_real + tilt_imag * tilt_imag, 0.25))
        extras = jnp.where(lane8 == 3 * i, gain * tilt_real / size, extras)
        extras = jnp.where(lane8 == 3 * i + 1, -gain * tilt_imag / size, extras)
        extras = jnp.where(lane8 == 3 * i + 2, energy, extras)
    out_ref[plan.per * NM :] = extras


def solve(plan, total_rows, packed, start):
    return pl.pallas_call(
        functools.partial(solve_kernel, plan, total_rows),
        in_specs=[pl.BlockSpec(memory_space=pltpu.VMEM)] * 2,
        out_specs=pl.BlockSpec(memory_space=pltpu.VMEM),
        out_shape=jax.ShapeDtypeStruct(((plan.per + 1) * NM, LANES), jnp.float32),
        compiler_params=pltpu.CompilerParams(vmem_limit_bytes=SOLVE_MIB * MIB),
        name="solve",
    )(packed, start)


def modes_kernel(plan, coef_ref, near_ref, far_ref, weight_ref, out_ref, energy_ref):
    tile = out_ref.shape[2]
    here = pl.ds(pl.multiple_of(pl.program_id(0) * tile, tile), tile)
    inverse_root = 1.0 / jnp.sqrt(weight_ref[...])
    left = lane_index((NM, LANES)) < NB
    lane8 = lane_index((NM, LANES))

    def one_slot(core_slot, pay_ref, slot, energies):
        first = plan.first_freq(core_slot, slot // plan.deep, slot % plan.deep)
        for j in range(plan.per):
            f = first + j
            c = pay_ref[slot, j * NM : (j + 1) * NM, :]
            matrix = jnp.concatenate([jnp.where(left, c, -c), pltpu.roll(c, NB, 1)], axis=0)
            extras = pay_ref[slot, plan.per * NM :, :]
            factor_real = extras[:, 3 * j : 3 * j + 1]
            factor_imag = extras[:, 3 * j + 1 : 3 * j + 2]
            projected = jnp.dot(
                matrix.astype(jnp.bfloat16), coef_ref[f, :, here], preferred_element_type=jnp.float32
            )
            real = projected[:NM]
            imag = projected[NM:]
            out_ref[f, :NM, :] = (real * factor_real - imag * factor_imag) * inverse_root
            out_ref[f, NM:, :] = (real * factor_imag + imag * factor_real) * inverse_root
            energies = jnp.where(lane8 == f, extras[:, 3 * j + 2 : 3 * j + 3], energies)
        return energies

    energies = jnp.zeros((NM, LANES), jnp.float32)
    for core_slot, pay_ref in ((0, near_ref), (1, far_ref)):
        energies = lax.fori_loop(
            0,
            plan.g_slots * plan.deep,
            functools.partial(one_slot, core_slot, pay_ref),
            energies,
            unroll=8,
        )
    energy_ref[...] = energies[:, :NF]


def modes(plan, coeffs, near, far, weights):
    rows_here = coeffs.shape[2]
    tile = min(256, rows_here)
    return pl.pallas_call(
        functools.partial(modes_kernel, plan),
        grid=(rows_here // tile,),
        in_specs=[
            pl.BlockSpec(memory_space=pltpu.VMEM),
            pl.BlockSpec(memory_space=pltpu.VMEM),
            pl.BlockSpec(memory_space=pltpu.VMEM),
            pl.BlockSpec((1, tile), lambda i: (0, i)),
        ],
        out_specs=[
            pl.BlockSpec((NF, 2 * NM, tile), lambda i: (0, 0, i)),
            pl.BlockSpec((NM, NF), lambda i: (0, 0)),
        ],
        out_shape=[
            jax.ShapeDtypeStruct((NF, 2 * NM, rows_here), jnp.float32),
            jax.ShapeDtypeStruct((NM, NF), jnp.float32),
        ],
        compiler_params=pltpu.CompilerParams(vmem_limit_bytes=MODES_MIB * MIB),
        name="modes",
    )(coeffs, near, far, weights[None])


def swap(x, axis, size, offset):
    return lax.ppermute(x, axis, [(i, i ^ offset) for i in range(size)])


def shards(plan, snapshots, weights, reference_field, start_basis):
    total_rows = snapshots.shape[1] * plan.grp * plan.row
    start = lax.dynamic_slice_in_dim(start_basis, plan.first_freq(0, 0, 0), plan.per, 0)
    start = jnp.pad(start, ((0, 0), (0, 0), (0, NB - NBLK), (0, 0)))
    start = jnp.transpose(start, (0, 3, 1, 2)).reshape(plan.per, NM, 2 * NB)

    coeffs, keep, send = transform(plan, snapshots, weights, reference_field)

    held = keep + swap(send, "row", plan.row, 1)
    if plan.split_grp:
        held = held.reshape((plan.grp, plan.deep * plan.per) + held.shape[1:])
        arrived = [swap(held[d], "grp", plan.grp, d) for d in range(1, plan.grp)]
        held = functools.reduce(jnp.add, arrived, held[0])
    held = held.reshape((plan.deep, plan.per) + held.shape[1:])
    arrived = [swap(held[d], "row", plan.row, 2 * d) for d in range(1, plan.deep)]
    held = functools.reduce(jnp.add, arrived, held[0])
    if not plan.split_grp:
        held = lax.psum(held, "grp")

    payload = solve(plan, total_rows, held, start)

    payload = jnp.stack(
        [payload] + [swap(payload, "row", plan.row, 2 * d) for d in range(1, plan.deep)]
    )
    if plan.split_grp:
        payload = jnp.concatenate(
            [payload] + [swap(payload, "grp", plan.grp, d) for d in range(1, plan.grp)]
        )
    far = swap(payload, "row", plan.row, 1)
    spod_modes, energies = modes(plan, coeffs, payload, far, weights)
    return spod_modes, jnp.transpose(energies)


def solution(mesh):
    plan = Plan(mesh.shape["grp"], mesh.shape["row"])
    in_specs = (P(None, ("grp", "row")), P(("grp", "row")), P(("grp", "row")), P())
    out_specs = (P(None, None, ("grp", "row")), P())
    return jax.shard_map(
        functools.partial(shards, plan),
        mesh=mesh,
        in_specs=in_specs,
        out_specs=out_specs,
        check_vma=False,
    )
```

```python
import functools
import math

import jax
import jax.numpy as jnp
import numpy as np
from jax import lax
from jax.experimental import pallas as pl
from jax.experimental.pallas import tpu as pltpu
from jax.sharding import PartitionSpec as P

NFFT = 256
HALF = NFFT // 2
NBLK = 63
NB = 64
NF = 64
NM = 8
ITERS = 12
EPS = 1e-06
LANES = 128
PITCH = 2 * NB + 1
MIB = 1024 * 1024
TRANSFORM_MIB, SOLVE_MIB, MODES_MIB = 28, 8, 8


def dft_table():
    time_steps = np.arange(NFFT, dtype=np.int32)
    freq_bins = np.arange(1, NF + 1, dtype=np.int32)
    wrapped = freq_bins[:, None] * time_steps[None, :] % NFFT
    angles = np.float32(2.0 * math.pi / NFFT) * wrapped.astype(np.float32)
    taper = np.float32(0.5) - np.float32(0.5) * np.cos(
        np.float32(2.0 * math.pi / NFFT) * time_steps.astype(np.float32)
    )
    taper = taper / np.sqrt(np.sum(taper * taper))
    stacked = np.concatenate([np.cos(angles), -np.sin(angles)]) * taper[None, :]
    return jnp.asarray(stacked, dtype=jnp.float32).astype(jnp.bfloat16)


class Plan:
    def __init__(self, grp, row):
        self.grp, self.row, self.deep = grp, row, row // 2
        self.split_grp = NF % (grp * row) == 0
        self.g_slots = grp if self.split_grp else 1
        self.owners = row * self.g_slots
        self.per = NF // self.owners

    def first_freq(self, core_slot, grp_slot, z_slot):
        row_index = lax.axis_index("row")
        core = (row_index & 1) ^ core_slot
        deep = (row_index >> 1) ^ z_slot
        owner = deep * 2 + core
        if self.split_grp:
            owner = (lax.axis_index("grp") ^ grp_slot) * self.row + owner
        return owner * self.per


def lane_index(shape):
    return lax.broadcasted_iota(jnp.int32, shape, 1)


def row_index_of(shape):
    return lax.broadcasted_iota(jnp.int32, shape, 0)


def transform_kernel(plan, snap_ref, weight_ref, field_ref, table_ref, coef_ref, keep_ref, send_ref, flip, gram):
    step = pl.program_id(0)
    tile = snap_ref.shape[1]
    pieces = tile // LANES
    table = table_ref[...]
    root = jnp.sqrt(weight_ref[...])
    probe_row = (root * field_ref[...]).astype(jnp.bfloat16).astype(jnp.float32)
    here = pl.ds(pl.multiple_of(step * tile, tile), tile)

    def one_block(b, carry):
        rows = snap_ref[pl.ds(pl.multiple_of(b * HALF, HALF), NFFT), :]
        out = jnp.dot(table, rows, preferred_element_type=jnp.float32) * root
        for part in range(2):
            for piece in range(pieces):
                flip[piece, pl.ds(part * NB + b, NF, stride=PITCH), :] = out[
                    part * NF : (part + 1) * NF, piece * LANES : (piece + 1) * LANES
                ]
        return carry

    lax.fori_loop(0, NBLK, one_block, 0, unroll=63)
    for piece in range(pieces):
        probe = probe_row[:, piece * LANES : (piece + 1) * LANES]
        flip[piece, pl.ds(NB - 1, NF, stride=PITCH), :] = jnp.broadcast_to(probe, (NF, LANES))
        flip[piece, pl.ds(2 * NB - 1, NF, stride=PITCH), :] = jnp.zeros((NF, LANES), jnp.float32)

    @pl.when(step == 0)
    def _():
        gram[...] = jnp.zeros_like(gram)

    def one_freq(f, carry):
        wide = jnp.concatenate(
            [flip[piece, pl.ds(f * PITCH, 2 * NB), :] for piece in range(pieces)], axis=1
        )
        coefs = wide.astype(jnp.bfloat16)
        coef_ref[f, :, here] = coefs
        gram[f] += lax.dot_general(
            coefs, coefs, (((1,), (1,)), ((), ())), preferred_element_type=jnp.float32
        )
        return carry

    lax.fori_loop(0, NF, one_freq, 0, unroll=64)

    @pl.when(step == pl.num_programs(0) - 1)
    def _():
        row = row_index_of((NB, LANES))
        lane = lane_index((NB, LANES))
        left = lane < NB
        upper = row < (lane & (NB - 1))
        left_half = left[: NB // 2]

        def pack(f):
            top = gram[f, :NB, :]
            low = gram[f, NB:, :]
            parts = jnp.where(left, jnp.where(upper, -low, top), jnp.where(upper, top, low))
            first, second = parts[: NB // 2], parts[NB // 2 :]
            other = pltpu.roll(jnp.where(left_half, second, first), NB, 1)
            return jnp.where(left_half, first, second) + other

        for core_slot, out_ref in ((0, keep_ref), (1, send_ref)):

            def one_slot(slot, carry):
                first = plan.first_freq(core_slot, slot // plan.deep, slot % plan.deep)
                for j in range(plan.per):
                    out_ref[slot * plan.per + j] = pack(first + j)
                return carry

            lax.fori_loop(0, plan.g_slots * plan.deep, one_slot, 0, unroll=8)


def transform(plan, snapshots, weights, reference_field):
    rows_here = snapshots.shape[1]
    tile = min(256, rows_here)
    half_freqs = NF // 2
    packed = jax.ShapeDtypeStruct((half_freqs, NB // 2, LANES), jnp.float32)
    packed_spec = pl.BlockSpec((half_freqs, NB // 2, LANES), lambda i: (0, 0, 0))
    return pl.pallas_call(
        functools.partial(transform_kernel, plan),
        grid=(rows_here // tile,),
        in_specs=[
            pl.BlockSpec((snapshots.shape[0], tile), lambda i: (0, i)),
            pl.BlockSpec((1, tile), lambda i: (0, i)),
            pl.BlockSpec((1, tile), lambda i: (0, i)),
            pl.BlockSpec((2 * NF, NFFT), lambda i: (0, 0)),
        ],
        out_specs=[
            pl.BlockSpec(memory_space=pltpu.VMEM),
            packed_spec,
            packed_spec,
        ],
        out_shape=[
            jax.ShapeDtypeStruct((NF, 2 * NB, rows_here), jnp.bfloat16),
            packed,
            packed,
        ],
        scratch_shapes=[
            pltpu.VMEM((tile // LANES, NF * PITCH, LANES), jnp.float32),
            pltpu.VMEM((NF, 2 * NB, LANES), jnp.float32),
        ],
        compiler_params=pltpu.CompilerParams(vmem_limit_bytes=TRANSFORM_MIB * MIB),
        name="transform",
    )(snapshots, weights[None], reference_field[None], dft_table())


def split_three(x):
    high = x.astype(jnp.bfloat16)
    rest = x - high.astype(jnp.float32)
    middle = rest.astype(jnp.bfloat16)
    low = (rest - middle.astype(jnp.float32)).astype(jnp.bfloat16)
    return high, middle, low


def solve_kernel(plan, total_rows, packed_ref, start_ref, out_ref):
    lane = lane_index((NB, LANES))
    row = row_index_of((NB, LANES))
    col = lane & (NB - 1)
    left = lane < NB
    inside = (row < NBLK) & (col < NBLK)
    lane8 = lane_index((NM, LANES))
    row8 = row_index_of((NM, LANES))
    left8 = lane8 < NB

    systems, probes, basis = [], [], []
    for i in range(plan.per):
        folded = packed_ref[i]
        turned = pltpu.roll(folded, NB, 1)
        wide = jnp.concatenate([folded, turned], axis=0)
        twice = jnp.where(left, wide, pltpu.roll(wide, NB, 1))
        flipped = jnp.transpose(jnp.concatenate([twice, twice], axis=0))[:NB]
        real = jnp.where(inside, jnp.where(row >= col, twice, flipped), 0.0) / total_rows
        imag = jnp.where(row < col, twice, jnp.where(row > col, -flipped, 0.0))
        imag = jnp.where(inside, imag, 0.0) / total_rows
        system = jnp.concatenate([jnp.where(left, real, -imag), jnp.where(left, imag, real)], axis=0)
        high, middle, low = split_three(system)
        systems.append(
            jnp.concatenate(
                [
                    jnp.concatenate([high, low], axis=1),
                    jnp.concatenate([middle, jnp.zeros_like(low)], axis=1),
                ],
                axis=0,
            )
        )
        along = twice[NB - 1 :]
        across = flipped[NB - 1 :]
        left1 = lane_index((1, LANES)) < NB
        probes.append((jnp.where(left1, along, across), jnp.where(left1, -across, along)))
        basis.append(start_ref[i])

    def image_of(i, v):
        high, middle, low = split_three(v)
        zeros = jnp.zeros_like(high)
        parts = jnp.concatenate(
            [
                jnp.concatenate([high, high], axis=1),
                jnp.concatenate([middle, middle], axis=1),
                jnp.concatenate([low, zeros], axis=1),
                jnp.concatenate([zeros, zeros], axis=1),
            ],
            axis=0,
        )
        out = jnp.dot(parts, systems[i], preferred_element_type=jnp.float32)
        small = out[:NM, LANES:] + out[2 * NM : 3 * NM, :LANES]
        return out[:NM, :LANES] + (out[NM : 2 * NM, :LANES] + small)

    def lane_sum(x):
        return jnp.sum(x, axis=1, keepdims=True)

    def orthonormalize(y):
        swapped = pltpu.roll(y, NB, 1)
        turned = jnp.where(left8, -swapped, swapped)
        v = jnp.zeros_like(y)
        for j in range(NM):
            pivot = jnp.broadcast_to(y[j : j + 1], y.shape)
            pivot_turned = jnp.broadcast_to(turned[j : j + 1], y.shape)
            size = lane_sum(pivot * pivot) + EPS
            v = jnp.where(row8 == j, pivot * lax.rsqrt(size), v)
            if j < NM - 1:
                inner_real = lane_sum(pivot * y)
                inner_imag = lane_sum(pivot_turned * y)
                inverse = 1.0 / size
                later = row8 > j
                a = jnp.where(later, inner_real * inverse, 0.0)
                c = jnp.where(later, inner_imag * inverse, 0.0)
                y, turned = (
                    y - (a * pivot + c * pivot_turned),
                    turned - (a * pivot_turned - c * pivot),
                )
        return v

    def sweep(index, current):
        images = [image_of(i, v) for i, v in enumerate(current)]
        return tuple(orthonormalize(y) for y in images)

    basis = lax.fori_loop(0, ITERS, sweep, tuple(basis))
    extras = jnp.zeros((NM, LANES), jnp.float32)
    scale = 1.0 / math.sqrt(total_rows)
    for i, v in enumerate(basis):
        energy = lane_sum(v * image_of(i, v))
        coef = v.astype(jnp.bfloat16).astype(jnp.float32)
        out_ref[i * NM : (i + 1) * NM] = coef
        gain = 1.0 / jnp.sqrt(energy + EPS)
        tilt_real = gain * (lane_sum(coef * probes[i][0]) * scale)
        tilt_imag = gain * (lane_sum(coef * probes[i][1]) * scale)
        size = jnp.sqrt(jnp.maximum(tilt_real * tilt_real + tilt_imag * tilt_imag, 0.25))
        extras = jnp.where(lane8 == 3 * i, gain * tilt_real / size, extras)
        extras = jnp.where(lane8 == 3 * i + 1, -gain * tilt_imag / size, extras)
        extras = jnp.where(lane8 == 3 * i + 2, energy, extras)
    out_ref[plan.per * NM :] = extras


def solve(plan, total_rows, packed, start):
    return pl.pallas_call(
        functools.partial(solve_kernel, plan, total_rows),
        in_specs=[pl.BlockSpec(memory_space=pltpu.VMEM)] * 2,
        out_specs=pl.BlockSpec(memory_space=pltpu.VMEM),
        out_shape=jax.ShapeDtypeStruct(((plan.per + 1) * NM, LANES), jnp.float32),
        compiler_params=pltpu.CompilerParams(vmem_limit_bytes=SOLVE_MIB * MIB),
        name="solve",
    )(packed, start)


def modes_kernel(plan, coef_ref, near_ref, far_ref, weight_ref, out_ref, energy_ref):
    tile = out_ref.shape[2]
    here = pl.ds(pl.multiple_of(pl.program_id(0) * tile, tile), tile)
    inverse_root = 1.0 / jnp.sqrt(weight_ref[...])
    left = lane_index((NM, LANES)) < NB
    lane8 = lane_index((NM, LANES))

    def one_slot(core_slot, pay_ref, slot, energies):
        first = plan.first_freq(core_slot, slot // plan.deep, slot % plan.deep)
        for j in range(plan.per):
            f = first + j
            c = pay_ref[slot, j * NM : (j + 1) * NM, :]
            matrix = jnp.concatenate([jnp.where(left, c, -c), pltpu.roll(c, NB, 1)], axis=0)
            extras = pay_ref[slot, plan.per * NM :, :]
            factor_real = extras[:, 3 * j : 3 * j + 1]
            factor_imag = extras[:, 3 * j + 1 : 3 * j + 2]
            projected = jnp.dot(
                matrix.astype(jnp.bfloat16), coef_ref[f, :, here], preferred_element_type=jnp.float32
            )
            real = projected[:NM]
            imag = projected[NM:]
            out_ref[f, :NM, :] = (real * factor_real - imag * factor_imag) * inverse_root
            out_ref[f, NM:, :] = (real * factor_imag + imag * factor_real) * inverse_root
            energies = jnp.where(lane8 == f, extras[:, 3 * j + 2 : 3 * j + 3], energies)
        return energies

    energies = jnp.zeros((NM, LANES), jnp.float32)
    for core_slot, pay_ref in ((0, near_ref), (1, far_ref)):
        energies = lax.fori_loop(
            0,
            plan.g_slots * plan.deep,
            functools.partial(one_slot, core_slot, pay_ref),
            energies,
            unroll=8,
        )
    energy_ref[...] = energies[:, :NF]


def modes(plan, coeffs, near, far, weights):
    rows_here = coeffs.shape[2]
    tile = min(256, rows_here)
    return pl.pallas_call(
        functools.partial(modes_kernel, plan),
        grid=(rows_here // tile,),
        in_specs=[
            pl.BlockSpec(memory_space=pltpu.VMEM),
            pl.BlockSpec(memory_space=pltpu.VMEM),
            pl.BlockSpec(memory_space=pltpu.VMEM),
            pl.BlockSpec((1, tile), lambda i: (0, i)),
        ],
        out_specs=[
            pl.BlockSpec((NF, 2 * NM, tile), lambda i: (0, 0, i)),
            pl.BlockSpec((NM, NF), lambda i: (0, 0)),
        ],
        out_shape=[
            jax.ShapeDtypeStruct((NF, 2 * NM, rows_here), jnp.float32),
            jax.ShapeDtypeStruct((NM, NF), jnp.float32),
        ],
        compiler_params=pltpu.CompilerParams(vmem_limit_bytes=MODES_MIB * MIB),
        name="modes",
    )(coeffs, near, far, weights[None])


def swap(x, axis, size, offset):
    return lax.ppermute(x, axis, [(i, i ^ offset) for i in range(size)])


def shards(plan, snapshots, weights, reference_field, start_basis):
    total_rows = snapshots.shape[1] * plan.grp * plan.row
    start = lax.dynamic_slice_in_dim(start_basis, plan.first_freq(0, 0, 0), plan.per, 0)
    start = jnp.pad(start, ((0, 0), (0, 0), (0, NB - NBLK), (0, 0)))
    start = jnp.transpose(start, (0, 3, 1, 2)).reshape(plan.per, NM, 2 * NB)
    snapshots, start = lax.optimization_barrier((snapshots, start))

    coeffs, keep, send = transform(plan, snapshots, weights, reference_field)

    held = keep + swap(send, "row", plan.row, 1)
    if plan.split_grp:
        held = held.reshape((plan.grp, plan.deep * plan.per) + held.shape[1:])
        arrived = [swap(held[d], "grp", plan.grp, d) for d in range(1, plan.grp)]
        held = functools.reduce(jnp.add, arrived, held[0])
    held = held.reshape((plan.deep, plan.per) + held.shape[1:])
    arrived = [swap(held[d], "row", plan.row, 2 * d) for d in range(1, plan.deep)]
    held = functools.reduce(jnp.add, arrived, held[0])
    if not plan.split_grp:
        held = lax.psum(held, "grp")

    payload = solve(plan, total_rows, held, start)

    payload = jnp.stack(
        [payload] + [swap(payload, "row", plan.row, 2 * d) for d in range(1, plan.deep)]
    )
    if plan.split_grp:
        payload = jnp.concatenate(
            [payload] + [swap(payload, "grp", plan.grp, d) for d in range(1, plan.grp)]
        )
    far = swap(payload, "row", plan.row, 1)
    spod_modes, energies = modes(plan, coeffs, payload, far, weights)
    return spod_modes, jnp.transpose(energies)


def solution(mesh):
    plan = Plan(mesh.shape["grp"], mesh.shape["row"])
    in_specs = (P(None, ("grp", "row")), P(("grp", "row")), P(("grp", "row")), P())
    out_specs = (P(None, None, ("grp", "row")), P())
    return jax.shard_map(
        functools.partial(shards, plan),
        mesh=mesh,
        in_specs=in_specs,
        out_specs=out_specs,
        check_vma=False,
    )
```

```python
import functools
import math

import jax
import jax.numpy as jnp
import numpy as np
from jax import lax
from jax.experimental import pallas as pl
from jax.experimental.pallas import tpu as pltpu
from jax.sharding import PartitionSpec as P

NFFT = 256
HALF = NFFT // 2
NBLK = 63
NB = 64
NF = 64
NM = 8
ITERS = 12
EPS = 1e-06
LEAST_LEFT = 1e-03
LANES = 128
PITCH = 2 * NB + 1
MIB = 1024 * 1024
TRANSFORM_MIB, SOLVE_MIB, MODES_MIB = 28, 8, 8
MODES_FREQS = 8


def dft_table():
    time_steps = np.arange(NFFT, dtype=np.int32)
    freq_bins = np.arange(1, NF + 1, dtype=np.int32)
    wrapped = freq_bins[:, None] * time_steps[None, :] % NFFT
    angles = np.float32(2.0 * math.pi / NFFT) * wrapped.astype(np.float32)
    taper = np.float32(0.5) - np.float32(0.5) * np.cos(
        np.float32(2.0 * math.pi / NFFT) * time_steps.astype(np.float32)
    )
    taper = taper / np.sqrt(np.sum(taper * taper))
    stacked = np.concatenate([np.cos(angles), -np.sin(angles)]) * taper[None, :]
    return jnp.asarray(stacked, dtype=jnp.float32).astype(jnp.bfloat16)


class Plan:
    def __init__(self, grp, row):
        self.grp, self.row, self.deep = grp, row, row // 2
        self.split_grp = NF % (grp * row) == 0
        self.g_slots = grp if self.split_grp else 1
        self.owners = row * self.g_slots
        self.per = NF // self.owners

    def first_freq(self, core_slot, grp_slot, z_slot):
        row_index = lax.axis_index("row")
        core = (row_index & 1) ^ core_slot
        deep = (row_index >> 1) ^ z_slot
        owner = deep * 2 + core
        if self.split_grp:
            owner = (lax.axis_index("grp") ^ grp_slot) * self.row + owner
        return owner * self.per

    def slot_of(self, f):
        owner = f // self.per
        row_index = lax.axis_index("row")
        slot = ((owner % self.row) ^ row_index) >> 1
        if self.split_grp:
            slot = ((owner // self.row) ^ lax.axis_index("grp")) * self.deep + slot
        return slot, ((owner ^ row_index) & 1) == 0


def lane_index(shape):
    return lax.broadcasted_iota(jnp.int32, shape, 1)


def row_index_of(shape):
    return lax.broadcasted_iota(jnp.int32, shape, 0)


def transform_kernel(plan, snap_ref, weight_ref, field_ref, table_ref, coef_ref, keep_ref, send_ref, flip, gram):
    step = pl.program_id(0)
    tile = snap_ref.shape[1]
    pieces = tile // LANES
    table = table_ref[...]
    root = jnp.sqrt(weight_ref[...])
    probe_row = (root * field_ref[...]).astype(jnp.bfloat16).astype(jnp.float32)
    here = pl.ds(pl.multiple_of(step * tile, tile), tile)

    def one_block(b, carry):
        rows = snap_ref[pl.ds(pl.multiple_of(b * HALF, HALF), NFFT), :]
        out = jnp.dot(table, rows, preferred_element_type=jnp.float32) * root
        for part in range(2):
            for piece in range(pieces):
                flip[piece, pl.ds(part * NB + b, NF, stride=PITCH), :] = out[
                    part * NF : (part + 1) * NF, piece * LANES : (piece + 1) * LANES
                ]
        return carry

    lax.fori_loop(0, NBLK, one_block, 0, unroll=63)
    for piece in range(pieces):
        probe = probe_row[:, piece * LANES : (piece + 1) * LANES]
        flip[piece, pl.ds(NB - 1, NF, stride=PITCH), :] = jnp.broadcast_to(probe, (NF, LANES))
        flip[piece, pl.ds(2 * NB - 1, NF, stride=PITCH), :] = jnp.zeros((NF, LANES), jnp.float32)

    @pl.when(step == 0)
    def _():
        gram[...] = jnp.zeros_like(gram)

    def one_freq(f, carry):
        wide = jnp.concatenate(
            [flip[piece, pl.ds(f * PITCH, 2 * NB), :] for piece in range(pieces)], axis=1
        )
        coefs = wide.astype(jnp.bfloat16)
        coef_ref[f, :, here] = coefs
        gram[f] += lax.dot_general(
            coefs, coefs, (((1,), (1,)), ((), ())), preferred_element_type=jnp.float32
        )
        return carry

    lax.fori_loop(0, NF, one_freq, 0, unroll=64)

    @pl.when(step == pl.num_programs(0) - 1)
    def _():
        row = row_index_of((NB, LANES))
        lane = lane_index((NB, LANES))
        left = lane < NB
        upper = row < (lane & (NB - 1))
        left_half = left[: NB // 2]

        def pack(f):
            top = gram[f, :NB, :]
            low = gram[f, NB:, :]
            parts = jnp.where(left, jnp.where(upper, -low, top), jnp.where(upper, top, low))
            first, second = parts[: NB // 2], parts[NB // 2 :]
            other = pltpu.roll(jnp.where(left_half, second, first), NB, 1)
            return jnp.where(left_half, first, second) + other

        for core_slot, out_ref in ((0, keep_ref), (1, send_ref)):

            def one_slot(slot, carry):
                first = plan.first_freq(core_slot, slot // plan.deep, slot % plan.deep)
                for j in range(plan.per):
                    out_ref[slot * plan.per + j] = pack(first + j)
                return carry

            lax.fori_loop(0, plan.g_slots * plan.deep, one_slot, 0, unroll=8)


def transform(plan, snapshots, weights, reference_field):
    rows_here = snapshots.shape[1]
    tile = min(256, rows_here)
    half_freqs = NF // 2
    packed = jax.ShapeDtypeStruct((half_freqs, NB // 2, LANES), jnp.float32)
    packed_spec = pl.BlockSpec((half_freqs, NB // 2, LANES), lambda i: (0, 0, 0))
    return pl.pallas_call(
        functools.partial(transform_kernel, plan),
        grid=(rows_here // tile,),
        in_specs=[
            pl.BlockSpec((snapshots.shape[0], tile), lambda i: (0, i)),
            pl.BlockSpec((1, tile), lambda i: (0, i)),
            pl.BlockSpec((1, tile), lambda i: (0, i)),
            pl.BlockSpec((2 * NF, NFFT), lambda i: (0, 0)),
        ],
        out_specs=[
            pl.BlockSpec(memory_space=pltpu.VMEM),
            packed_spec,
            packed_spec,
        ],
        out_shape=[
            jax.ShapeDtypeStruct((NF, 2 * NB, rows_here), jnp.bfloat16),
            packed,
            packed,
        ],
        scratch_shapes=[
            pltpu.VMEM((tile // LANES, NF * PITCH, LANES), jnp.float32),
            pltpu.VMEM((NF, 2 * NB, LANES), jnp.float32),
        ],
        compiler_params=pltpu.CompilerParams(vmem_limit_bytes=TRANSFORM_MIB * MIB),
        name="transform",
    )(snapshots, weights[None], reference_field[None], dft_table())


def split_three(x):
    high = x.astype(jnp.bfloat16)
    rest = x - high.astype(jnp.float32)
    middle = rest.astype(jnp.bfloat16)
    low = (rest - middle.astype(jnp.float32)).astype(jnp.bfloat16)
    return high, middle, low


def turn(y):
    swapped = pltpu.roll(y, NB, 1)
    return jnp.where(lane_index(y.shape) < NB, -swapped, swapped)


def lane_sum(x):
    return jnp.broadcast_to(jnp.sum(x, axis=1, keepdims=True), x.shape)


def spread(x, j):
    return jnp.broadcast_to(x[j : j + 1], x.shape)


def orthonormalize_checked(y, turned):
    row = row_index_of(y.shape)
    v = jnp.zeros_like(y)
    for j in range(NM):
        pivot, pivot_turned = spread(y, j), spread(turned, j)
        size = lane_sum(pivot * pivot) + EPS
        v = jnp.where(row == j, pivot * lax.rsqrt(size), v)
        if j < NM - 1:
            inverse = 1.0 / size
            a = jnp.where(row > j, lane_sum(pivot * y) * inverse, 0.0)
            c = jnp.where(row > j, lane_sum(pivot_turned * y) * inverse, 0.0)
            y, turned = (
                y - (a * pivot + c * pivot_turned),
                turned - (a * pivot_turned - c * pivot),
            )
    return v


def orthonormalize_quick(y, turned, worst):
    row = row_index_of(y.shape)
    real = [lane_sum(spread(y, j) * y) for j in range(NM)]
    imag = [lane_sum(spread(turned, j) * y) for j in range(NM - 1)]
    whole = [spread(real[j], j) + EPS for j in range(NM)]
    v = jnp.zeros_like(y)
    for j in range(NM):
        pivot, pivot_turned = spread(y, j), spread(turned, j)
        size = jnp.maximum(spread(real[j], j), 0.0) + EPS
        worst = jnp.minimum(worst, size / whole[j])
        v = jnp.where(row == j, pivot * lax.rsqrt(size), v)
        if j < NM - 1:
            inverse = 1.0 / size
            scale = (size + EPS) * inverse * inverse
            scaled_real, scaled_imag = real[j] * scale, imag[j] * scale
            for l in range(j + 1, NM):
                other_real, other_imag = spread(real[j], l), spread(imag[j], l)
                real[l] = real[l] - (scaled_real * other_real + scaled_imag * other_imag)
                if l < NM - 1:
                    imag[l] = imag[l] - (scaled_imag * other_real - scaled_real * other_imag)
            a = jnp.where(row > j, real[j] * inverse, 0.0)
            c = jnp.where(row > j, imag[j] * inverse, 0.0)
            y, turned = (
                y - (a * pivot + c * pivot_turned),
                turned - (a * pivot_turned - c * pivot),
            )
    return v, worst


def solve_kernel(plan, total_rows, packed_ref, start_ref, out_ref, basis_ref):
    lane = lane_index((NB, LANES))
    row = row_index_of((NB, LANES))
    col = lane & (NB - 1)
    left = lane < NB
    inside = (row < NBLK) & (col < NBLK)
    lane8 = lane_index((NM, LANES))

    systems, probes = [], []
    for i in range(plan.per):
        folded = packed_ref[i]
        turned = pltpu.roll(folded, NB, 1)
        wide = jnp.concatenate([folded, turned], axis=0)
        twice = jnp.where(left, wide, pltpu.roll(wide, NB, 1))
        flipped = jnp.transpose(jnp.concatenate([twice, twice], axis=0))[:NB]
        real = jnp.where(inside, jnp.where(row >= col, twice, flipped), 0.0) / total_rows
        imag = jnp.where(row < col, twice, jnp.where(row > col, -flipped, 0.0))
        imag = jnp.where(inside, imag, 0.0) / total_rows
        straight = jnp.concatenate(
            [jnp.where(left, real, -imag), jnp.where(left, imag, real)], axis=0
        )
        sides = []
        for system in (straight, turn(straight)):
            high, middle, low = split_three(system)
            sides.append(
                jnp.concatenate(
                    [
                        jnp.concatenate([high, low], axis=1),
                        jnp.concatenate([middle, jnp.zeros_like(low)], axis=1),
                    ],
                    axis=0,
                )
            )
        systems.append(jnp.concatenate(sides, axis=1))
        along = twice[NB - 1 :]
        across = flipped[NB - 1 :]
        left1 = lane_index((1, LANES)) < NB
        probes.append((jnp.where(left1, along, across), jnp.where(left1, -across, along)))

    def image_of(i, v):
        high, middle, low = split_three(v)
        zeros = jnp.zeros_like(high)
        parts = jnp.concatenate(
            [
                jnp.concatenate([high, high], axis=1),
                jnp.concatenate([middle, middle], axis=1),
                jnp.concatenate([low, zeros], axis=1),
                jnp.concatenate([zeros, zeros], axis=1),
            ],
            axis=0,
        )
        out = jnp.dot(parts, systems[i], preferred_element_type=jnp.float32)

        def total(out):
            small = out[:NM, LANES:] + out[2 * NM : 3 * NM, :LANES]
            return out[:NM, :LANES] + (out[NM : 2 * NM, :LANES] + small)

        return total(out[:, : 2 * LANES]), total(out[:, 2 * LANES :])

    start = tuple(start_ref[i] for i in range(plan.per))

    def quick_sweep(index, carry):
        current, worst = carry
        images = [image_of(i, v) for i, v in enumerate(current)]
        done = []
        for y, turned in images:
            v, worst = orthonormalize_quick(y, turned, worst)
            done.append(v)
        return tuple(done), worst

    def checked_sweep(index, current):
        images = [image_of(i, v) for i, v in enumerate(current)]
        return tuple(orthonormalize_checked(y, turned) for y, turned in images)

    basis, worst = lax.fori_loop(
        0, ITERS, quick_sweep, (start, jnp.ones((NM, LANES), jnp.float32))
    )
    for i, v in enumerate(basis):
        basis_ref[i] = v

    @pl.when(jnp.logical_not(jnp.min(worst) >= LEAST_LEFT))
    def _():
        for i, v in enumerate(lax.fori_loop(0, ITERS, checked_sweep, start)):
            basis_ref[i] = v

    extras = jnp.zeros((NM, LANES), jnp.float32)
    scale = 1.0 / math.sqrt(total_rows)
    for i in range(plan.per):
        v = basis_ref[i]
        energy = lane_sum(v * image_of(i, v)[0])
        coef = v.astype(jnp.bfloat16).astype(jnp.float32)
        out_ref[i * NM : (i + 1) * NM] = coef
        gain = 1.0 / jnp.sqrt(energy + EPS)
        tilt_real = gain * (lane_sum(coef * probes[i][0]) * scale)
        tilt_imag = gain * (lane_sum(coef * probes[i][1]) * scale)
        size = jnp.sqrt(jnp.maximum(tilt_real * tilt_real + tilt_imag * tilt_imag, 0.25))
        extras = jnp.where(lane8 == 3 * i, gain * tilt_real / size, extras)
        extras = jnp.where(lane8 == 3 * i + 1, -gain * tilt_imag / size, extras)
        extras = jnp.where(lane8 == 3 * i + 2, energy, extras)
    out_ref[plan.per * NM :] = extras


def solve(plan, total_rows, packed, start):
    return pl.pallas_call(
        functools.partial(solve_kernel, plan, total_rows),
        in_specs=[pl.BlockSpec(memory_space=pltpu.VMEM)] * 2,
        out_specs=pl.BlockSpec(memory_space=pltpu.VMEM),
        out_shape=jax.ShapeDtypeStruct(((plan.per + 1) * NM, LANES), jnp.float32),
        scratch_shapes=[pltpu.VMEM((plan.per, NM, LANES), jnp.float32)],
        compiler_params=pltpu.CompilerParams(vmem_limit_bytes=SOLVE_MIB * MIB),
        name="solve",
    )(packed, start)


def modes_kernel(plan, coef_ref, near_ref, far_ref, weight_ref, out_hbm, energy_ref, out, sems):
    inverse_root = 1.0 / jnp.sqrt(weight_ref[...])
    lane8 = lane_index((NM, LANES))
    left = lane8 < NB
    energies = jnp.zeros((NM, LANES), jnp.float32)
    copies = []
    for f in range(NF):
        slot, same_core = plan.slot_of(f)
        packed = jnp.where(same_core, near_ref[slot], far_ref[slot])
        j = f % plan.per
        c = packed[j * NM : (j + 1) * NM]
        extras = packed[plan.per * NM :]
        factor_real = extras[:, 3 * j : 3 * j + 1]
        factor_imag = extras[:, 3 * j + 1 : 3 * j + 2]
        matrix = jnp.concatenate([jnp.where(left, c, -c), pltpu.roll(c, NB, 1)], axis=0)
        projected = jnp.dot(
            matrix.astype(jnp.bfloat16), coef_ref[f], preferred_element_type=jnp.float32
        )
        real = projected[:NM]
        imag = projected[NM:]
        out[f, :NM, :] = (real * factor_real - imag * factor_imag) * inverse_root
        out[f, NM:, :] = (real * factor_imag + imag * factor_real) * inverse_root
        energies = jnp.where(lane8 == f, extras[:, 3 * j + 2 : 3 * j + 3], energies)
        if (f + 1) % MODES_FREQS == 0:
            done = pl.ds(f + 1 - MODES_FREQS, MODES_FREQS)
            copy = pltpu.make_async_copy(out.at[done], out_hbm.at[done], sems.at[len(copies)])
            copy.start()
            copies.append(copy)
    energy_ref[...] = energies[:, :NF]
    for copy in copies:
        copy.wait()


def modes(plan, coeffs, near, far, weights):
    rows_here = coeffs.shape[2]
    whole = jax.ShapeDtypeStruct((NF, 2 * NM, rows_here), jnp.float32)
    return pl.pallas_call(
        functools.partial(modes_kernel, plan),
        in_specs=[pl.BlockSpec(memory_space=pltpu.VMEM)] * 4,
        out_specs=[
            pl.BlockSpec(memory_space=pltpu.HBM),
            pl.BlockSpec(memory_space=pltpu.VMEM),
        ],
        out_shape=[whole, jax.ShapeDtypeStruct((NM, NF), jnp.float32)],
        scratch_shapes=[
            pltpu.VMEM(whole.shape, whole.dtype),
            pltpu.SemaphoreType.DMA((NF // MODES_FREQS,)),
        ],
        compiler_params=pltpu.CompilerParams(vmem_limit_bytes=MODES_MIB * MIB),
        name="modes",
    )(coeffs, near, far, weights[None])


def swap(x, axis, size, offset):
    return lax.ppermute(x, axis, [(i, i ^ offset) for i in range(size)])


def shards(plan, snapshots, weights, reference_field, start_basis):
    total_rows = snapshots.shape[1] * plan.grp * plan.row
    start = lax.dynamic_slice_in_dim(start_basis, plan.first_freq(0, 0, 0), plan.per, 0)
    start = jnp.pad(start, ((0, 0), (0, 0), (0, NB - NBLK), (0, 0)))
    start = jnp.transpose(start, (0, 3, 1, 2)).reshape(plan.per, NM, 2 * NB)
    snapshots, start = lax.optimization_barrier((snapshots, start))

    coeffs, keep, send = transform(plan, snapshots, weights, reference_field)

    held = keep + swap(send, "row", plan.row, 1)
    if plan.split_grp:
        held = held.reshape((plan.grp, plan.deep * plan.per) + held.shape[1:])
        arrived = [swap(held[d], "grp", plan.grp, d) for d in range(1, plan.grp)]
        held = functools.reduce(jnp.add, arrived, held[0])
    held = held.reshape((plan.deep, plan.per) + held.shape[1:])
    arrived = [swap(held[d], "row", plan.row, 2 * d) for d in range(1, plan.deep)]
    held = functools.reduce(jnp.add, arrived, held[0])
    if not plan.split_grp:
        held = lax.psum(held, "grp")

    payload = solve(plan, total_rows, held, start)

    payload = jnp.stack(
        [payload] + [swap(payload, "row", plan.row, 2 * d) for d in range(1, plan.deep)]
    )
    if plan.split_grp:
        payload = jnp.concatenate(
            [payload] + [swap(payload, "grp", plan.grp, d) for d in range(1, plan.grp)]
        )
    far = swap(payload, "row", plan.row, 1)
    spod_modes, energies = modes(plan, coeffs, payload, far, weights)
    return spod_modes, jnp.transpose(energies)


def solution(mesh):
    plan = Plan(mesh.shape["grp"], mesh.shape["row"])
    in_specs = (P(None, ("grp", "row")), P(("grp", "row")), P(("grp", "row")), P())
    out_specs = (P(None, None, ("grp", "row")), P())
    return jax.shard_map(
        functools.partial(shards, plan),
        mesh=mesh,
        in_specs=in_specs,
        out_specs=out_specs,
        check_vma=False,
    )
```

```python
import functools
import math

import jax
import jax.numpy as jnp
import numpy as np
from jax import lax
from jax.experimental import pallas as pl
from jax.experimental.pallas import tpu as pltpu
from jax.sharding import PartitionSpec as P

NFFT = 256
HALF = NFFT // 2
NBLK = 63
NB = 64
NF = 64
NM = 8
ITERS = 12
EPS = 1e-06
LEAST_LEFT = 1e-03
LANES = 128
PITCH = 2 * NB + 1
MIB = 1024 * 1024
TRANSFORM_MIB, SOLVE_MIB, MODES_MIB = 28, 8, 8


def dft_table():
    time_steps = np.arange(NFFT, dtype=np.int32)
    freq_bins = np.arange(1, NF + 1, dtype=np.int32)
    wrapped = freq_bins[:, None] * time_steps[None, :] % NFFT
    angles = np.float32(2.0 * math.pi / NFFT) * wrapped.astype(np.float32)
    taper = np.float32(0.5) - np.float32(0.5) * np.cos(
        np.float32(2.0 * math.pi / NFFT) * time_steps.astype(np.float32)
    )
    taper = taper / np.sqrt(np.sum(taper * taper))
    stacked = np.concatenate([np.cos(angles), -np.sin(angles)]) * taper[None, :]
    return jnp.asarray(stacked, dtype=jnp.float32).astype(jnp.bfloat16)


class Plan:
    def __init__(self, grp, row):
        self.grp, self.row, self.deep = grp, row, row // 2
        self.split_grp = NF % (grp * row) == 0
        self.g_slots = grp if self.split_grp else 1
        self.owners = row * self.g_slots
        self.per = NF // self.owners

    def half(self, other_core):
        row_index = lax.axis_index("row")
        core = (row_index & 1) ^ int(other_core)
        listed = []
        for q in range(self.owners // 2):
            owner = 2 * q + core
            slot = ((owner % self.row) >> 1) ^ (row_index >> 1)
            if self.split_grp:
                slot = ((owner // self.row) ^ lax.axis_index("grp")) * self.deep + slot
            for j in range(self.per):
                listed.append((q * self.per + j, owner * self.per + j, slot))
        return listed

    def first_freq(self):
        owner = lax.axis_index("row")
        if self.split_grp:
            owner = lax.axis_index("grp") * self.row + owner
        return owner * self.per


def lane_index(shape):
    return lax.broadcasted_iota(jnp.int32, shape, 1)


def row_index_of(shape):
    return lax.broadcasted_iota(jnp.int32, shape, 0)


def pack(top, low):
    row = row_index_of((NB, LANES))
    lane = lane_index((NB, LANES))
    left = lane < NB
    upper = row < (lane & (NB - 1))
    parts = jnp.where(left, jnp.where(upper, -low, top), jnp.where(upper, top, low))
    first, second = parts[: NB // 2], parts[NB // 2 :]
    left_half = left[: NB // 2]
    other = pltpu.roll(jnp.where(left_half, second, first), NB, 1)
    return jnp.where(left_half, first, second) + other


def square(coefs):
    return lax.dot_general(
        coefs, coefs, (((1,), (1,)), ((), ())), preferred_element_type=jnp.float32
    )


def transform_kernel(plan, snap_ref, weight_ref, field_ref, table_ref, coef_ref, send_ref, flip, gram):
    step = pl.program_id(0)
    tile = snap_ref.shape[1]
    pieces = tile // LANES
    table = table_ref[...]
    root = jnp.sqrt(weight_ref[...])
    probe_row = (root * field_ref[...]).astype(jnp.bfloat16).astype(jnp.float32)
    here = pl.ds(pl.multiple_of(step * tile, tile), tile)

    def one_block(b, carry):
        rows = snap_ref[pl.ds(pl.multiple_of(b * HALF, HALF), NFFT), :]
        out = jnp.dot(table, rows, preferred_element_type=jnp.float32) * root
        for part in range(2):
            for piece in range(pieces):
                flip[piece, pl.ds(part * NB + b, NF, stride=PITCH), :] = out[
                    part * NF : (part + 1) * NF, piece * LANES : (piece + 1) * LANES
                ]
        return carry

    lax.fori_loop(0, NBLK, one_block, 0, unroll=NBLK)
    for piece in range(pieces):
        probe = probe_row[:, piece * LANES : (piece + 1) * LANES]
        flip[piece, pl.ds(NB - 1, NF, stride=PITCH), :] = jnp.broadcast_to(probe, (NF, LANES))
        flip[piece, pl.ds(2 * NB - 1, NF, stride=PITCH), :] = jnp.zeros((NF, LANES), jnp.float32)

    @pl.when(step == 0)
    def _():
        gram[...] = jnp.zeros_like(gram)

    def rounded(f):
        wide = jnp.concatenate(
            [flip[piece, pl.ds(f * PITCH, 2 * NB), :] for piece in range(pieces)], axis=1
        )
        coefs = wide.astype(jnp.bfloat16)
        coef_ref[f, :, here] = coefs
        return coefs

    def one_freq(f, carry):
        rounded(f)
        return carry

    lax.fori_loop(0, NF, one_freq, 0, unroll=NF)

    @pl.when(step == pl.num_programs(0) - 1)
    def _():
        for n, f, slot in plan.half(True):
            whole = square(coef_ref[f])
            send_ref[slot * plan.per + n % plan.per] = pack(whole[:NB], whole[NB:])


def transform(plan, snapshots, weights, reference_field):
    rows_here = snapshots.shape[1]
    tile = min(256, rows_here)
    half_freqs = NF // 2
    return pl.pallas_call(
        functools.partial(transform_kernel, plan),
        grid=(rows_here // tile,),
        in_specs=[
            pl.BlockSpec((snapshots.shape[0], tile), lambda i: (0, i)),
            pl.BlockSpec((1, tile), lambda i: (0, i)),
            pl.BlockSpec((1, tile), lambda i: (0, i)),
            pl.BlockSpec((2 * NF, NFFT), lambda i: (0, 0)),
        ],
        out_specs=[pl.BlockSpec(memory_space=pltpu.VMEM)] * 2,
        out_shape=[
            jax.ShapeDtypeStruct((NF, 2 * NB, rows_here), jnp.bfloat16),
            jax.ShapeDtypeStruct((half_freqs, NB // 2, LANES), jnp.float32),
        ],
        scratch_shapes=[
            pltpu.VMEM((tile // LANES, NF * PITCH, LANES), jnp.float32),
            pltpu.VMEM((half_freqs, 2 * NB, LANES), jnp.float32),
        ],
        compiler_params=pltpu.CompilerParams(vmem_limit_bytes=TRANSFORM_MIB * MIB),
        name="transform",
    )(snapshots, weights[None], reference_field[None], dft_table())


def own_gram_kernel(plan, coef_ref, keep_ref):
    for n, f, slot in plan.half(False):
        whole = square(coef_ref[f])
        keep_ref[slot * plan.per + n % plan.per] = pack(whole[:NB], whole[NB:])


def own_gram(plan, coeffs):
    freqs, rows, columns = coeffs.shape
    return pl.pallas_call(
        functools.partial(own_gram_kernel, plan),
        in_specs=[pl.BlockSpec(memory_space=pltpu.VMEM)],
        out_specs=pl.BlockSpec(memory_space=pltpu.VMEM),
        out_shape=jax.ShapeDtypeStruct((NF // 2, NB // 2, LANES), jnp.float32),
        cost_estimate=pl.CostEstimate(
            flops=freqs * rows * rows * columns, bytes_accessed=freqs * rows * columns, transcendentals=0
        ),
        compiler_params=pltpu.CompilerParams(vmem_limit_bytes=SOLVE_MIB * MIB),
        name="own_gram",
    )(coeffs)


def start_kernel(plan, basis_ref, out_ref):
    lane = lane_index((NM, LANES))
    lane_in = lane_index((NM, basis_ref.shape[3]))
    for j in range(plan.per):
        chosen = lane_in == plan.first_freq() + j
        rows = jnp.zeros((NM, LANES), jnp.float32)
        for part in range(2):
            for b in range(NBLK):
                value = jnp.sum(jnp.where(chosen, basis_ref[part, b], 0.0), axis=1, keepdims=True)
                rows = jnp.where(lane == part * NB + b, value, rows)
        out_ref[j] = rows


def start_rows(plan, start_basis):
    return pl.pallas_call(
        functools.partial(start_kernel, plan),
        in_specs=[pl.BlockSpec(memory_space=pltpu.VMEM)],
        out_specs=pl.BlockSpec(memory_space=pltpu.VMEM),
        out_shape=jax.ShapeDtypeStruct((plan.per, NM, LANES), jnp.float32),
        compiler_params=pltpu.CompilerParams(vmem_limit_bytes=SOLVE_MIB * MIB),
        name="start_rows",
    )(jnp.transpose(start_basis, (1, 2, 3, 0)))


def split_three(x):
    high = x.astype(jnp.bfloat16)
    rest = x - high.astype(jnp.float32)
    middle = rest.astype(jnp.bfloat16)
    low = (rest - middle.astype(jnp.float32)).astype(jnp.bfloat16)
    return high, middle, low


def turn(y):
    swapped = pltpu.roll(y, NB, 1)
    return jnp.where(lane_index(y.shape) < NB, -swapped, swapped)


def lane_sum(x):
    return jnp.broadcast_to(jnp.sum(x, axis=1, keepdims=True), x.shape)


def spread(x, j):
    return jnp.broadcast_to(x[j : j + 1], x.shape)


def orthonormalize_checked(y, turned):
    row = row_index_of(y.shape)
    v = jnp.zeros_like(y)
    for j in range(NM):
        pivot, pivot_turned = spread(y, j), spread(turned, j)
        size = lane_sum(pivot * pivot) + EPS
        v = jnp.where(row == j, pivot * lax.rsqrt(size), v)
        if j < NM - 1:
            inverse = 1.0 / size
            a = jnp.where(row > j, lane_sum(pivot * y) * inverse, 0.0)
            c = jnp.where(row > j, lane_sum(pivot_turned * y) * inverse, 0.0)
            y, turned = (
                y - (a * pivot + c * pivot_turned),
                turned - (a * pivot_turned - c * pivot),
            )
    return v


def orthonormalize_quick(y, turned, worst):
    row = row_index_of(y.shape)
    real = [lane_sum(spread(y, j) * y) for j in range(NM)]
    imag = [lane_sum(spread(turned, j) * y) for j in range(NM - 1)]
    whole = [spread(real[j], j) + EPS for j in range(NM)]
    v = jnp.zeros_like(y)
    for j in range(NM):
        pivot, pivot_turned = spread(y, j), spread(turned, j)
        size = jnp.maximum(spread(real[j], j), 0.0) + EPS
        worst = jnp.minimum(worst, size / whole[j])
        v = jnp.where(row == j, pivot * lax.rsqrt(size), v)
        if j < NM - 1:
            inverse = 1.0 / size
            scale = (size + EPS) * inverse * inverse
            scaled_real, scaled_imag = real[j] * scale, imag[j] * scale
            for l in range(j + 1, NM):
                other_real, other_imag = spread(real[j], l), spread(imag[j], l)
                real[l] = real[l] - (scaled_real * other_real + scaled_imag * other_imag)
                if l < NM - 1:
                    imag[l] = imag[l] - (scaled_imag * other_real - scaled_real * other_imag)
            a = jnp.where(row > j, real[j] * inverse, 0.0)
            c = jnp.where(row > j, imag[j] * inverse, 0.0)
            y, turned = (
                y - (a * pivot + c * pivot_turned),
                turned - (a * pivot_turned - c * pivot),
            )
    return v, worst


def solve_kernel(plan, total_rows, packed_ref, start_ref, out_ref, basis_ref):
    lane = lane_index((NB, LANES))
    row = row_index_of((NB, LANES))
    col = lane & (NB - 1)
    left = lane < NB
    inside = (row < NBLK) & (col < NBLK)
    lane8 = lane_index((NM, LANES))

    systems, probes = [], []
    for i in range(plan.per):
        folded = packed_ref[i]
        turned = pltpu.roll(folded, NB, 1)
        wide = jnp.concatenate([folded, turned], axis=0)
        twice = jnp.where(left, wide, pltpu.roll(wide, NB, 1))
        flipped = jnp.transpose(jnp.concatenate([twice, twice], axis=0))[:NB]
        real = jnp.where(inside, jnp.where(row >= col, twice, flipped), 0.0) / total_rows
        imag = jnp.where(row < col, twice, jnp.where(row > col, -flipped, 0.0))
        imag = jnp.where(inside, imag, 0.0) / total_rows
        straight = jnp.concatenate(
            [jnp.where(left, real, -imag), jnp.where(left, imag, real)], axis=0
        )
        sides = []
        for system in (straight, turn(straight)):
            high, middle, low = split_three(system)
            sides.append(
                jnp.concatenate(
                    [
                        jnp.concatenate([high, low], axis=1),
                        jnp.concatenate([middle, jnp.zeros_like(low)], axis=1),
                    ],
                    axis=0,
                )
            )
        systems.append(jnp.concatenate(sides, axis=1))
        along = twice[NB - 1 :]
        across = flipped[NB - 1 :]
        left1 = lane_index((1, LANES)) < NB
        probes.append((jnp.where(left1, along, across), jnp.where(left1, -across, along)))

    def image_of(i, v):
        high, middle, low = split_three(v)
        zeros = jnp.zeros_like(high)
        parts = jnp.concatenate(
            [
                jnp.concatenate([high, high], axis=1),
                jnp.concatenate([middle, middle], axis=1),
                jnp.concatenate([low, zeros], axis=1),
                jnp.concatenate([zeros, zeros], axis=1),
            ],
            axis=0,
        )
        out = jnp.dot(parts, systems[i], preferred_element_type=jnp.float32)

        def total(out):
            small = out[:NM, LANES:] + out[2 * NM : 3 * NM, :LANES]
            return out[:NM, :LANES] + (out[NM : 2 * NM, :LANES] + small)

        return total(out[:, : 2 * LANES]), total(out[:, 2 * LANES :])

    start = tuple(start_ref[i] for i in range(plan.per))

    def quick_sweep(index, carry):
        current, worst = carry
        images = [image_of(i, v) for i, v in enumerate(current)]
        done = []
        for y, turned in images:
            v, worst = orthonormalize_quick(y, turned, worst)
            done.append(v)
        return tuple(done), worst

    def checked_sweep(index, current):
        images = [image_of(i, v) for i, v in enumerate(current)]
        return tuple(orthonormalize_checked(y, turned) for y, turned in images)

    basis, worst = lax.fori_loop(
        0, ITERS, quick_sweep, (start, jnp.ones((NM, LANES), jnp.float32))
    )
    for i, v in enumerate(basis):
        basis_ref[i] = v

    @pl.when(jnp.logical_not(jnp.min(worst) >= LEAST_LEFT))
    def _():
        for i, v in enumerate(lax.fori_loop(0, ITERS, checked_sweep, start)):
            basis_ref[i] = v

    extras = jnp.zeros((NM, LANES), jnp.float32)
    scale = 1.0 / math.sqrt(total_rows)
    for i in range(plan.per):
        v = basis_ref[i]
        energy = lane_sum(v * image_of(i, v)[0])
        coef = v.astype(jnp.bfloat16).astype(jnp.float32)
        out_ref[i * NM : (i + 1) * NM] = coef
        gain = 1.0 / jnp.sqrt(energy + EPS)
        tilt_real = gain * (lane_sum(coef * probes[i][0]) * scale)
        tilt_imag = gain * (lane_sum(coef * probes[i][1]) * scale)
        size = jnp.sqrt(jnp.maximum(tilt_real * tilt_real + tilt_imag * tilt_imag, 0.25))
        extras = jnp.where(lane8 == 3 * i, gain * tilt_real / size, extras)
        extras = jnp.where(lane8 == 3 * i + 1, -gain * tilt_imag / size, extras)
        extras = jnp.where(lane8 == 3 * i + 2, energy, extras)
    out_ref[plan.per * NM :] = extras


def solve(plan, total_rows, packed, start):
    return pl.pallas_call(
        functools.partial(solve_kernel, plan, total_rows),
        in_specs=[pl.BlockSpec(memory_space=pltpu.VMEM)] * 2,
        out_specs=pl.BlockSpec(memory_space=pltpu.VMEM),
        out_shape=jax.ShapeDtypeStruct(((plan.per + 1) * NM, LANES), jnp.float32),
        scratch_shapes=[pltpu.VMEM((plan.per, NM, LANES), jnp.float32)],
        compiler_params=pltpu.CompilerParams(vmem_limit_bytes=SOLVE_MIB * MIB),
        name="solve",
    )(packed, start)


def modes_kernel(plan, other_core, coef_ref, pay_ref, weight_ref, *refs):
    out_hbm, energy_ref, out, sems = refs[-4:]
    inverse_root = 1.0 / jnp.sqrt(weight_ref[...])
    lane8 = lane_index((NM, LANES))
    left = lane8 < NB
    energies = jnp.zeros((NM, LANES), jnp.float32)
    copies = []
    for n, f, slot in plan.half(other_core):
        j = n % plan.per
        c = pay_ref[slot, j * NM : (j + 1) * NM]
        extras = pay_ref[slot, plan.per * NM :]
        factor_real = extras[:, 3 * j : 3 * j + 1]
        factor_imag = extras[:, 3 * j + 1 : 3 * j + 2]
        matrix = jnp.concatenate([jnp.where(left, c, -c), pltpu.roll(c, NB, 1)], axis=0)
        projected = jnp.dot(
            matrix.astype(jnp.bfloat16), coef_ref[f], preferred_element_type=jnp.float32
        )
        real = projected[:NM]
        imag = projected[NM:]
        out[n, :NM, :] = (real * factor_real - imag * factor_imag) * inverse_root
        out[n, NM:, :] = (real * factor_imag + imag * factor_real) * inverse_root
        energies = jnp.where(lane8 == f, extras[:, 3 * j + 2 : 3 * j + 3], energies)
        if j == plan.per - 1:
            copy = pltpu.make_async_copy(
                out.at[pl.ds(n - j, plan.per)],
                out_hbm.at[pl.ds(f - j, plan.per)],
                sems.at[len(copies)],
            )
            copy.start()
            copies.append(copy)
    energies = energies[:, :NF]
    energy_ref[...] = energies + refs[1][...] if other_core else energies
    for copy in copies:
        copy.wait()


def modes(plan, coeffs, payload, weights, earlier=()):
    rows_here = coeffs.shape[2]
    whole = jax.ShapeDtypeStruct((NF, 2 * NM, rows_here), jnp.float32)
    places = [pltpu.HBM, pltpu.VMEM]
    return pl.pallas_call(
        functools.partial(modes_kernel, plan, bool(earlier)),
        in_specs=[pl.BlockSpec(memory_space=pltpu.VMEM)] * 3
        + [pl.BlockSpec(memory_space=place) for place in places[: len(earlier)]],
        out_specs=[pl.BlockSpec(memory_space=place) for place in places],
        out_shape=[whole, jax.ShapeDtypeStruct((NM, NF), jnp.float32)],
        input_output_aliases={3: 0} if earlier else {},
        scratch_shapes=[
            pltpu.VMEM((NF // 2,) + whole.shape[1:], whole.dtype),
            pltpu.SemaphoreType.DMA((plan.owners // 2,)),
        ],
        cost_estimate=pl.CostEstimate(
            flops=2 * NF * NM * 2 * NB * rows_here,
            bytes_accessed=2 * NF * NM * 4 * rows_here,
            transcendentals=0,
        ),
        compiler_params=pltpu.CompilerParams(vmem_limit_bytes=MODES_MIB * MIB),
        name="other_modes" if earlier else "own_modes",
    )(coeffs, payload, weights[None], *earlier)


def swap(x, axis, size, offset):
    return lax.ppermute(x, axis, [(i, i ^ offset) for i in range(size)])


def shards(plan, snapshots, weights, reference_field, start_basis):
    total_rows = snapshots.shape[1] * plan.grp * plan.row
    coeffs, send = transform(plan, snapshots, weights, reference_field)
    start_basis, send = lax.optimization_barrier((start_basis, send))
    start = start_rows(plan, start_basis)

    arrived = swap(send, "row", plan.row, 1)
    held = own_gram(plan, coeffs) + arrived
    if plan.split_grp:
        held = held.reshape((plan.grp, plan.deep * plan.per) + held.shape[1:])
        arrived = [swap(held[d], "grp", plan.grp, d) for d in range(1, plan.grp)]
        held = functools.reduce(jnp.add, arrived, held[0])
    held = held.reshape((plan.deep, plan.per) + held.shape[1:])
    arrived = [swap(held[d], "row", plan.row, 2 * d) for d in range(1, plan.deep)]
    held = functools.reduce(jnp.add, arrived, held[0])
    if not plan.split_grp:
        held = lax.psum(held, "grp")

    payload = solve(plan, total_rows, held, start)

    payload = jnp.stack(
        [payload] + [swap(payload, "row", plan.row, 2 * d) for d in range(1, plan.deep)]
    )
    if plan.split_grp:
        payload = jnp.concatenate(
            [payload] + [swap(payload, "grp", plan.grp, d) for d in range(1, plan.grp)]
        )
    far = swap(payload, "row", plan.row, 1)
    own = modes(plan, coeffs, payload, weights)
    spod_modes, energies = modes(plan, coeffs, far, weights, own)
    return spod_modes, jnp.transpose(energies)


def solution(mesh):
    plan = Plan(mesh.shape["grp"], mesh.shape["row"])
    in_specs = (P(None, ("grp", "row")), P(("grp", "row")), P(("grp", "row")), P())
    out_specs = (P(None, None, ("grp", "row")), P())
    return jax.shard_map(
        functools.partial(shards, plan),
        mesh=mesh,
        in_specs=in_specs,
        out_specs=out_specs,
        check_vma=False,
    )
```

```python
import functools
import math

import jax
import jax.numpy as jnp
import numpy as np
from jax import lax
from jax.experimental import pallas as pl
from jax.experimental.pallas import tpu as pltpu
from jax.sharding import Mesh
from jax.sharding import PartitionSpec as P

NFFT = 256
HALF = NFFT // 2
NBLK = 63
NB = 64
NF = 64
NM = 8
ITERS = 12
EPS = 1e-06
LEAST_LEFT = 1e-03
LANES = 128
PITCH = 2 * NB + 1
MIB = 1024 * 1024
TRANSFORM_MIB, SOLVE_MIB, MODES_MIB = 28, 8, 8


def dft_table():
    time_steps = np.arange(NFFT, dtype=np.int32)
    freq_bins = np.arange(1, NF + 1, dtype=np.int32)
    wrapped = freq_bins[:, None] * time_steps[None, :] % NFFT
    angles = np.float32(2.0 * math.pi / NFFT) * wrapped.astype(np.float32)
    taper = np.float32(0.5) - np.float32(0.5) * np.cos(
        np.float32(2.0 * math.pi / NFFT) * time_steps.astype(np.float32)
    )
    taper = taper / np.sqrt(np.sum(taper * taper))
    stacked = np.concatenate([np.cos(angles), -np.sin(angles)]) * taper[None, :]
    return jnp.asarray(stacked, dtype=jnp.float32).astype(jnp.bfloat16)


class Plan:
    def __init__(self, grp, row):
        self.grp, self.deep = grp, row // 2
        self.split_grp = NF % (grp * row) == 0
        self.chips = self.deep * (grp if self.split_grp else 1)
        self.chip_axes = ("grp", "z") if self.split_grp else ("z",)
        self.per = NF // (2 * self.chips)

    def chip(self):
        z = lax.axis_index("z")
        return lax.axis_index("grp") * self.deep + z if self.split_grp else z

    def first_freq(self):
        return (self.chip() * 2 + lax.axis_index("core")) * self.per

    def half(self, other_core):
        core = lax.axis_index("core") ^ int(other_core)
        return [
            (chip, (2 * chip + core) * self.per + j)
            for chip in range(self.chips)
            for j in range(self.per)
        ]


def lane_index(shape):
    return lax.broadcasted_iota(jnp.int32, shape, 1)


def row_index_of(shape):
    return lax.broadcasted_iota(jnp.int32, shape, 0)


def pack(top, low):
    row = row_index_of((NB, LANES))
    lane = lane_index((NB, LANES))
    left = lane < NB
    upper = row < (lane & (NB - 1))
    parts = jnp.where(left, jnp.where(upper, -low, top), jnp.where(upper, top, low))
    first, second = parts[: NB // 2], parts[NB // 2 :]
    left_half = left[: NB // 2]
    other = pltpu.roll(jnp.where(left_half, second, first), NB, 1)
    return jnp.where(left_half, first, second) + other


def pack_half(plan, other_core, coef_ref, out_ref):
    for n, (chip, f) in enumerate(plan.half(other_core)):
        coefs = coef_ref[f]
        whole = lax.dot_general(
            coefs, coefs, (((1,), (1,)), ((), ())), preferred_element_type=jnp.float32
        )
        place = (plan.chip() ^ chip) * plan.per + n % plan.per
        out_ref[place] = pack(whole[:NB], whole[NB:])


def transform_kernel(plan, snap_ref, weight_ref, field_ref, table_ref, coef_ref, send_ref, flip):
    step = pl.program_id(0)
    tile = snap_ref.shape[1]
    pieces = tile // LANES
    table = table_ref[...]
    root = jnp.sqrt(weight_ref[...])
    probe_row = (root * field_ref[...]).astype(jnp.bfloat16).astype(jnp.float32)
    here = pl.ds(pl.multiple_of(step * tile, tile), tile)

    def one_block(b, carry):
        rows = snap_ref[pl.ds(pl.multiple_of(b * HALF, HALF), NFFT), :]
        out = jnp.dot(table, rows, preferred_element_type=jnp.float32) * root
        for part in range(2):
            for piece in range(pieces):
                flip[piece, pl.ds(part * NB + b, NF, stride=PITCH), :] = out[
                    part * NF : (part + 1) * NF, piece * LANES : (piece + 1) * LANES
                ]
        return carry

    lax.fori_loop(0, NBLK, one_block, 0, unroll=NBLK)
    for piece in range(pieces):
        probe = probe_row[:, piece * LANES : (piece + 1) * LANES]
        flip[piece, pl.ds(NB - 1, NF, stride=PITCH), :] = jnp.broadcast_to(probe, (NF, LANES))
        flip[piece, pl.ds(2 * NB - 1, NF, stride=PITCH), :] = jnp.zeros((NF, LANES), jnp.float32)

    def one_freq(f, carry):
        wide = jnp.concatenate(
            [flip[piece, pl.ds(f * PITCH, 2 * NB), :] for piece in range(pieces)], axis=1
        )
        coefs = wide.astype(jnp.bfloat16)
        coef_ref[f, :, here] = coefs
        return carry

    lax.fori_loop(0, NF, one_freq, 0, unroll=NF)

    @pl.when(step == pl.num_programs(0) - 1)
    def _():
        pack_half(plan, True, coef_ref, send_ref)


def transform(plan, snapshots, weights, reference_field):
    rows_here = snapshots.shape[1]
    tile = min(256, rows_here)
    half_freqs = NF // 2
    return pl.pallas_call(
        functools.partial(transform_kernel, plan),
        grid=(rows_here // tile,),
        in_specs=[
            pl.BlockSpec((snapshots.shape[0], tile), lambda i: (0, i)),
            pl.BlockSpec((1, tile), lambda i: (0, i)),
            pl.BlockSpec((1, tile), lambda i: (0, i)),
            pl.BlockSpec((2 * NF, NFFT), lambda i: (0, 0)),
        ],
        out_specs=[pl.BlockSpec(memory_space=pltpu.VMEM)] * 2,
        out_shape=[
            jax.ShapeDtypeStruct((NF, 2 * NB, rows_here), jnp.bfloat16),
            jax.ShapeDtypeStruct((half_freqs, NB // 2, LANES), jnp.float32),
        ],
        scratch_shapes=[
            pltpu.VMEM((tile // LANES, NF * PITCH, LANES), jnp.float32),
        ],
        compiler_params=pltpu.CompilerParams(vmem_limit_bytes=TRANSFORM_MIB * MIB),
        name="transform",
    )(snapshots, *(pltpu.with_memory_space_constraint(x, pltpu.HBM) for x in (weights[None], reference_field[None])), dft_table())


def own_gram_kernel(plan, coef_ref, keep_ref):
    pack_half(plan, False, coef_ref, keep_ref)


def own_gram(plan, coeffs):
    freqs, rows, columns = coeffs.shape
    return pl.pallas_call(
        functools.partial(own_gram_kernel, plan),
        in_specs=[pl.BlockSpec(memory_space=pltpu.VMEM)],
        out_specs=pl.BlockSpec(memory_space=pltpu.VMEM),
        out_shape=jax.ShapeDtypeStruct((NF // 2, NB // 2, LANES), jnp.float32),
        cost_estimate=pl.CostEstimate(
            flops=freqs * rows * rows * columns, bytes_accessed=freqs * rows * columns, transcendentals=0
        ),
        compiler_params=pltpu.CompilerParams(vmem_limit_bytes=SOLVE_MIB * MIB),
        name="own_gram",
    )(coeffs)


def start_kernel(plan, basis_ref, out_ref):
    lane = lane_index((NM, LANES))
    lane_in = lane_index((NM, basis_ref.shape[3]))
    for j in range(plan.per):
        chosen = lane_in == plan.first_freq() + j
        rows = jnp.zeros((NM, LANES), jnp.float32)
        for part in range(2):
            for b in range(NBLK):
                value = jnp.sum(jnp.where(chosen, basis_ref[part, b], 0.0), axis=1, keepdims=True)
                rows = jnp.where(lane == part * NB + b, value, rows)
        out_ref[j] = rows


def start_rows(plan, start_basis):
    return pl.pallas_call(
        functools.partial(start_kernel, plan),
        in_specs=[pl.BlockSpec(memory_space=pltpu.VMEM)],
        out_specs=pl.BlockSpec(memory_space=pltpu.VMEM),
        out_shape=jax.ShapeDtypeStruct((plan.per, NM, LANES), jnp.float32),
        compiler_params=pltpu.CompilerParams(vmem_limit_bytes=SOLVE_MIB * MIB),
        name="start_rows",
    )(jnp.transpose(start_basis, (1, 2, 3, 0)))


def split_three(x):
    high = x.astype(jnp.bfloat16)
    rest = x - high.astype(jnp.float32)
    middle = rest.astype(jnp.bfloat16)
    low = (rest - middle.astype(jnp.float32)).astype(jnp.bfloat16)
    return high, middle, low


def turn(y):
    swapped = pltpu.roll(y, NB, 1)
    return jnp.where(lane_index(y.shape) < NB, -swapped, swapped)


def lane_sum(x):
    return jnp.broadcast_to(jnp.sum(x, axis=1, keepdims=True), x.shape)


def spread(x, j):
    return jnp.broadcast_to(x[j : j + 1], x.shape)


def orthonormalize_checked(y, turned):
    row = row_index_of(y.shape)
    v = jnp.zeros_like(y)
    for j in range(NM):
        pivot, pivot_turned = spread(y, j), spread(turned, j)
        size = lane_sum(pivot * pivot) + EPS
        v = jnp.where(row == j, pivot * lax.rsqrt(size), v)
        if j < NM - 1:
            inverse = 1.0 / size
            a = jnp.where(row > j, lane_sum(pivot * y) * inverse, 0.0)
            c = jnp.where(row > j, lane_sum(pivot_turned * y) * inverse, 0.0)
            y, turned = (
                y - (a * pivot + c * pivot_turned),
                turned - (a * pivot_turned - c * pivot),
            )
    return v


def orthonormalize_quick(y, turned, worst):
    row = row_index_of(y.shape)
    real = [lane_sum(spread(y, j) * y) for j in range(NM)]
    imag = [lane_sum(spread(turned, j) * y) for j in range(NM - 1)]
    whole = [spread(real[j], j) + EPS for j in range(NM)]
    v = jnp.zeros_like(y)
    for j in range(NM):
        pivot, pivot_turned = spread(y, j), spread(turned, j)
        size = jnp.maximum(spread(real[j], j), 0.0) + EPS
        worst = jnp.minimum(worst, size / whole[j])
        v = jnp.where(row == j, pivot * lax.rsqrt(size), v)
        if j < NM - 1:
            inverse = 1.0 / size
            scale = (size + EPS) * inverse * inverse
            scaled_real, scaled_imag = real[j] * scale, imag[j] * scale
            for l in range(j + 1, NM):
                other_real, other_imag = spread(real[j], l), spread(imag[j], l)
                real[l] = real[l] - (scaled_real * other_real + scaled_imag * other_imag)
                if l < NM - 1:
                    imag[l] = imag[l] - (scaled_imag * other_real - scaled_real * other_imag)
            a = jnp.where(row > j, real[j] * inverse, 0.0)
            c = jnp.where(row > j, imag[j] * inverse, 0.0)
            y, turned = (
                y - (a * pivot + c * pivot_turned),
                turned - (a * pivot_turned - c * pivot),
            )
    return v, worst


def solve_kernel(plan, total_rows, packed_ref, start_ref, out_ref, basis_ref):
    lane = lane_index((NB, LANES))
    row = row_index_of((NB, LANES))
    col = lane & (NB - 1)
    left = lane < NB
    inside = (row < NBLK) & (col < NBLK)
    lane8 = lane_index((NM, LANES))

    systems, probes = [], []
    for i in range(plan.per):
        folded = packed_ref[i]
        turned = pltpu.roll(folded, NB, 1)
        wide = jnp.concatenate([folded, turned], axis=0)
        twice = jnp.where(left, wide, pltpu.roll(wide, NB, 1))
        flipped = jnp.transpose(jnp.concatenate([twice, twice], axis=0))[:NB]
        real = jnp.where(inside, jnp.where(row >= col, twice, flipped), 0.0) / total_rows
        imag = jnp.where(row < col, twice, jnp.where(row > col, -flipped, 0.0))
        imag = jnp.where(inside, imag, 0.0) / total_rows
        straight = jnp.concatenate(
            [jnp.where(left, real, -imag), jnp.where(left, imag, real)], axis=0
        )
        sides = []
        for system in (straight, turn(straight)):
            high, middle, low = split_three(system)
            sides.append(
                jnp.concatenate(
                    [
                        jnp.concatenate([high, low], axis=1),
                        jnp.concatenate([middle, jnp.zeros_like(low)], axis=1),
                    ],
                    axis=0,
                )
            )
        systems.append(jnp.concatenate(sides, axis=1))
        along = twice[NB - 1 :]
        across = flipped[NB - 1 :]
        left1 = lane_index((1, LANES)) < NB
        probes.append((jnp.where(left1, along, across), jnp.where(left1, -across, along)))

    def image_of(i, v):
        high, middle, low = split_three(v)
        zeros = jnp.zeros_like(high)
        parts = jnp.concatenate(
            [
                jnp.concatenate([high, high], axis=1),
                jnp.concatenate([middle, middle], axis=1),
                jnp.concatenate([low, zeros], axis=1),
                jnp.concatenate([zeros, zeros], axis=1),
            ],
            axis=0,
        )
        out = jnp.dot(parts, systems[i], preferred_element_type=jnp.float32)

        def total(out):
            small = out[:NM, LANES:] + out[2 * NM : 3 * NM, :LANES]
            return out[:NM, :LANES] + (out[NM : 2 * NM, :LANES] + small)

        return total(out[:, : 2 * LANES]), total(out[:, 2 * LANES :])

    start = tuple(start_ref[i] for i in range(plan.per))

    def quick_sweep(index, carry):
        current, worst = carry
        images = [image_of(i, v) for i, v in enumerate(current)]
        done = []
        for y, turned in images:
            v, worst = orthonormalize_quick(y, turned, worst)
            done.append(v)
        return tuple(done), worst

    def checked_sweep(index, current):
        images = [image_of(i, v) for i, v in enumerate(current)]
        return tuple(orthonormalize_checked(y, turned) for y, turned in images)

    basis, worst = lax.fori_loop(
        0, ITERS, quick_sweep, (start, jnp.ones((NM, LANES), jnp.float32))
    )
    for i, v in enumerate(basis):
        basis_ref[i] = v

    @pl.when(jnp.logical_not(jnp.min(worst) >= LEAST_LEFT))
    def _():
        for i, v in enumerate(lax.fori_loop(0, ITERS, checked_sweep, start)):
            basis_ref[i] = v

    extras = jnp.zeros((NM, LANES), jnp.float32)
    scale = 1.0 / math.sqrt(total_rows)
    for i in range(plan.per):
        v = basis_ref[i]
        energy = lane_sum(v * image_of(i, v)[0])
        coef = v.astype(jnp.bfloat16).astype(jnp.float32)
        out_ref[i * NM : (i + 1) * NM] = coef
        gain = 1.0 / jnp.sqrt(energy + EPS)
        tilt_real = gain * (lane_sum(coef * probes[i][0]) * scale)
        tilt_imag = gain * (lane_sum(coef * probes[i][1]) * scale)
        size = jnp.sqrt(jnp.maximum(tilt_real * tilt_real + tilt_imag * tilt_imag, 0.25))
        extras = jnp.where(lane8 == 3 * i, gain * tilt_real / size, extras)
        extras = jnp.where(lane8 == 3 * i + 1, -gain * tilt_imag / size, extras)
        extras = jnp.where(lane8 == 3 * i + 2, energy, extras)
    out_ref[plan.per * NM :] = extras


def solve(plan, total_rows, packed, start):
    return pl.pallas_call(
        functools.partial(solve_kernel, plan, total_rows),
        in_specs=[pl.BlockSpec(memory_space=pltpu.VMEM)] * 2,
        out_specs=pl.BlockSpec(memory_space=pltpu.VMEM),
        out_shape=jax.ShapeDtypeStruct(((plan.per + 1) * NM, LANES), jnp.float32),
        scratch_shapes=[pltpu.VMEM((plan.per, NM, LANES), jnp.float32)],
        compiler_params=pltpu.CompilerParams(vmem_limit_bytes=SOLVE_MIB * MIB),
        name="solve",
    )(packed, start)


def modes_kernel(plan, other_core, coef_ref, pay_ref, weight_ref, *refs):
    out_hbm, energy_ref, out, sems = refs[-4:]
    inverse_root = 1.0 / jnp.sqrt(weight_ref[...])
    lane8 = lane_index((NM, LANES))
    left = lane8 < NB
    energies = jnp.zeros((NM, LANES), jnp.float32)
    copies = []
    for n, (chip, f) in enumerate(plan.half(other_core)):
        j = n % plan.per
        c = pay_ref[chip, j * NM : (j + 1) * NM]
        extras = pay_ref[chip, plan.per * NM :]
        factor_real = extras[:, 3 * j : 3 * j + 1]
        factor_imag = extras[:, 3 * j + 1 : 3 * j + 2]
        matrix = jnp.concatenate([jnp.where(left, c, -c), pltpu.roll(c, NB, 1)], axis=0)
        projected = jnp.dot(
            matrix.astype(jnp.bfloat16), coef_ref[f], preferred_element_type=jnp.float32
        )
        real = projected[:NM]
        imag = projected[NM:]
        out[n, :NM, :] = (real * factor_real - imag * factor_imag) * inverse_root
        out[n, NM:, :] = (real * factor_imag + imag * factor_real) * inverse_root
        energies = jnp.where(lane8 == f, extras[:, 3 * j + 2 : 3 * j + 3], energies)
        if j == plan.per - 1:
            copy = pltpu.make_async_copy(
                out.at[pl.ds(n - j, plan.per)],
                out_hbm.at[pl.ds(f - j, plan.per)],
                sems.at[len(copies)],
            )
            copy.start()
            copies.append(copy)
    energies = energies[:, :NF]
    energy_ref[...] = energies + refs[1][...] if other_core else energies
    for copy in copies:
        copy.wait()


def modes(plan, coeffs, payload, weights, earlier=()):
    rows_here = coeffs.shape[2]
    whole = jax.ShapeDtypeStruct((NF, 2 * NM, rows_here), jnp.float32)
    places = [pltpu.HBM, pltpu.VMEM]
    return pl.pallas_call(
        functools.partial(modes_kernel, plan, bool(earlier)),
        in_specs=[pl.BlockSpec(memory_space=pltpu.VMEM)] * 3
        + [pl.BlockSpec(memory_space=place) for place in places[: len(earlier)]],
        out_specs=[pl.BlockSpec(memory_space=place) for place in places],
        out_shape=[whole, jax.ShapeDtypeStruct((NM, NF), jnp.float32)],
        input_output_aliases={3: 0} if earlier else {},
        scratch_shapes=[
            pltpu.VMEM((NF // 2,) + whole.shape[1:], whole.dtype),
            pltpu.SemaphoreType.DMA((plan.chips,)),
        ],
        cost_estimate=pl.CostEstimate(
            flops=2 * NF * NM * 2 * NB * rows_here,
            bytes_accessed=2 * NF * NM * 4 * rows_here,
            transcendentals=0,
        ),
        compiler_params=pltpu.CompilerParams(vmem_limit_bytes=MODES_MIB * MIB),
        name="other_modes" if earlier else "own_modes",
    )(coeffs, payload, weights[None], *earlier)


def swap(x, axis, size, offset):
    return lax.ppermute(x, axis, [(i, i ^ offset) for i in range(size)])


def shards(plan, snapshots, weights, reference_field, start_basis):
    total_rows = snapshots.shape[1] * plan.grp * plan.deep * 2
    coeffs, send = transform(plan, snapshots, weights, reference_field)
    start_basis, send = lax.optimization_barrier((start_basis, send))
    start = start_rows(plan, start_basis)

    arrived = swap(send, "core", 2, 1)
    held = own_gram(plan, coeffs) + arrived
    if plan.split_grp:
        held = held.reshape((plan.grp, plan.deep * plan.per) + held.shape[1:])
        arrived = [
            swap(held[d].astype(jnp.bfloat16), "grp", plan.grp, d).astype(jnp.float32) for d in range(1, plan.grp)
        ]
        held = functools.reduce(jnp.add, arrived, held[0])
    held = held.reshape((plan.deep, plan.per) + held.shape[1:])
    arrived = [swap(held[d], "z", plan.deep, d) for d in range(1, plan.deep)]
    held = functools.reduce(jnp.add, arrived, held[0])
    if not plan.split_grp:
        held = lax.psum(held, "grp")

    payload = solve(plan, total_rows, held, start)
    payload = jnp.broadcast_to(payload, (plan.chips,) + payload.shape)
    payload = lax.all_to_all(payload, plan.chip_axes, 0, 0, tiled=True)
    far = swap(payload, "core", 2, 1)
    own = modes(plan, coeffs, payload, weights)
    spod_modes, energies = modes(plan, coeffs, far, weights, own)
    return spod_modes, jnp.transpose(energies)


def solution(mesh):
    plan = Plan(mesh.shape["grp"], mesh.shape["row"])
    parted = Mesh(mesh.devices.reshape(plan.grp, plan.deep, 2), ("grp", "z", "core"))
    rows = ("grp", "z", "core")
    in_specs = (P(None, rows), P(rows), P(rows), P())
    out_specs = (P(None, None, rows), P())
    return jax.shard_map(
        functools.partial(shards, plan),
        mesh=parted,
        in_specs=in_specs,
        out_specs=out_specs,
        check_vma=False,
    )
```

```python
import functools
import math

import jax
import jax.numpy as jnp
import numpy as np
from jax import lax
from jax.experimental import pallas as pl
from jax.experimental.pallas import tpu as pltpu
from jax.sharding import Mesh
from jax.sharding import PartitionSpec as P

NFFT = 256
HALF = NFFT // 2
NBLK = 63
NB = 64
NF = 64
NM = 8
ITERS = 12
EPS = 1e-06
LEAST_LEFT = 1e-03
LANES = 128
PITCH = 2 * NB + 1
MIB = 1024 * 1024
TRANSFORM_MIB, SOLVE_MIB, MODES_MIB = 28, 8, 8


def dft_table():
    time_steps = np.arange(NFFT, dtype=np.int32)
    freq_bins = np.arange(1, NF + 1, dtype=np.int32)
    wrapped = freq_bins[:, None] * time_steps[None, :] % NFFT
    angles = np.float32(2.0 * math.pi / NFFT) * wrapped.astype(np.float32)
    taper = np.float32(0.5) - np.float32(0.5) * np.cos(
        np.float32(2.0 * math.pi / NFFT) * time_steps.astype(np.float32)
    )
    taper = taper / np.sqrt(np.sum(taper * taper))
    stacked = np.concatenate([np.cos(angles), -np.sin(angles)]) * taper[None, :]
    return jnp.asarray(stacked, dtype=jnp.float32).astype(jnp.bfloat16)


class Plan:
    def __init__(self, grp, row):
        self.grp, self.deep = grp, row // 2
        self.split_grp = NF % (grp * row) == 0
        self.chips = self.deep * (grp if self.split_grp else 1)
        self.chip_axes = ("grp", "z") if self.split_grp else ("z",)
        self.per = NF // (2 * self.chips)
        self.near = self.deep if self.split_grp else 1

    def chip(self):
        z = lax.axis_index("z")
        return lax.axis_index("grp") * self.deep + z if self.split_grp else z

    def first_freq(self):
        return (self.chip() * 2 + lax.axis_index("core")) * self.per

    def half(self, other_core):
        core = lax.axis_index("core") ^ int(other_core)
        return [
            (chip, (2 * chip + core) * self.per + j)
            for chip in range(self.chips)
            for j in range(self.per)
        ]


def lane_index(shape):
    return lax.broadcasted_iota(jnp.int32, shape, 1)


def row_index_of(shape):
    return lax.broadcasted_iota(jnp.int32, shape, 0)


def pack(top, low):
    row = row_index_of((NB, LANES))
    lane = lane_index((NB, LANES))
    left = lane < NB
    upper = row < (lane & (NB - 1))
    parts = jnp.where(left, jnp.where(upper, -low, top), jnp.where(upper, top, low))
    first, second = parts[: NB // 2], parts[NB // 2 :]
    left_half = left[: NB // 2]
    other = pltpu.roll(jnp.where(left_half, second, first), NB, 1)
    return jnp.where(left_half, first, second) + other


def pack_some(plan, other_core, offsets, coef_ref, out_ref):
    core = lax.axis_index("core") ^ int(other_core)
    for n, offset in enumerate(offsets):
        first = (2 * (plan.chip() ^ offset) + core) * plan.per
        for j in range(plan.per):
            coefs = coef_ref[first + j]
            whole = lax.dot_general(
                coefs, coefs, (((1,), (1,)), ((), ())), preferred_element_type=jnp.float32
            )
            out_ref[n * plan.per + j] = pack(whole[:NB], whole[NB:])


def transform_kernel(plan, table_ref, weight_ref, field_ref, snap_ref, coef_ref, send_ref, flip):
    step = pl.program_id(0)
    tile = snap_ref.shape[1]
    pieces = tile // LANES
    table = table_ref[...]
    root = jnp.sqrt(weight_ref[...])
    probe_row = (root * field_ref[...]).astype(jnp.bfloat16).astype(jnp.float32)
    here = pl.ds(pl.multiple_of(step * tile, tile), tile)

    def one_block(b, carry):
        rows = snap_ref[pl.ds(pl.multiple_of(b * HALF, HALF), NFFT), :]
        out = jnp.dot(table, rows, preferred_element_type=jnp.float32) * root
        for part in range(2):
            for piece in range(pieces):
                flip[piece, pl.ds(part * NB + b, NF, stride=PITCH), :] = out[
                    part * NF : (part + 1) * NF, piece * LANES : (piece + 1) * LANES
                ]
        return carry

    lax.fori_loop(0, NBLK, one_block, 0, unroll=NBLK)
    for piece in range(pieces):
        probe = probe_row[:, piece * LANES : (piece + 1) * LANES]
        flip[piece, pl.ds(NB - 1, NF, stride=PITCH), :] = jnp.broadcast_to(probe, (NF, LANES))
        flip[piece, pl.ds(2 * NB - 1, NF, stride=PITCH), :] = jnp.zeros((NF, LANES), jnp.float32)

    def one_freq(f, carry):
        wide = jnp.concatenate(
            [flip[piece, pl.ds(f * PITCH, 2 * NB), :] for piece in range(pieces)], axis=1
        )
        coefs = wide.astype(jnp.bfloat16)
        coef_ref[f, :, here] = coefs
        return carry

    lax.fori_loop(0, NF, one_freq, 0, unroll=NF)

    @pl.when(step == pl.num_programs(0) - 1)
    def _():
        pack_some(plan, True, range(plan.chips), coef_ref, send_ref)


def transform(plan, snapshots, weights, reference_field):
    rows_here = snapshots.shape[1]
    tile = min(256, rows_here)
    small = [
        pltpu.with_memory_space_constraint(x, pltpu.HBM)
        for x in (dft_table(), weights[None], reference_field[None])
    ]
    return pl.pallas_call(
        functools.partial(transform_kernel, plan),
        grid=(rows_here // tile,),
        in_specs=[
            pl.BlockSpec((2 * NF, NFFT), lambda i: (0, 0)),
            pl.BlockSpec((1, tile), lambda i: (0, i)),
            pl.BlockSpec((1, tile), lambda i: (0, i)),
            pl.BlockSpec((snapshots.shape[0], tile), lambda i: (0, i)),
        ],
        out_specs=[pl.BlockSpec(memory_space=pltpu.VMEM)] * 2,
        out_shape=[
            jax.ShapeDtypeStruct((NF, 2 * NB, rows_here), jnp.bfloat16),
            packed_shape(plan, plan.chips),
        ],
        scratch_shapes=[
            pltpu.VMEM((tile // LANES, NF * PITCH, LANES), jnp.float32),
        ],
        compiler_params=pltpu.CompilerParams(vmem_limit_bytes=TRANSFORM_MIB * MIB),
        name="transform",
    )(*small, snapshots)


def packed_shape(plan, chips):
    return jax.ShapeDtypeStruct((chips * plan.per, NB // 2, LANES), jnp.float32)


def grams(plan, coeffs, other_core, offsets, name):
    _, rows, columns = coeffs.shape
    freqs = plan.per * len(offsets)
    return pl.pallas_call(
        functools.partial(pack_some, plan, other_core, offsets),
        in_specs=[pl.BlockSpec(memory_space=pltpu.VMEM)],
        out_specs=pl.BlockSpec(memory_space=pltpu.VMEM),
        out_shape=packed_shape(plan, len(offsets)),
        cost_estimate=pl.CostEstimate(
            flops=2 * freqs * rows * rows * columns,
            bytes_accessed=2 * freqs * rows * columns,
            transcendentals=0,
        ),
        compiler_params=pltpu.CompilerParams(vmem_limit_bytes=SOLVE_MIB * MIB),
        name=name,
    )(coeffs)


def start_kernel(plan, basis_ref, out_ref):
    lane = lane_index((NM, LANES))
    lane_in = lane_index((NM, basis_ref.shape[3]))
    for j in range(plan.per):
        chosen = lane_in == plan.first_freq() + j
        rows = jnp.zeros((NM, LANES), jnp.float32)
        for part in range(2):
            for b in range(NBLK):
                value = jnp.sum(jnp.where(chosen, basis_ref[part, b], 0.0), axis=1, keepdims=True)
                rows = jnp.where(lane == part * NB + b, value, rows)
        out_ref[j] = rows


def start_rows(plan, start_basis):
    return pl.pallas_call(
        functools.partial(start_kernel, plan),
        in_specs=[pl.BlockSpec(memory_space=pltpu.VMEM)],
        out_specs=pl.BlockSpec(memory_space=pltpu.VMEM),
        out_shape=jax.ShapeDtypeStruct((plan.per, NM, LANES), jnp.float32),
        compiler_params=pltpu.CompilerParams(vmem_limit_bytes=SOLVE_MIB * MIB),
        name="start_rows",
    )(jnp.transpose(start_basis, (1, 2, 3, 0)))


def split_three(x):
    high = x.astype(jnp.bfloat16)
    rest = x - high.astype(jnp.float32)
    middle = rest.astype(jnp.bfloat16)
    low = (rest - middle.astype(jnp.float32)).astype(jnp.bfloat16)
    return high, middle, low


def turn(y):
    swapped = pltpu.roll(y, NB, 1)
    return jnp.where(lane_index(y.shape) < NB, -swapped, swapped)


def lane_sum(x):
    return jnp.broadcast_to(jnp.sum(x, axis=1, keepdims=True), x.shape)


def spread(x, j):
    return jnp.broadcast_to(x[j : j + 1], x.shape)


def orthonormalize_checked(y, turned):
    row = row_index_of(y.shape)
    v = jnp.zeros_like(y)
    for j in range(NM):
        pivot, pivot_turned = spread(y, j), spread(turned, j)
        size = lane_sum(pivot * pivot) + EPS
        v = jnp.where(row == j, pivot * lax.rsqrt(size), v)
        if j < NM - 1:
            inverse = 1.0 / size
            a = jnp.where(row > j, lane_sum(pivot * y) * inverse, 0.0)
            c = jnp.where(row > j, lane_sum(pivot_turned * y) * inverse, 0.0)
            y, turned = (
                y - (a * pivot + c * pivot_turned),
                turned - (a * pivot_turned - c * pivot),
            )
    return v


def orthonormalize_quick(y, turned, worst):
    row = row_index_of(y.shape)
    real = [lane_sum(spread(y, j) * y) for j in range(NM)]
    imag = [lane_sum(spread(turned, j) * y) for j in range(NM - 1)]
    whole = [spread(real[j], j) + EPS for j in range(NM)]
    v = jnp.zeros_like(y)
    for j in range(NM):
        pivot, pivot_turned = spread(y, j), spread(turned, j)
        size = jnp.maximum(spread(real[j], j), 0.0) + EPS
        worst = jnp.minimum(worst, size / whole[j])
        v = jnp.where(row == j, pivot * lax.rsqrt(size), v)
        if j < NM - 1:
            inverse = 1.0 / size
            scale = (size + EPS) * inverse * inverse
            scaled_real, scaled_imag = real[j] * scale, imag[j] * scale
            for l in range(j + 1, NM):
                other_real, other_imag = spread(real[j], l), spread(imag[j], l)
                real[l] = real[l] - (scaled_real * other_real + scaled_imag * other_imag)
                if l < NM - 1:
                    imag[l] = imag[l] - (scaled_imag * other_real - scaled_real * other_imag)
            a = jnp.where(row > j, real[j] * inverse, 0.0)
            c = jnp.where(row > j, imag[j] * inverse, 0.0)
            y, turned = (
                y - (a * pivot + c * pivot_turned),
                turned - (a * pivot_turned - c * pivot),
            )
    return v, worst


def solve_kernel(plan, total_rows, packed_ref, start_ref, out_ref, basis_ref):
    lane = lane_index((NB, LANES))
    row = row_index_of((NB, LANES))
    col = lane & (NB - 1)
    left = lane < NB
    inside = (row < NBLK) & (col < NBLK)
    lane8 = lane_index((NM, LANES))

    systems, probes = [], []
    for i in range(plan.per):
        folded = packed_ref[i]
        turned = pltpu.roll(folded, NB, 1)
        wide = jnp.concatenate([folded, turned], axis=0)
        twice = jnp.where(left, wide, pltpu.roll(wide, NB, 1))
        flipped = jnp.transpose(jnp.concatenate([twice, twice], axis=0))[:NB]
        real = jnp.where(inside, jnp.where(row >= col, twice, flipped), 0.0) / total_rows
        imag = jnp.where(row < col, twice, jnp.where(row > col, -flipped, 0.0))
        imag = jnp.where(inside, imag, 0.0) / total_rows
        straight = jnp.concatenate(
            [jnp.where(left, real, -imag), jnp.where(left, imag, real)], axis=0
        )
        sides = []
        for system in (straight, turn(straight)):
            high, middle, low = split_three(system)
            sides.append(
                jnp.concatenate(
                    [
                        jnp.concatenate([high, low], axis=1),
                        jnp.concatenate([middle, jnp.zeros_like(low)], axis=1),
                    ],
                    axis=0,
                )
            )
        systems.append(jnp.concatenate(sides, axis=1))
        along = twice[NB - 1 :]
        across = flipped[NB - 1 :]
        left1 = lane_index((1, LANES)) < NB
        probes.append((jnp.where(left1, along, across), jnp.where(left1, -across, along)))

    def image_of(i, v):
        high, middle, low = split_three(v)
        zeros = jnp.zeros_like(high)
        parts = jnp.concatenate(
            [
                jnp.concatenate([high, high], axis=1),
                jnp.concatenate([middle, middle], axis=1),
                jnp.concatenate([low, zeros], axis=1),
                jnp.concatenate([zeros, zeros], axis=1),
            ],
            axis=0,
        )
        out = jnp.dot(parts, systems[i], preferred_element_type=jnp.float32)

        def total(out):
            small = out[:NM, LANES:] + out[2 * NM : 3 * NM, :LANES]
            return out[:NM, :LANES] + (out[NM : 2 * NM, :LANES] + small)

        return total(out[:, : 2 * LANES]), total(out[:, 2 * LANES :])

    start = tuple(start_ref[i] for i in range(plan.per))

    def quick_sweep(index, carry):
        current, worst = carry
        images = [image_of(i, v) for i, v in enumerate(current)]
        done = []
        for y, turned in images:
            v, worst = orthonormalize_quick(y, turned, worst)
            done.append(v)
        return tuple(done), worst

    def checked_sweep(index, current):
        images = [image_of(i, v) for i, v in enumerate(current)]
        return tuple(orthonormalize_checked(y, turned) for y, turned in images)

    basis, worst = lax.fori_loop(
        0, ITERS, quick_sweep, (start, jnp.ones((NM, LANES), jnp.float32))
    )
    for i, v in enumerate(basis):
        basis_ref[i] = v

    @pl.when(jnp.logical_not(jnp.min(worst) >= LEAST_LEFT))
    def _():
        for i, v in enumerate(lax.fori_loop(0, ITERS, checked_sweep, start)):
            basis_ref[i] = v

    extras = jnp.zeros((NM, LANES), jnp.float32)
    scale = 1.0 / math.sqrt(total_rows)
    for i in range(plan.per):
        v = basis_ref[i]
        energy = lane_sum(v * image_of(i, v)[0])
        coef = v.astype(jnp.bfloat16).astype(jnp.float32)
        out_ref[i * NM : (i + 1) * NM] = coef
        gain = 1.0 / jnp.sqrt(energy + EPS)
        tilt_real = gain * (lane_sum(coef * probes[i][0]) * scale)
        tilt_imag = gain * (lane_sum(coef * probes[i][1]) * scale)
        size = jnp.sqrt(jnp.maximum(tilt_real * tilt_real + tilt_imag * tilt_imag, 0.25))
        extras = jnp.where(lane8 == 3 * i, gain * tilt_real / size, extras)
        extras = jnp.where(lane8 == 3 * i + 1, -gain * tilt_imag / size, extras)
        extras = jnp.where(lane8 == 3 * i + 2, energy, extras)
    out_ref[plan.per * NM :] = extras


def solve(plan, total_rows, packed, start):
    return pl.pallas_call(
        functools.partial(solve_kernel, plan, total_rows),
        in_specs=[pl.BlockSpec(memory_space=pltpu.VMEM)] * 2,
        out_specs=pl.BlockSpec(memory_space=pltpu.VMEM),
        out_shape=jax.ShapeDtypeStruct(((plan.per + 1) * NM, LANES), jnp.float32),
        scratch_shapes=[pltpu.VMEM((plan.per, NM, LANES), jnp.float32)],
        compiler_params=pltpu.CompilerParams(vmem_limit_bytes=SOLVE_MIB * MIB),
        name="solve",
    )(packed, start)


def modes_kernel(plan, other_core, coef_ref, pay_ref, weight_ref, *refs):
    out_hbm, energy_ref, out, sems = refs[-4:]
    inverse_root = 1.0 / jnp.sqrt(weight_ref[...])
    lane8 = lane_index((NM, LANES))
    left = lane8 < NB
    energies = jnp.zeros((NM, LANES), jnp.float32)
    copies = []
    for n, (chip, f) in enumerate(plan.half(other_core)):
        j = n % plan.per
        c = pay_ref[chip, j * NM : (j + 1) * NM]
        extras = pay_ref[chip, plan.per * NM :]
        factor_real = extras[:, 3 * j : 3 * j + 1]
        factor_imag = extras[:, 3 * j + 1 : 3 * j + 2]
        matrix = jnp.concatenate([jnp.where(left, c, -c), pltpu.roll(c, NB, 1)], axis=0)
        projected = jnp.dot(
            matrix.astype(jnp.bfloat16), coef_ref[f], preferred_element_type=jnp.float32
        )
        real = projected[:NM]
        imag = projected[NM:]
        out[n, :NM, :] = (real * factor_real - imag * factor_imag) * inverse_root
        out[n, NM:, :] = (real * factor_imag + imag * factor_real) * inverse_root
        energies = jnp.where(lane8 == f, extras[:, 3 * j + 2 : 3 * j + 3], energies)
        if j == plan.per - 1:
            copy = pltpu.make_async_copy(
                out.at[pl.ds(n - j, plan.per)],
                out_hbm.at[pl.ds(f - j, plan.per)],
                sems.at[len(copies)],
            )
            copy.start()
            copies.append(copy)
    energies = energies[:, :NF]
    energy_ref[...] = energies + refs[1][...] if other_core else energies
    for copy in copies:
        copy.wait()


def modes(plan, coeffs, payload, weights, earlier=()):
    rows_here = coeffs.shape[2]
    whole = jax.ShapeDtypeStruct((NF, 2 * NM, rows_here), jnp.float32)
    places = [pltpu.HBM, pltpu.VMEM]
    return pl.pallas_call(
        functools.partial(modes_kernel, plan, bool(earlier)),
        in_specs=[pl.BlockSpec(memory_space=pltpu.VMEM)] * 3
        + [pl.BlockSpec(memory_space=place) for place in places[: len(earlier)]],
        out_specs=[pl.BlockSpec(memory_space=place) for place in places],
        out_shape=[whole, jax.ShapeDtypeStruct((NM, NF), jnp.float32)],
        input_output_aliases={3: 0} if earlier else {},
        scratch_shapes=[
            pltpu.VMEM((NF // 2,) + whole.shape[1:], whole.dtype),
            pltpu.SemaphoreType.DMA((plan.chips,)),
        ],
        cost_estimate=pl.CostEstimate(
            flops=2 * NF * NM * 2 * NB * rows_here,
            bytes_accessed=2 * NF * NM * 4 * rows_here,
            transcendentals=0,
        ),
        compiler_params=pltpu.CompilerParams(vmem_limit_bytes=MODES_MIB * MIB),
        name="other_modes" if earlier else "own_modes",
    )(coeffs, payload, weights[None], *earlier)


def swap(x, axis, size, offset):
    return lax.ppermute(x, axis, [(i, i ^ offset) for i in range(size)])


def shards(plan, snapshots, weights, reference_field, start_basis):
    total_rows = snapshots.shape[1] * plan.grp * plan.deep * 2
    coeffs, send = transform(plan, snapshots, weights, reference_field)
    start_basis, send = lax.optimization_barrier((start_basis, send))
    start = start_rows(plan, start_basis)

    arrived = swap(send, "core", 2, 1)
    mine, near = arrived[: plan.near * plan.per], range(plan.near)
    own = grams(plan, coeffs, False, range(plan.near, plan.chips), "own_gram")
    held = own + arrived[plan.near * plan.per :]
    late, held = lax.optimization_barrier((coeffs, held))
    if plan.split_grp:
        held = held.reshape((plan.grp - 1, plan.deep * plan.per) + held.shape[1:])
        arrived = [
            swap(held[d - 1].astype(jnp.bfloat16), "grp", plan.grp, d).astype(jnp.float32)
            for d in range(1, plan.grp)
        ]
    else:
        held = held.reshape((plan.deep - 1, plan.per) + held.shape[1:])
        arrived = [swap(held[d - 1], "z", plan.deep, d) for d in range(1, plan.deep)]
    held = functools.reduce(jnp.add, arrived, grams(plan, late, False, near, "near_gram") + mine)
    if plan.split_grp:
        held = held.reshape((plan.deep, plan.per) + held.shape[1:])
        arrived = [swap(held[d], "z", plan.deep, d) for d in range(1, plan.deep)]
        held = functools.reduce(jnp.add, arrived, held[0])
    else:
        held = lax.psum(held, "grp")

    payload = solve(plan, total_rows, held, start)
    payload = jnp.broadcast_to(payload, (plan.chips,) + payload.shape)
    payload = lax.all_to_all(payload, plan.chip_axes, 0, 0, tiled=True)
    far = swap(payload, "core", 2, 1)
    own = modes(plan, coeffs, payload, weights)
    spod_modes, energies = modes(plan, coeffs, far, weights, own)
    return spod_modes, jnp.transpose(energies)


def solution(mesh):
    plan = Plan(mesh.shape["grp"], mesh.shape["row"])
    parted = Mesh(mesh.devices.reshape(plan.grp, plan.deep, 2), ("grp", "z", "core"))
    rows = ("grp", "z", "core")
    in_specs = (P(None, rows), P(rows), P(rows), P())
    out_specs = (P(None, None, rows), P())
    return jax.shard_map(
        functools.partial(shards, plan),
        mesh=parted,
        in_specs=in_specs,
        out_specs=out_specs,
        check_vma=False,
    )
```

```python
import functools
import math

import jax
import jax.numpy as jnp
import numpy as np
from jax import lax
from jax.experimental import pallas as pl
from jax.experimental.pallas import tpu as pltpu
from jax.sharding import Mesh
from jax.sharding import PartitionSpec as P

NFFT = 256
HALF = NFFT // 2
NBLK = 63
NB = 64
NF = 64
NM = 8
ITERS = 12
EPS = 1e-06
LEAST_LEFT = 1e-03
LANES = 128
PITCH = 2 * NB + 1
MIB = 1024 * 1024
TRANSFORM_MIB, SOLVE_MIB, MODES_MIB = 28, 8, 8


def dft_table():
    time_steps = np.arange(NFFT, dtype=np.int32)
    freq_bins = np.arange(1, NF + 1, dtype=np.int32)
    wrapped = freq_bins[:, None] * time_steps[None, :] % NFFT
    angles = np.float32(2.0 * math.pi / NFFT) * wrapped.astype(np.float32)
    taper = np.float32(0.5) - np.float32(0.5) * np.cos(
        np.float32(2.0 * math.pi / NFFT) * time_steps.astype(np.float32)
    )
    taper = taper / np.sqrt(np.sum(taper * taper))
    stacked = np.concatenate([np.cos(angles), -np.sin(angles)]) * taper[None, :]
    return jnp.asarray(stacked, dtype=jnp.float32).astype(jnp.bfloat16)


class Plan:
    def __init__(self, grp, row):
        self.grp, self.deep = grp, row // 2
        self.split_grp = NF % (grp * row) == 0
        self.chips = self.deep * (grp if self.split_grp else 1)
        self.chip_axes = ("grp", "z") if self.split_grp else ("z",)
        self.per = NF // (2 * self.chips)
        self.near = self.deep if self.split_grp else 1

    def chip(self):
        z = lax.axis_index("z")
        return lax.axis_index("grp") * self.deep + z if self.split_grp else z

    def first_freq(self):
        return (self.chip() * 2 + lax.axis_index("core")) * self.per

    def half(self, other_core):
        core = lax.axis_index("core") ^ int(other_core)
        return [
            (chip, (2 * chip + core) * self.per + j)
            for chip in range(self.chips)
            for j in range(self.per)
        ]


def lane_index(shape):
    return lax.broadcasted_iota(jnp.int32, shape, 1)


def row_index_of(shape):
    return lax.broadcasted_iota(jnp.int32, shape, 0)


def pack(top, low):
    row = row_index_of((NB, LANES))
    lane = lane_index((NB, LANES))
    left = lane < NB
    upper = row < (lane & (NB - 1))
    parts = jnp.where(left, jnp.where(upper, -low, top), jnp.where(upper, top, low))
    first, second = parts[: NB // 2], parts[NB // 2 :]
    left_half = left[: NB // 2]
    other = pltpu.roll(jnp.where(left_half, second, first), NB, 1)
    return jnp.where(left_half, first, second) + other


def pack_some(plan, other_core, offsets, coef_ref, out_ref):
    core = lax.axis_index("core") ^ int(other_core)
    for n, offset in enumerate(offsets):
        first = (2 * (plan.chip() ^ offset) + core) * plan.per
        for j in range(plan.per):
            coefs = coef_ref[first + j]
            whole = lax.dot_general(
                coefs, coefs, (((1,), (1,)), ((), ())), preferred_element_type=jnp.float32
            )
            out_ref[n * plan.per + j] = pack(whole[:NB], whole[NB:])


def transform_kernel(plan, table_ref, weight_ref, field_ref, snap_ref, coef_ref, send_ref, flip):
    step = pl.program_id(0)
    tile = snap_ref.shape[1]
    pieces = tile // LANES
    table = table_ref[...]
    root = jnp.sqrt(weight_ref[...])
    probe_row = (root * field_ref[...]).astype(jnp.bfloat16).astype(jnp.float32)
    here = pl.ds(pl.multiple_of(step * tile, tile), tile)

    def one_block(b, carry):
        rows = snap_ref[pl.ds(pl.multiple_of(b * HALF, HALF), NFFT), :]
        out = jnp.dot(table, rows, preferred_element_type=jnp.float32) * root
        for part in range(2):
            for piece in range(pieces):
                flip[piece, pl.ds(part * NB + b, NF, stride=PITCH), :] = out[
                    part * NF : (part + 1) * NF, piece * LANES : (piece + 1) * LANES
                ]
        return carry

    lax.fori_loop(0, NBLK, one_block, 0, unroll=NBLK)
    for piece in range(pieces):
        probe = probe_row[:, piece * LANES : (piece + 1) * LANES]
        flip[piece, pl.ds(NB - 1, NF, stride=PITCH), :] = jnp.broadcast_to(probe, (NF, LANES))
        flip[piece, pl.ds(2 * NB - 1, NF, stride=PITCH), :] = jnp.zeros((NF, LANES), jnp.float32)

    def one_freq(f, carry):
        wide = jnp.concatenate(
            [flip[piece, pl.ds(f * PITCH, 2 * NB), :] for piece in range(pieces)], axis=1
        )
        coefs = wide.astype(jnp.bfloat16)
        coef_ref[f, :, here] = coefs
        return carry

    lax.fori_loop(0, NF, one_freq, 0, unroll=NF)

    @pl.when(step == pl.num_programs(0) - 1)
    def _():
        pack_some(plan, True, range(plan.chips), coef_ref, send_ref)


def transform(plan, snapshots, weights, reference_field):
    rows_here = snapshots.shape[1]
    tile = min(256, rows_here)
    small = [
        pltpu.with_memory_space_constraint(x, pltpu.HBM)
        for x in (dft_table(), weights[None], reference_field[None])
    ]
    return pl.pallas_call(
        functools.partial(transform_kernel, plan),
        grid=(rows_here // tile,),
        in_specs=[
            pl.BlockSpec((2 * NF, NFFT), lambda i: (0, 0)),
            pl.BlockSpec((1, tile), lambda i: (0, i)),
            pl.BlockSpec((1, tile), lambda i: (0, i)),
            pl.BlockSpec((snapshots.shape[0], tile), lambda i: (0, i)),
        ],
        out_specs=[pl.BlockSpec(memory_space=pltpu.VMEM)] * 2,
        out_shape=[
            jax.ShapeDtypeStruct((NF, 2 * NB, rows_here), jnp.bfloat16),
            packed_shape(plan, plan.chips),
        ],
        scratch_shapes=[
            pltpu.VMEM((tile // LANES, NF * PITCH, LANES), jnp.float32),
        ],
        compiler_params=pltpu.CompilerParams(vmem_limit_bytes=TRANSFORM_MIB * MIB),
        name="transform",
    )(*small, snapshots)


def packed_shape(plan, chips):
    return jax.ShapeDtypeStruct((chips * plan.per, NB // 2, LANES), jnp.float32)


def grams(plan, coeffs, other_core, offsets, name):
    _, rows, columns = coeffs.shape
    freqs = plan.per * len(offsets)
    return pl.pallas_call(
        functools.partial(pack_some, plan, other_core, offsets),
        in_specs=[pl.BlockSpec(memory_space=pltpu.VMEM)],
        out_specs=pl.BlockSpec(memory_space=pltpu.VMEM),
        out_shape=packed_shape(plan, len(offsets)),
        cost_estimate=pl.CostEstimate(
            flops=2 * freqs * rows * rows * columns,
            bytes_accessed=2 * freqs * rows * columns,
            transcendentals=0,
        ),
        compiler_params=pltpu.CompilerParams(vmem_limit_bytes=SOLVE_MIB * MIB),
        name=name,
    )(coeffs)


def start_kernel(plan, basis_ref, out_ref):
    lane = lane_index((NM, LANES))
    lane_in = lane_index((NM, basis_ref.shape[3]))
    for j in range(plan.per):
        chosen = lane_in == plan.first_freq() + j
        rows = jnp.zeros((NM, LANES), jnp.float32)
        for part in range(2):
            for b in range(NBLK):
                value = jnp.sum(jnp.where(chosen, basis_ref[part, b], 0.0), axis=1, keepdims=True)
                rows = jnp.where(lane == part * NB + b, value, rows)
        out_ref[j] = rows


def start_rows(plan, start_basis):
    return pl.pallas_call(
        functools.partial(start_kernel, plan),
        in_specs=[pl.BlockSpec(memory_space=pltpu.VMEM)],
        out_specs=pl.BlockSpec(memory_space=pltpu.VMEM),
        out_shape=jax.ShapeDtypeStruct((plan.per, NM, LANES), jnp.float32),
        compiler_params=pltpu.CompilerParams(vmem_limit_bytes=SOLVE_MIB * MIB),
        name="start_rows",
    )(jnp.transpose(start_basis, (1, 2, 3, 0)))


def split_three(x):
    high = x.astype(jnp.bfloat16)
    rest = x - high.astype(jnp.float32)
    middle = rest.astype(jnp.bfloat16)
    low = (rest - middle.astype(jnp.float32)).astype(jnp.bfloat16)
    return high, middle, low


def turn(y):
    swapped = pltpu.roll(y, NB, 1)
    return jnp.where(lane_index(y.shape) < NB, -swapped, swapped)


def lane_sum(x):
    return jnp.broadcast_to(jnp.sum(x, axis=1, keepdims=True), x.shape)


def spread(x, j):
    return jnp.broadcast_to(x[j : j + 1], x.shape)


def orthonormalize_checked(y, turned):
    row = row_index_of(y.shape)
    v = jnp.zeros_like(y)
    for j in range(NM):
        pivot, pivot_turned = spread(y, j), spread(turned, j)
        size = lane_sum(pivot * pivot) + EPS
        v = jnp.where(row == j, pivot * lax.rsqrt(size), v)
        if j < NM - 1:
            inverse = 1.0 / size
            a = jnp.where(row > j, lane_sum(pivot * y) * inverse, 0.0)
            c = jnp.where(row > j, lane_sum(pivot_turned * y) * inverse, 0.0)
            y, turned = (
                y - (a * pivot + c * pivot_turned),
                turned - (a * pivot_turned - c * pivot),
            )
    return v


def orthonormalize_quick(y, turned, worst):
    row = row_index_of(y.shape)
    real = [lane_sum(spread(y, j) * y) for j in range(NM)]
    imag = [lane_sum(spread(turned, j) * y) for j in range(NM - 1)]
    whole = [spread(real[j], j) + EPS for j in range(NM)]
    v = jnp.zeros_like(y)
    for j in range(NM):
        pivot, pivot_turned = spread(y, j), spread(turned, j)
        size = jnp.maximum(spread(real[j], j), 0.0) + EPS
        worst = jnp.minimum(worst, size / whole[j])
        v = jnp.where(row == j, pivot * lax.rsqrt(size), v)
        if j < NM - 1:
            inverse = 1.0 / size
            scale = (1.0 + EPS * inverse) * inverse
            for l in range(j + 1, NM):
                other_real, other_imag = spread(real[j], l), spread(imag[j], l)
                both = real[j] * other_real + imag[j] * other_imag
                real[l] = real[l] - scale * both
                if l < NM - 1:
                    cross = imag[j] * other_real - real[j] * other_imag
                    imag[l] = imag[l] - scale * cross
            a = jnp.where(row > j, real[j] * inverse, 0.0)
            c = jnp.where(row > j, imag[j] * inverse, 0.0)
            y, turned = (
                y - (a * pivot + c * pivot_turned),
                turned - (a * pivot_turned - c * pivot),
            )
    return v, worst


def solve_kernel(plan, total_rows, packed_ref, start_ref, out_ref, basis_ref):
    lane = lane_index((NB, LANES))
    row = row_index_of((NB, LANES))
    col = lane & (NB - 1)
    left = lane < NB
    inside = (row < NBLK) & (col < NBLK)
    lane8 = lane_index((NM, LANES))

    systems, probes = [], []
    for i in range(plan.per):
        folded = packed_ref[i]
        turned = pltpu.roll(folded, NB, 1)
        wide = jnp.concatenate([folded, turned], axis=0)
        twice = jnp.where(left, wide, pltpu.roll(wide, NB, 1))
        flipped = jnp.transpose(jnp.concatenate([twice, twice], axis=0))[:NB]
        real = jnp.where(inside, jnp.where(row >= col, twice, flipped), 0.0) / total_rows
        imag = jnp.where(row < col, twice, jnp.where(row > col, -flipped, 0.0))
        imag = jnp.where(inside, imag, 0.0) / total_rows
        straight = jnp.concatenate(
            [jnp.where(left, real, -imag), jnp.where(left, imag, real)], axis=0
        )
        sides = []
        for system in (straight, turn(straight)):
            high, middle, low = split_three(system)
            sides.append(
                jnp.concatenate(
                    [
                        jnp.concatenate([high, low], axis=1),
                        jnp.concatenate([middle, jnp.zeros_like(low)], axis=1),
                    ],
                    axis=0,
                )
            )
        systems.append(jnp.concatenate(sides, axis=1))
        along = twice[NB - 1 :]
        across = flipped[NB - 1 :]
        left1 = lane_index((1, LANES)) < NB
        probes.append((jnp.where(left1, along, across), jnp.where(left1, -across, along)))

    def image_of(i, v):
        high, middle, low = split_three(v)
        zeros = jnp.zeros_like(high)
        parts = jnp.concatenate(
            [
                jnp.concatenate([high, high], axis=1),
                jnp.concatenate([middle, middle], axis=1),
                jnp.concatenate([low, zeros], axis=1),
                jnp.concatenate([zeros, zeros], axis=1),
            ],
            axis=0,
        )
        out = jnp.dot(parts, systems[i], preferred_element_type=jnp.float32)

        def total(out):
            small = out[:NM, LANES:] + out[2 * NM : 3 * NM, :LANES]
            return out[:NM, :LANES] + (out[NM : 2 * NM, :LANES] + small)

        return total(out[:, : 2 * LANES]), total(out[:, 2 * LANES :])

    start = tuple(start_ref[i] for i in range(plan.per))

    def quick_sweep(index, carry):
        current, worst = carry
        images = [image_of(i, v) for i, v in enumerate(current)]
        done = []
        for y, turned in images:
            v, worst = orthonormalize_quick(y, turned, worst)
            done.append(v)
        return tuple(done), worst

    def checked_sweep(index, current):
        images = [image_of(i, v) for i, v in enumerate(current)]
        return tuple(orthonormalize_checked(y, turned) for y, turned in images)

    basis, worst = lax.fori_loop(
        0, ITERS, quick_sweep, (start, jnp.ones((NM, LANES), jnp.float32)), unroll=4
    )
    for i, v in enumerate(basis):
        basis_ref[i] = v

    @pl.when(jnp.logical_not(jnp.min(worst) >= LEAST_LEFT))
    def _():
        for i, v in enumerate(lax.fori_loop(0, ITERS, checked_sweep, start)):
            basis_ref[i] = v

    extras = jnp.zeros((NM, LANES), jnp.float32)
    scale = 1.0 / math.sqrt(total_rows)
    for i in range(plan.per):
        v = basis_ref[i]
        energy = lane_sum(v * image_of(i, v)[0])
        coef = v.astype(jnp.bfloat16).astype(jnp.float32)
        out_ref[i * NM : (i + 1) * NM] = coef
        gain = 1.0 / jnp.sqrt(energy + EPS)
        tilt_real = gain * (lane_sum(coef * probes[i][0]) * scale)
        tilt_imag = gain * (lane_sum(coef * probes[i][1]) * scale)
        size = jnp.sqrt(jnp.maximum(tilt_real * tilt_real + tilt_imag * tilt_imag, 0.25))
        extras = jnp.where(lane8 == 3 * i, gain * tilt_real / size, extras)
        extras = jnp.where(lane8 == 3 * i + 1, -gain * tilt_imag / size, extras)
        extras = jnp.where(lane8 == 3 * i + 2, energy, extras)
    out_ref[plan.per * NM :] = extras


def solve(plan, total_rows, packed, start):
    return pl.pallas_call(
        functools.partial(solve_kernel, plan, total_rows),
        in_specs=[pl.BlockSpec(memory_space=pltpu.VMEM)] * 2,
        out_specs=pl.BlockSpec(memory_space=pltpu.VMEM),
        out_shape=jax.ShapeDtypeStruct(((plan.per + 1) * NM, LANES), jnp.float32),
        scratch_shapes=[pltpu.VMEM((plan.per, NM, LANES), jnp.float32)],
        compiler_params=pltpu.CompilerParams(vmem_limit_bytes=SOLVE_MIB * MIB),
        name="solve",
    )(packed, start)


def modes_kernel(plan, other_core, coef_ref, pay_ref, weight_ref, *refs):
    out_hbm, energy_ref, out, sems = refs[-4:]
    inverse_root = 1.0 / jnp.sqrt(weight_ref[...])
    lane8 = lane_index((NM, LANES))
    left = lane8 < NB
    energies = jnp.zeros((NM, LANES), jnp.float32)
    copies = []
    for n, (chip, f) in enumerate(plan.half(other_core)):
        j = n % plan.per
        c = pay_ref[chip, j * NM : (j + 1) * NM]
        extras = pay_ref[chip, plan.per * NM :]
        factor_real = extras[:, 3 * j : 3 * j + 1]
        factor_imag = extras[:, 3 * j + 1 : 3 * j + 2]
        matrix = jnp.concatenate([jnp.where(left, c, -c), pltpu.roll(c, NB, 1)], axis=0)
        projected = jnp.dot(
            matrix.astype(jnp.bfloat16), coef_ref[f], preferred_element_type=jnp.float32
        )
        real = projected[:NM]
        imag = projected[NM:]
        out[n, :NM, :] = (real * factor_real - imag * factor_imag) * inverse_root
        out[n, NM:, :] = (real * factor_imag + imag * factor_real) * inverse_root
        energies = jnp.where(lane8 == f, extras[:, 3 * j + 2 : 3 * j + 3], energies)
        if j == plan.per - 1:
            copy = pltpu.make_async_copy(
                out.at[pl.ds(n - j, plan.per)],
                out_hbm.at[pl.ds(f - j, plan.per)],
                sems.at[len(copies)],
            )
            copy.start()
            copies.append(copy)
    energies = energies[:, :NF]
    energy_ref[...] = energies + refs[1][...] if other_core else energies
    for copy in copies:
        copy.wait()


def modes(plan, coeffs, payload, weights, earlier=()):
    rows_here = coeffs.shape[2]
    whole = jax.ShapeDtypeStruct((NF, 2 * NM, rows_here), jnp.float32)
    places = [pltpu.HBM, pltpu.VMEM]
    return pl.pallas_call(
        functools.partial(modes_kernel, plan, bool(earlier)),
        in_specs=[pl.BlockSpec(memory_space=pltpu.VMEM)] * 3
        + [pl.BlockSpec(memory_space=place) for place in places[: len(earlier)]],
        out_specs=[pl.BlockSpec(memory_space=place) for place in places],
        out_shape=[whole, jax.ShapeDtypeStruct((NM, NF), jnp.float32)],
        input_output_aliases={3: 0} if earlier else {},
        scratch_shapes=[
            pltpu.VMEM((NF // 2,) + whole.shape[1:], whole.dtype),
            pltpu.SemaphoreType.DMA((plan.chips,)),
        ],
        cost_estimate=pl.CostEstimate(
            flops=2 * NF * NM * 2 * NB * rows_here,
            bytes_accessed=2 * NF * NM * 4 * rows_here,
            transcendentals=0,
        ),
        compiler_params=pltpu.CompilerParams(vmem_limit_bytes=MODES_MIB * MIB),
        name="other_modes" if earlier else "own_modes",
    )(coeffs, payload, weights[None], *earlier)


def swap(x, axis, size, offset):
    return lax.ppermute(x, axis, [(i, i ^ offset) for i in range(size)])


def shards(plan, snapshots, weights, reference_field, start_basis):
    total_rows = snapshots.shape[1] * plan.grp * plan.deep * 2
    coeffs, send = transform(plan, snapshots, weights, reference_field)
    start_basis, send = lax.optimization_barrier((start_basis, send))
    start = start_rows(plan, start_basis)

    arrived = swap(send, "core", 2, 1)
    mine, near = arrived[: plan.near * plan.per], range(plan.near)
    own = grams(plan, coeffs, False, range(plan.near, plan.chips), "own_gram")
    held = own + arrived[plan.near * plan.per :]
    late, held = lax.optimization_barrier((coeffs, held))
    if plan.split_grp:
        held = held.reshape((plan.grp - 1, plan.deep * plan.per) + held.shape[1:])
        arrived = [
            swap(held[d - 1].astype(jnp.bfloat16), "grp", plan.grp, d).astype(jnp.float32)
            for d in range(1, plan.grp)
        ]
    else:
        held = held.reshape((plan.deep - 1, plan.per) + held.shape[1:])
        arrived = [swap(held[d - 1], "z", plan.deep, d) for d in range(1, plan.deep)]
    held = functools.reduce(jnp.add, arrived, grams(plan, late, False, near, "near_gram") + mine)
    if plan.split_grp:
        held = held.reshape((plan.deep, plan.per) + held.shape[1:])
        arrived = [swap(held[d], "z", plan.deep, d) for d in range(1, plan.deep)]
        held = functools.reduce(jnp.add, arrived, held[0])
    else:
        held = lax.psum(held, "grp")

    payload = solve(plan, total_rows, held, start)
    payload = jnp.broadcast_to(payload, (plan.chips,) + payload.shape)
    payload = lax.all_to_all(payload, plan.chip_axes, 0, 0, tiled=True)
    far = swap(payload, "core", 2, 1)
    own = modes(plan, coeffs, payload, weights)
    spod_modes, energies = modes(plan, coeffs, far, weights, own)
    return spod_modes, jnp.transpose(energies)


def solution(mesh):
    plan = Plan(mesh.shape["grp"], mesh.shape["row"])
    parted = Mesh(mesh.devices.reshape(plan.grp, plan.deep, 2), ("grp", "z", "core"))
    rows = ("grp", "z", "core")
    in_specs = (P(None, rows), P(rows), P(rows), P())
    out_specs = (P(None, None, rows), P())
    return jax.shard_map(
        functools.partial(shards, plan),
        mesh=parted,
        in_specs=in_specs,
        out_specs=out_specs,
        check_vma=False,
    )
```

```python
import functools
import math

import jax
import jax.numpy as jnp
import numpy as np
from jax import lax
from jax.experimental import pallas as pl
from jax.experimental.pallas import tpu as pltpu
from jax.sharding import Mesh
from jax.sharding import PartitionSpec as P

NFFT = 256
HALF = NFFT // 2
NBLK = 63
NB = 64
NF = 64
NM = 8
ITERS = 12
EPS = 1e-06
LEAST_LEFT = 1e-03
LANES = 128
PITCH = 2 * NB + 1
MIB = 1024 * 1024
TRANSFORM_MIB, SOLVE_MIB, MODES_MIB = 28, 8, 8


def dft_table():
    time_steps = np.arange(NFFT, dtype=np.int32)
    freq_bins = np.arange(1, NF + 1, dtype=np.int32)
    wrapped = freq_bins[:, None] * time_steps[None, :] % NFFT
    angles = np.float32(2.0 * math.pi / NFFT) * wrapped.astype(np.float32)
    taper = np.float32(0.5) - np.float32(0.5) * np.cos(
        np.float32(2.0 * math.pi / NFFT) * time_steps.astype(np.float32)
    )
    taper = taper / np.sqrt(np.sum(taper * taper))
    stacked = np.concatenate([np.cos(angles), -np.sin(angles)]) * taper[None, :]
    return jnp.asarray(stacked, dtype=jnp.float32).astype(jnp.bfloat16)


class Plan:
    def __init__(self, grp, row):
        self.grp, self.deep = grp, row // 2
        self.split_grp = NF % (grp * row) == 0
        self.chips = self.deep * (grp if self.split_grp else 1)
        self.chip_axes = ("grp", "z") if self.split_grp else ("z",)
        self.per = NF // (2 * self.chips)
        self.near = self.deep if self.split_grp else 1

    def chip(self):
        z = lax.axis_index("z")
        return lax.axis_index("grp") * self.deep + z if self.split_grp else z

    def first_freq(self):
        return (self.chip() * 2 + lax.axis_index("core")) * self.per

    def half(self, other_core):
        core = lax.axis_index("core") ^ int(other_core)
        return [
            (chip, (2 * chip + core) * self.per + j)
            for chip in range(self.chips)
            for j in range(self.per)
        ]


def lane_index(shape):
    return lax.broadcasted_iota(jnp.int32, shape, 1)


def row_index_of(shape):
    return lax.broadcasted_iota(jnp.int32, shape, 0)


def pack(top, low):
    row = row_index_of((NB, LANES))
    lane = lane_index((NB, LANES))
    left = lane < NB
    upper = row < (lane & (NB - 1))
    parts = jnp.where(left, jnp.where(upper, -low, top), jnp.where(upper, top, low))
    first, second = parts[: NB // 2], parts[NB // 2 :]
    left_half = left[: NB // 2]
    other = pltpu.roll(jnp.where(left_half, second, first), NB, 1)
    return jnp.where(left_half, first, second) + other


def pack_some(plan, other_core, offsets, coef_ref, out_ref):
    core = lax.axis_index("core") ^ int(other_core)
    for n, offset in enumerate(offsets):
        first = (2 * (plan.chip() ^ offset) + core) * plan.per
        for j in range(plan.per):
            coefs = coef_ref[first + j]
            whole = lax.dot_general(
                coefs, coefs, (((1,), (1,)), ((), ())), preferred_element_type=jnp.float32
            )
            out_ref[n * plan.per + j] = pack(whole[:NB], whole[NB:])


def transform_kernel(plan, table_ref, weight_ref, field_ref, snap_ref, coef_ref, send_ref, flip):
    step = pl.program_id(0)
    tile = snap_ref.shape[1]
    pieces = tile // LANES
    table = table_ref[...]
    root = jnp.sqrt(weight_ref[...])
    probe_row = (root * field_ref[...]).astype(jnp.bfloat16).astype(jnp.float32)
    here = pl.ds(pl.multiple_of(step * tile, tile), tile)

    def one_block(b, carry):
        rows = snap_ref[pl.ds(pl.multiple_of(b * HALF, HALF), NFFT), :]
        out = jnp.dot(table, rows, preferred_element_type=jnp.float32) * root
        for part in range(2):
            for piece in range(pieces):
                flip[piece, pl.ds(part * NB + b, NF, stride=PITCH), :] = out[
                    part * NF : (part + 1) * NF, piece * LANES : (piece + 1) * LANES
                ]
        return carry

    lax.fori_loop(0, NBLK, one_block, 0, unroll=NBLK)
    for piece in range(pieces):
        probe = probe_row[:, piece * LANES : (piece + 1) * LANES]
        flip[piece, pl.ds(NB - 1, NF, stride=PITCH), :] = jnp.broadcast_to(probe, (NF, LANES))
        flip[piece, pl.ds(2 * NB - 1, NF, stride=PITCH), :] = jnp.zeros((NF, LANES), jnp.float32)

    def one_freq(f, carry):
        wide = jnp.concatenate(
            [flip[piece, pl.ds(f * PITCH, 2 * NB), :] for piece in range(pieces)], axis=1
        )
        coefs = wide.astype(jnp.bfloat16)
        coef_ref[f, :, here] = coefs
        return carry

    lax.fori_loop(0, NF, one_freq, 0, unroll=NF)

    @pl.when(step == pl.num_programs(0) - 1)
    def _():
        pack_some(plan, True, range(plan.chips), coef_ref, send_ref)


def transform(plan, snapshots, weights, reference_field):
    rows_here = snapshots.shape[1]
    tile = min(256, rows_here)
    small = [
        pltpu.with_memory_space_constraint(x, pltpu.HBM)
        for x in (dft_table(), weights[None], reference_field[None])
    ]
    return pl.pallas_call(
        functools.partial(transform_kernel, plan),
        grid=(rows_here // tile,),
        in_specs=[
            pl.BlockSpec((2 * NF, NFFT), lambda i: (0, 0)),
            pl.BlockSpec((1, tile), lambda i: (0, i)),
            pl.BlockSpec((1, tile), lambda i: (0, i)),
            pl.BlockSpec((snapshots.shape[0], tile), lambda i: (0, i)),
        ],
        out_specs=[pl.BlockSpec(memory_space=pltpu.VMEM)] * 2,
        out_shape=[
            jax.ShapeDtypeStruct((NF, 2 * NB, rows_here), jnp.bfloat16),
            packed_shape(plan, plan.chips),
        ],
        scratch_shapes=[
            pltpu.VMEM((tile // LANES, NF * PITCH, LANES), jnp.float32),
        ],
        compiler_params=pltpu.CompilerParams(vmem_limit_bytes=TRANSFORM_MIB * MIB),
        name="transform",
    )(*small, snapshots)


def packed_shape(plan, chips):
    return jax.ShapeDtypeStruct((chips * plan.per, NB // 2, LANES), jnp.float32)


def grams(plan, coeffs, other_core, offsets, name):
    _, rows, columns = coeffs.shape
    freqs = plan.per * len(offsets)
    return pl.pallas_call(
        functools.partial(pack_some, plan, other_core, offsets),
        in_specs=[pl.BlockSpec(memory_space=pltpu.VMEM)],
        out_specs=pl.BlockSpec(memory_space=pltpu.VMEM),
        out_shape=packed_shape(plan, len(offsets)),
        cost_estimate=pl.CostEstimate(
            flops=2 * freqs * rows * rows * columns,
            bytes_accessed=2 * freqs * rows * columns,
            transcendentals=0,
        ),
        compiler_params=pltpu.CompilerParams(vmem_limit_bytes=SOLVE_MIB * MIB),
        name=name,
    )(coeffs)


def start_kernel(plan, basis_ref, out_ref):
    lane = lane_index((NM, LANES))
    lane_in = lane_index((NM, basis_ref.shape[3]))
    for j in range(plan.per):
        chosen = lane_in == plan.first_freq() + j
        rows = jnp.zeros((NM, LANES), jnp.float32)
        for part in range(2):
            for b in range(NBLK):
                value = jnp.sum(jnp.where(chosen, basis_ref[part, b], 0.0), axis=1, keepdims=True)
                rows = jnp.where(lane == part * NB + b, value, rows)
        out_ref[j] = rows


def start_rows(plan, start_basis):
    return pl.pallas_call(
        functools.partial(start_kernel, plan),
        in_specs=[pl.BlockSpec(memory_space=pltpu.VMEM)],
        out_specs=pl.BlockSpec(memory_space=pltpu.VMEM),
        out_shape=jax.ShapeDtypeStruct((plan.per, NM, LANES), jnp.float32),
        compiler_params=pltpu.CompilerParams(vmem_limit_bytes=SOLVE_MIB * MIB),
        name="start_rows",
    )(jnp.transpose(start_basis, (1, 2, 3, 0)))


def split_three(x):
    high = x.astype(jnp.bfloat16)
    rest = x - high.astype(jnp.float32)
    middle = rest.astype(jnp.bfloat16)
    low = (rest - middle.astype(jnp.float32)).astype(jnp.bfloat16)
    return high, middle, low


def turn(y):
    swapped = pltpu.roll(y, NB, 1)
    return jnp.where(lane_index(y.shape) < NB, -swapped, swapped)


def lane_sum(x):
    return jnp.broadcast_to(jnp.sum(x, axis=1, keepdims=True), x.shape)


def spread(x, j):
    return jnp.broadcast_to(x[j : j + 1], x.shape)


def orthonormalize_checked(y, turned):
    row = row_index_of(y.shape)
    v = jnp.zeros_like(y)
    for j in range(NM):
        pivot, pivot_turned = spread(y, j), spread(turned, j)
        size = lane_sum(pivot * pivot) + EPS
        v = jnp.where(row == j, pivot * lax.rsqrt(size), v)
        if j < NM - 1:
            inverse = 1.0 / size
            a = jnp.where(row > j, lane_sum(pivot * y) * inverse, 0.0)
            c = jnp.where(row > j, lane_sum(pivot_turned * y) * inverse, 0.0)
            y, turned = (
                y - (a * pivot + c * pivot_turned),
                turned - (a * pivot_turned - c * pivot),
            )
    return v


def orthonormalize_quick(y, turned, worst):
    row = row_index_of(y.shape)
    real = [lane_sum(spread(y, j) * y) for j in range(NM)]
    imag = [lane_sum(spread(turned, j) * y) for j in range(NM - 1)]
    whole = [spread(real[j], j) + EPS for j in range(NM)]
    v = jnp.zeros_like(y)
    for j in range(NM):
        pivot, pivot_turned = spread(y, j), spread(turned, j)
        size = jnp.maximum(spread(real[j], j), 0.0) + EPS
        worst = jnp.minimum(worst, size / whole[j])
        v = jnp.where(row == j, pivot * lax.rsqrt(size), v)
        if j < NM - 1:
            inverse = 1.0 / size
            scale = (1.0 + EPS * inverse) * inverse
            for l in range(j + 1, NM):
                other_real, other_imag = spread(real[j], l), spread(imag[j], l)
                both = real[j] * other_real + imag[j] * other_imag
                real[l] = real[l] - scale * both
                if l < NM - 1:
                    cross = imag[j] * other_real - real[j] * other_imag
                    imag[l] = imag[l] - scale * cross
            a = jnp.where(row > j, real[j] * inverse, 0.0)
            c = jnp.where(row > j, imag[j] * inverse, 0.0)
            y, turned = (
                y - (a * pivot + c * pivot_turned),
                turned - (a * pivot_turned - c * pivot),
            )
    return v, worst


def solve_kernel(plan, total_rows, packed_ref, start_ref, out_ref, basis_ref):
    lane = lane_index((NB, LANES))
    row = row_index_of((NB, LANES))
    col = lane & (NB - 1)
    left = lane < NB
    inside = (row < NBLK) & (col < NBLK)
    lane8 = lane_index((NM, LANES))

    systems, probes = [], []
    for i in range(plan.per):
        folded = packed_ref[i]
        turned = pltpu.roll(folded, NB, 1)
        wide = jnp.concatenate([folded, turned], axis=0)
        twice = jnp.where(left, wide, pltpu.roll(wide, NB, 1))
        flipped = jnp.transpose(jnp.concatenate([twice, twice], axis=0))[:NB]
        real = jnp.where(inside, jnp.where(row >= col, twice, flipped), 0.0) / total_rows
        imag = jnp.where(row < col, twice, jnp.where(row > col, -flipped, 0.0))
        imag = jnp.where(inside, imag, 0.0) / total_rows
        straight = jnp.concatenate(
            [jnp.where(left, real, -imag), jnp.where(left, imag, real)], axis=0
        )
        sides = []
        for system in (straight, turn(straight)):
            high, middle, low = split_three(system)
            sides.append(
                jnp.concatenate(
                    [
                        jnp.concatenate([high, low], axis=1),
                        jnp.concatenate([middle, jnp.zeros_like(low)], axis=1),
                    ],
                    axis=0,
                )
            )
        systems.append(jnp.concatenate(sides, axis=1))
        along = twice[NB - 1 :]
        across = flipped[NB - 1 :]
        left1 = lane_index((1, LANES)) < NB
        probes.append((jnp.where(left1, along, across), jnp.where(left1, -across, along)))

    def image_of(i, v):
        high, middle, low = split_three(v)
        zeros = jnp.zeros_like(high)
        parts = jnp.concatenate(
            [
                jnp.concatenate([high, high], axis=1),
                jnp.concatenate([middle, middle], axis=1),
                jnp.concatenate([low, zeros], axis=1),
                jnp.concatenate([zeros, zeros], axis=1),
            ],
            axis=0,
        )
        out = jnp.dot(parts, systems[i], preferred_element_type=jnp.float32)

        def total(out):
            small = out[:NM, LANES:] + out[2 * NM : 3 * NM, :LANES]
            return out[:NM, :LANES] + (out[NM : 2 * NM, :LANES] + small)

        return total(out[:, : 2 * LANES]), total(out[:, 2 * LANES :])

    start = tuple(start_ref[i] for i in range(plan.per))

    def quick_sweep(index, carry):
        current, worst = carry
        images = [image_of(i, v) for i, v in enumerate(current)]
        done = []
        for y, turned in images:
            v, worst = orthonormalize_quick(y, turned, worst)
            done.append(v)
        return tuple(done), worst

    def checked_sweep(index, current):
        images = [image_of(i, v) for i, v in enumerate(current)]
        return tuple(orthonormalize_checked(y, turned) for y, turned in images)

    basis, worst = lax.fori_loop(
        0, ITERS, quick_sweep, (start, jnp.ones((NM, LANES), jnp.float32)), unroll=4
    )
    for i, v in enumerate(basis):
        basis_ref[i] = v

    @pl.when(jnp.logical_not(jnp.min(worst) >= LEAST_LEFT))
    def _():
        for i, v in enumerate(lax.fori_loop(0, ITERS, checked_sweep, start)):
            basis_ref[i] = v

    extras = jnp.zeros((NM, LANES), jnp.float32)
    scale = 1.0 / math.sqrt(total_rows)
    for i in range(plan.per):
        v = basis_ref[i]
        energy = lane_sum(v * image_of(i, v)[0])
        coef = v.astype(jnp.bfloat16).astype(jnp.float32)
        out_ref[i * NM : (i + 1) * NM] = coef
        gain = 1.0 / jnp.sqrt(energy + EPS)
        tilt_real = gain * (lane_sum(coef * probes[i][0]) * scale)
        tilt_imag = gain * (lane_sum(coef * probes[i][1]) * scale)
        size = jnp.sqrt(jnp.maximum(tilt_real * tilt_real + tilt_imag * tilt_imag, 0.25))
        extras = jnp.where(lane8 == 3 * i, gain * tilt_real / size, extras)
        extras = jnp.where(lane8 == 3 * i + 1, -gain * tilt_imag / size, extras)
        extras = jnp.where(lane8 == 3 * i + 2, energy, extras)
    out_ref[plan.per * NM :] = extras


def solve(plan, total_rows, packed, start):
    return pl.pallas_call(
        functools.partial(solve_kernel, plan, total_rows),
        in_specs=[pl.BlockSpec(memory_space=pltpu.VMEM)] * 2,
        out_specs=pl.BlockSpec(memory_space=pltpu.VMEM),
        out_shape=jax.ShapeDtypeStruct(((plan.per + 1) * NM, LANES), jnp.float32),
        scratch_shapes=[pltpu.VMEM((plan.per, NM, LANES), jnp.float32)],
        compiler_params=pltpu.CompilerParams(vmem_limit_bytes=SOLVE_MIB * MIB),
        name="solve",
    )(packed, start)


def modes_kernel(plan, other_core, coef_ref, pay_ref, weight_ref, *refs):
    out_hbm, energy_ref, out, sems = refs[-4:]
    inverse_root = 1.0 / jnp.sqrt(weight_ref[...])
    lane8 = lane_index((NM, LANES))
    left = lane8 < NB
    energies = jnp.zeros((NM, LANES), jnp.float32)
    copies = []
    for n, (chip, f) in enumerate(plan.half(other_core)):
        j = n % plan.per
        c = pay_ref[chip, j * NM : (j + 1) * NM]
        extras = pay_ref[chip, plan.per * NM :]
        factor_real = extras[:, 3 * j : 3 * j + 1]
        factor_imag = extras[:, 3 * j + 1 : 3 * j + 2]
        matrix = jnp.concatenate([jnp.where(left, c, -c), pltpu.roll(c, NB, 1)], axis=0)
        projected = jnp.dot(
            matrix.astype(jnp.bfloat16), coef_ref[f], preferred_element_type=jnp.float32
        )
        real = projected[:NM]
        imag = projected[NM:]
        out[n, :NM, :] = (real * factor_real - imag * factor_imag) * inverse_root
        out[n, NM:, :] = (real * factor_imag + imag * factor_real) * inverse_root
        energies = jnp.where(lane8 == f, extras[:, 3 * j + 2 : 3 * j + 3], energies)
        if j == plan.per - 1:
            copy = pltpu.make_async_copy(
                out.at[pl.ds(n - j, plan.per)],
                out_hbm.at[pl.ds(f - j, plan.per)],
                sems.at[len(copies)],
            )
            copy.start()
            copies.append(copy)
    energies = energies[:, :NF]
    energy_ref[...] = energies + refs[1][...] if other_core else energies
    for copy in copies:
        copy.wait()


def modes(plan, coeffs, payload, weights, earlier=()):
    rows_here = coeffs.shape[2]
    whole = jax.ShapeDtypeStruct((NF, 2 * NM, rows_here), jnp.float32)
    places = [pltpu.HBM, pltpu.VMEM]
    return pl.pallas_call(
        functools.partial(modes_kernel, plan, bool(earlier)),
        in_specs=[pl.BlockSpec(memory_space=pltpu.VMEM)] * 3
        + [pl.BlockSpec(memory_space=place) for place in places[: len(earlier)]],
        out_specs=[pl.BlockSpec(memory_space=place) for place in places],
        out_shape=[whole, jax.ShapeDtypeStruct((NM, NF), jnp.float32)],
        input_output_aliases={3: 0} if earlier else {},
        scratch_shapes=[
            pltpu.VMEM((NF // 2,) + whole.shape[1:], whole.dtype),
            pltpu.SemaphoreType.DMA((plan.chips,)),
        ],
        cost_estimate=pl.CostEstimate(
            flops=2 * NF * NM * 2 * NB * rows_here,
            bytes_accessed=2 * NF * NM * 4 * rows_here,
            transcendentals=0,
        ),
        compiler_params=pltpu.CompilerParams(vmem_limit_bytes=MODES_MIB * MIB),
        name="other_modes" if earlier else "own_modes",
    )(coeffs, payload, weights[None], *earlier)


def swap(x, axis, size, offset):
    return lax.ppermute(x, axis, [(i, i ^ offset) for i in range(size)])


def shards(plan, snapshots, weights, reference_field, start_basis):
    total_rows = snapshots.shape[1] * plan.grp * plan.deep * 2
    coeffs, send = transform(plan, snapshots, weights, reference_field)
    start_basis, send = lax.optimization_barrier((start_basis, send))
    start = start_rows(plan, start_basis)

    arrived = swap(send, "core", 2, 1)
    mine, near = arrived[: plan.near * plan.per], range(plan.near)
    own = grams(plan, coeffs, False, range(plan.near, plan.chips), "own_gram")
    held = own + arrived[plan.near * plan.per :]
    late, held = lax.optimization_barrier((coeffs, held))
    if plan.split_grp:
        held = held.reshape((plan.grp - 1, plan.deep * plan.per) + held.shape[1:])
        arrived = [swap(held[d - 1], "grp", plan.grp, d) for d in range(1, plan.grp)]
    else:
        held = held.reshape((plan.deep - 1, plan.per) + held.shape[1:])
        arrived = [swap(held[d - 1], "z", plan.deep, d) for d in range(1, plan.deep)]
    held = functools.reduce(jnp.add, arrived, grams(plan, late, False, near, "near_gram") + mine)
    if plan.split_grp:
        held = held.reshape((plan.deep, plan.per) + held.shape[1:])
        arrived = [swap(held[d], "z", plan.deep, d) for d in range(1, plan.deep)]
        held = functools.reduce(jnp.add, arrived, held[0])
    else:
        held = lax.psum(held, "grp")

    payload = solve(plan, total_rows, held, start)
    payload = jnp.broadcast_to(payload, (plan.chips,) + payload.shape)
    payload = lax.all_to_all(payload, plan.chip_axes, 0, 0, tiled=True)
    far = swap(payload, "core", 2, 1)
    own = modes(plan, coeffs, payload, weights)
    spod_modes, energies = modes(plan, coeffs, far, weights, own)
    return spod_modes, jnp.transpose(energies)


def solution(mesh):
    plan = Plan(mesh.shape["grp"], mesh.shape["row"])
    parted = Mesh(mesh.devices.reshape(plan.grp, plan.deep, 2), ("grp", "z", "core"))
    rows = ("grp", "z", "core")
    in_specs = (P(None, rows), P(rows), P(rows), P())
    out_specs = (P(None, None, rows), P())
    return jax.shard_map(
        functools.partial(shards, plan),
        mesh=parted,
        in_specs=in_specs,
        out_specs=out_specs,
        check_vma=False,
    )
```

```python
import functools
import math

import jax
import jax.numpy as jnp
import numpy as np
from jax import lax
from jax.experimental import pallas as pl
from jax.experimental.pallas import tpu as pltpu
from jax.sharding import Mesh
from jax.sharding import PartitionSpec as P

NFFT = 256
HALF = NFFT // 2
NBLK = 63
NB = 64
NF = 64
NM = 8
ITERS = 12
EPS = 1e-06
PART = 32
LEAST_LEFT = 1e-03
LANES = 128
PITCH = 2 * NB + 1
MIB = 1024 * 1024
TRANSFORM_MIB, SOLVE_MIB, MODES_MIB = 28, 8, 8


def dft_table():
    time_steps = np.arange(NFFT, dtype=np.int32)
    freq_bins = np.arange(1, NF + 1, dtype=np.int32)
    wrapped = freq_bins[:, None] * time_steps[None, :] % NFFT
    angles = np.float32(2.0 * math.pi / NFFT) * wrapped.astype(np.float32)
    taper = np.float32(0.5) - np.float32(0.5) * np.cos(
        np.float32(2.0 * math.pi / NFFT) * time_steps.astype(np.float32)
    )
    taper = taper / np.sqrt(np.sum(taper * taper))
    stacked = np.concatenate([np.cos(angles), -np.sin(angles)]) * taper[None, :]
    return jnp.asarray(stacked, dtype=jnp.float32).astype(jnp.bfloat16)


class Plan:
    def __init__(self, grp, row):
        self.grp, self.deep = grp, row // 2
        self.split_grp = NF % (grp * row) == 0
        self.chips = self.deep * (grp if self.split_grp else 1)
        self.chip_axes = ("grp", "z") if self.split_grp else ("z",)
        self.per = NF // (2 * self.chips)
        self.near = self.deep if self.split_grp else 1

    def chip(self):
        z = lax.axis_index("z")
        return lax.axis_index("grp") * self.deep + z if self.split_grp else z

    def first_freq(self):
        return (self.chip() * 2 + lax.axis_index("core")) * self.per

    def half(self, other_core):
        core = lax.axis_index("core") ^ int(other_core)
        return [
            (chip, (2 * chip + core) * self.per + j)
            for chip in range(self.chips)
            for j in range(self.per)
        ]


def lane_index(shape):
    return lax.broadcasted_iota(jnp.int32, shape, 1)


def row_index_of(shape):
    return lax.broadcasted_iota(jnp.int32, shape, 0)


def pack(top, low):
    row = row_index_of((NB, LANES))
    lane = lane_index((NB, LANES))
    left = lane < NB
    upper = row < (lane & (NB - 1))
    parts = jnp.where(left, jnp.where(upper, -low, top), jnp.where(upper, top, low))
    first, second = parts[: NB // 2], parts[NB // 2 :]
    left_half = left[: NB // 2]
    other = pltpu.roll(jnp.where(left_half, second, first), NB, 1)
    return jnp.where(left_half, first, second) + other


def pack_some(plan, other_core, offsets, coef_ref, out_ref):
    core = lax.axis_index("core") ^ int(other_core)
    for n, offset in enumerate(offsets):
        first = (2 * (plan.chip() ^ offset) + core) * plan.per
        for j in range(plan.per):
            coefs = coef_ref[first + j]
            whole = lax.dot_general(
                coefs, coefs, (((1,), (1,)), ((), ())), preferred_element_type=jnp.float32
            )
            out_ref[n * plan.per + j] = pack(whole[:NB], whole[NB:])


def transform_kernel(plan, table_ref, weight_ref, field_ref, snap_ref, coef_ref, send_ref, flip):
    step = pl.program_id(0)
    tile = snap_ref.shape[1]
    pieces = tile // LANES
    table = table_ref[...]
    root = jnp.sqrt(weight_ref[...])
    probe_row = (root * field_ref[...]).astype(jnp.bfloat16).astype(jnp.float32)
    here = pl.ds(pl.multiple_of(step * tile, tile), tile)

    def one_block(b, carry):
        rows = snap_ref[pl.ds(pl.multiple_of(b * HALF, HALF), NFFT), :]
        out = jnp.dot(table, rows, preferred_element_type=jnp.float32) * root
        for part in range(2):
            for piece in range(pieces):
                flip[piece, pl.ds(part * NB + b, NF, stride=PITCH), :] = out[
                    part * NF : (part + 1) * NF, piece * LANES : (piece + 1) * LANES
                ]
        return carry

    lax.fori_loop(0, NBLK, one_block, 0, unroll=NBLK)
    for piece in range(pieces):
        probe = probe_row[:, piece * LANES : (piece + 1) * LANES]
        flip[piece, pl.ds(NB - 1, NF, stride=PITCH), :] = jnp.broadcast_to(probe, (NF, LANES))
        flip[piece, pl.ds(2 * NB - 1, NF, stride=PITCH), :] = jnp.zeros((NF, LANES), jnp.float32)

    def one_freq(f, carry):
        wide = jnp.concatenate(
            [flip[piece, pl.ds(f * PITCH, 2 * NB), :] for piece in range(pieces)], axis=1
        )
        coefs = wide.astype(jnp.bfloat16)
        coef_ref[f, :, here] = coefs
        return carry

    lax.fori_loop(0, NF, one_freq, 0, unroll=NF)

    @pl.when(step == pl.num_programs(0) - 1)
    def _():
        pack_some(plan, True, range(plan.chips), coef_ref, send_ref)


def transform(plan, snapshots, weights, reference_field):
    rows_here = snapshots.shape[1]
    tile = min(256, rows_here)
    small = [
        pltpu.with_memory_space_constraint(x, pltpu.HBM)
        for x in (dft_table(), weights[None], reference_field[None])
    ]
    return pl.pallas_call(
        functools.partial(transform_kernel, plan),
        grid=(rows_here // tile,),
        in_specs=[
            pl.BlockSpec((2 * NF, NFFT), lambda i: (0, 0)),
            pl.BlockSpec((1, tile), lambda i: (0, i)),
            pl.BlockSpec((1, tile), lambda i: (0, i)),
            pl.BlockSpec((snapshots.shape[0], tile), lambda i: (0, i)),
        ],
        out_specs=[pl.BlockSpec(memory_space=pltpu.VMEM)] * 2,
        out_shape=[
            jax.ShapeDtypeStruct((NF, 2 * NB, rows_here), jnp.bfloat16),
            packed_shape(plan, plan.chips),
        ],
        scratch_shapes=[
            pltpu.VMEM((tile // LANES, NF * PITCH, LANES), jnp.float32),
        ],
        compiler_params=pltpu.CompilerParams(vmem_limit_bytes=TRANSFORM_MIB * MIB),
        name="transform",
    )(*small, snapshots)


def packed_shape(plan, chips):
    return jax.ShapeDtypeStruct((chips * plan.per, NB // 2, LANES), jnp.float32)


def grams(plan, coeffs, other_core, offsets, name):
    _, rows, columns = coeffs.shape
    freqs = plan.per * len(offsets)
    return pl.pallas_call(
        functools.partial(pack_some, plan, other_core, offsets),
        in_specs=[pl.BlockSpec(memory_space=pltpu.VMEM)],
        out_specs=pl.BlockSpec(memory_space=pltpu.VMEM),
        out_shape=packed_shape(plan, len(offsets)),
        cost_estimate=pl.CostEstimate(
            flops=2 * freqs * rows * rows * columns,
            bytes_accessed=2 * freqs * rows * columns,
            transcendentals=0,
        ),
        compiler_params=pltpu.CompilerParams(vmem_limit_bytes=SOLVE_MIB * MIB),
        name=name,
    )(coeffs)


def start_kernel(plan, basis_ref, out_ref):
    lane = lane_index((NM, LANES))
    lane_in = lane_index((NM, basis_ref.shape[3]))
    for j in range(plan.per):
        chosen = lane_in == plan.first_freq() + j
        rows = jnp.zeros((NM, LANES), jnp.float32)
        for part in range(2):
            for b in range(NBLK):
                value = jnp.sum(jnp.where(chosen, basis_ref[part, b], 0.0), axis=1, keepdims=True)
                rows = jnp.where(lane == part * NB + b, value, rows)
        out_ref[j] = rows


def start_rows(plan, start_basis):
    return pl.pallas_call(
        functools.partial(start_kernel, plan),
        in_specs=[pl.BlockSpec(memory_space=pltpu.VMEM)],
        out_specs=pl.BlockSpec(memory_space=pltpu.VMEM),
        out_shape=jax.ShapeDtypeStruct((plan.per, NM, LANES), jnp.float32),
        compiler_params=pltpu.CompilerParams(vmem_limit_bytes=SOLVE_MIB * MIB),
        name="start_rows",
    )(jnp.transpose(start_basis, (1, 2, 3, 0)))


def split_three(x):
    high = x.astype(jnp.bfloat16)
    rest = x - high.astype(jnp.float32)
    middle = rest.astype(jnp.bfloat16)
    low = (rest - middle.astype(jnp.float32)).astype(jnp.bfloat16)
    return high, middle, low


def turn(y):
    swapped = pltpu.roll(y, NB, 1)
    return jnp.where(lane_index(y.shape) < NB, -swapped, swapped)


def lane_sum(x):
    return jnp.broadcast_to(jnp.sum(x, axis=1, keepdims=True), x.shape)


def spread(x, j):
    return jnp.broadcast_to(x[j : j + 1], x.shape)


def orthonormalize_checked(y, turned):
    row = row_index_of(y.shape)
    v = jnp.zeros_like(y)
    for j in range(NM):
        pivot, pivot_turned = spread(y, j), spread(turned, j)
        size = lane_sum(pivot * pivot) + EPS
        v = jnp.where(row == j, pivot * lax.rsqrt(size), v)
        if j < NM - 1:
            inverse = 1.0 / size
            a = jnp.where(row > j, lane_sum(pivot * y) * inverse, 0.0)
            c = jnp.where(row > j, lane_sum(pivot_turned * y) * inverse, 0.0)
            y, turned = (
                y - (a * pivot + c * pivot_turned),
                turned - (a * pivot_turned - c * pivot),
            )
    return v


def orthonormalize_quick(y, turned, worst):
    row = row_index_of(y.shape)
    real = [lane_sum(spread(y, j) * y) for j in range(NM)]
    imag = [lane_sum(spread(turned, j) * y) for j in range(NM - 1)]
    whole = [spread(real[j], j) + EPS for j in range(NM)]
    v = jnp.zeros_like(y)
    for j in range(NM):
        pivot, pivot_turned = spread(y, j), spread(turned, j)
        size = jnp.maximum(spread(real[j], j), 0.0) + EPS
        worst = jnp.minimum(worst, size / whole[j])
        v = jnp.where(row == j, pivot * lax.rsqrt(size), v)
        if j < NM - 1:
            inverse = 1.0 / size
            scale = (1.0 + EPS * inverse) * inverse
            for l in range(j + 1, NM):
                other_real, other_imag = spread(real[j], l), spread(imag[j], l)
                both = real[j] * other_real + imag[j] * other_imag
                real[l] = real[l] - scale * both
                if l < NM - 1:
                    cross = imag[j] * other_real - real[j] * other_imag
                    imag[l] = imag[l] - scale * cross
            a = jnp.where(row > j, real[j] * inverse, 0.0)
            c = jnp.where(row > j, imag[j] * inverse, 0.0)
            y, turned = (
                y - (a * pivot + c * pivot_turned),
                turned - (a * pivot_turned - c * pivot),
            )
    return v, worst


def solve_kernel(plan, total_rows, packed_ref, start_ref, out_ref, basis_ref):
    lane = lane_index((NB, LANES))
    row = row_index_of((NB, LANES))
    col = lane & (NB - 1)
    left = lane < NB
    inside = (row < NBLK) & (col < NBLK)
    lane8 = lane_index((NM, LANES))

    systems, probes = [], []
    for i in range(plan.per):
        folded = packed_ref[i]
        turned = pltpu.roll(folded, NB, 1)
        wide = jnp.concatenate([folded, turned], axis=0)
        twice = jnp.where(left, wide, pltpu.roll(wide, NB, 1))
        flipped = jnp.transpose(jnp.concatenate([twice, twice], axis=0))[:NB]
        real = jnp.where(inside, jnp.where(row >= col, twice, flipped), 0.0) / total_rows
        imag = jnp.where(row < col, twice, jnp.where(row > col, -flipped, 0.0))
        imag = jnp.where(inside, imag, 0.0) / total_rows
        straight = jnp.concatenate(
            [jnp.where(left, real, -imag), jnp.where(left, imag, real)], axis=0
        )
        sides = []
        for system in (straight, turn(straight)):
            high, middle, low = split_three(system)
            sides.append(
                jnp.concatenate(
                    [
                        jnp.concatenate([high, low], axis=1),
                        jnp.concatenate([middle, jnp.zeros_like(low)], axis=1),
                    ],
                    axis=0,
                )
            )
        systems.append(jnp.concatenate(sides, axis=1))
        along = twice[NB - 1 :]
        across = flipped[NB - 1 :]
        left1 = lane_index((1, LANES)) < NB
        probes.append((jnp.where(left1, along, across), jnp.where(left1, -across, along)))

    def image_of(i, v):
        high, middle, low = split_three(v)
        zeros = jnp.zeros_like(high)
        parts = jnp.concatenate(
            [
                jnp.concatenate([high, high], axis=1),
                jnp.concatenate([middle, middle], axis=1),
                jnp.concatenate([low, zeros], axis=1),
                jnp.concatenate([zeros, zeros], axis=1),
            ],
            axis=0,
        )
        out = jnp.dot(parts, systems[i], preferred_element_type=jnp.float32)

        def total(out):
            small = out[:NM, LANES:] + out[2 * NM : 3 * NM, :LANES]
            return out[:NM, :LANES] + (out[NM : 2 * NM, :LANES] + small)

        return total(out[:, : 2 * LANES]), total(out[:, 2 * LANES :])

    start = tuple(start_ref[i] for i in range(plan.per))

    def quick_sweep(index, carry):
        current, worst = carry
        images = [image_of(i, v) for i, v in enumerate(current)]
        done = []
        for y, turned in images:
            v, worst = orthonormalize_quick(y, turned, worst)
            done.append(v)
        return tuple(done), worst

    def checked_sweep(index, current):
        images = [image_of(i, v) for i, v in enumerate(current)]
        return tuple(orthonormalize_checked(y, turned) for y, turned in images)

    basis, worst = lax.fori_loop(
        0, ITERS, quick_sweep, (start, jnp.ones((NM, LANES), jnp.float32)), unroll=4
    )
    for i, v in enumerate(basis):
        basis_ref[i] = v

    @pl.when(jnp.logical_not(jnp.min(worst) >= LEAST_LEFT))
    def _():
        for i, v in enumerate(lax.fori_loop(0, ITERS, checked_sweep, start)):
            basis_ref[i] = v

    rows = []
    extras = jnp.zeros((NM, LANES), jnp.float32)
    scale = 1.0 / math.sqrt(total_rows)
    for i in range(plan.per):
        v = basis_ref[i]
        energy = lane_sum(v * image_of(i, v)[0])
        coef = v.astype(jnp.bfloat16).astype(jnp.float32)
        rows.append(coef)
        gain = 1.0 / jnp.sqrt(energy + EPS)
        tilt_real = gain * (lane_sum(coef * probes[i][0]) * scale)
        tilt_imag = gain * (lane_sum(coef * probes[i][1]) * scale)
        size = jnp.sqrt(jnp.maximum(tilt_real * tilt_real + tilt_imag * tilt_imag, 0.25))
        extras = jnp.where(lane8 == 3 * i, gain * tilt_real / size, extras)
        extras = jnp.where(lane8 == 3 * i + 1, -gain * tilt_imag / size, extras)
        extras = jnp.where(lane8 == 3 * i + 2, energy, extras)
    high, middle, low = (part.astype(jnp.float32) for part in split_three(extras))
    apart = high + pltpu.roll(middle, PART, 1) + pltpu.roll(low, 2 * PART, 1)
    rows += [apart, jnp.zeros_like(apart)]
    out_ref[...] = jnp.concatenate(rows, axis=0).astype(jnp.bfloat16)


def solve(plan, total_rows, packed, start):
    return pl.pallas_call(
        functools.partial(solve_kernel, plan, total_rows),
        in_specs=[pl.BlockSpec(memory_space=pltpu.VMEM)] * 2,
        out_specs=pl.BlockSpec(memory_space=pltpu.VMEM),
        out_shape=jax.ShapeDtypeStruct(((plan.per + 2) * NM, LANES), jnp.bfloat16),
        scratch_shapes=[pltpu.VMEM((plan.per, NM, LANES), jnp.float32)],
        compiler_params=pltpu.CompilerParams(vmem_limit_bytes=SOLVE_MIB * MIB),
        name="solve",
    )(packed, start)


def modes_kernel(plan, other_core, coef_ref, pay_ref, weight_ref, *refs):
    out_hbm, energy_ref, out, sems = refs[-4:]
    inverse_root = 1.0 / jnp.sqrt(weight_ref[...])
    lane8 = lane_index((NM, LANES))
    left = lane8 < NB
    energies = jnp.zeros((NM, LANES), jnp.float32)
    copies = []
    for n, (chip, f) in enumerate(plan.half(other_core)):
        j = n % plan.per
        if j == 0:
            whole_pay = pay_ref[chip].astype(jnp.float32)
            apart = whole_pay[plan.per * NM : (plan.per + 1) * NM]
            extras = apart + (
                pltpu.roll(apart, LANES - PART, 1) + pltpu.roll(apart, LANES - 2 * PART, 1)
            )
        c = whole_pay[j * NM : (j + 1) * NM]
        factor_real = extras[:, 3 * j : 3 * j + 1]
        factor_imag = extras[:, 3 * j + 1 : 3 * j + 2]
        matrix = jnp.concatenate([jnp.where(left, c, -c), pltpu.roll(c, NB, 1)], axis=0)
        projected = jnp.dot(
            matrix.astype(jnp.bfloat16), coef_ref[f], preferred_element_type=jnp.float32
        )
        real = projected[:NM]
        imag = projected[NM:]
        out[n, :NM, :] = (real * factor_real - imag * factor_imag) * inverse_root
        out[n, NM:, :] = (real * factor_imag + imag * factor_real) * inverse_root
        energies = jnp.where(lane8 == f, extras[:, 3 * j + 2 : 3 * j + 3], energies)
        if j == plan.per - 1:
            copy = pltpu.make_async_copy(
                out.at[pl.ds(n - j, plan.per)],
                out_hbm.at[pl.ds(f - j, plan.per)],
                sems.at[len(copies)],
            )
            copy.start()
            copies.append(copy)
    energies = energies[:, :NF]
    energy_ref[...] = energies + refs[1][...] if other_core else energies
    for copy in copies:
        copy.wait()


def modes(plan, coeffs, payload, weights, earlier=()):
    rows_here = coeffs.shape[2]
    whole = jax.ShapeDtypeStruct((NF, 2 * NM, rows_here), jnp.float32)
    places = [pltpu.HBM, pltpu.VMEM]
    return pl.pallas_call(
        functools.partial(modes_kernel, plan, bool(earlier)),
        in_specs=[pl.BlockSpec(memory_space=pltpu.VMEM)] * 3
        + [pl.BlockSpec(memory_space=place) for place in places[: len(earlier)]],
        out_specs=[pl.BlockSpec(memory_space=place) for place in places],
        out_shape=[whole, jax.ShapeDtypeStruct((NM, NF), jnp.float32)],
        input_output_aliases={3: 0} if earlier else {},
        scratch_shapes=[
            pltpu.VMEM((NF // 2,) + whole.shape[1:], whole.dtype),
            pltpu.SemaphoreType.DMA((plan.chips,)),
        ],
        cost_estimate=pl.CostEstimate(
            flops=2 * NF * NM * 2 * NB * rows_here,
            bytes_accessed=2 * NF * NM * 4 * rows_here,
            transcendentals=0,
        ),
        compiler_params=pltpu.CompilerParams(vmem_limit_bytes=MODES_MIB * MIB),
        name="other_modes" if earlier else "own_modes",
    )(coeffs, payload, weights[None], *earlier)


def swap(x, axis, size, offset):
    return lax.ppermute(x, axis, [(i, i ^ offset) for i in range(size)])


def shards(plan, snapshots, weights, reference_field, start_basis):
    total_rows = snapshots.shape[1] * plan.grp * plan.deep * 2
    coeffs, send = transform(plan, snapshots, weights, reference_field)
    start_basis, send = lax.optimization_barrier((start_basis, send))
    start = start_rows(plan, start_basis)

    arrived = swap(send, "core", 2, 1)
    mine, near = arrived[: plan.near * plan.per], range(plan.near)
    own = grams(plan, coeffs, False, range(plan.near, plan.chips), "own_gram")
    held = own + arrived[plan.near * plan.per :]
    late, held = lax.optimization_barrier((coeffs, held))
    if plan.split_grp:
        held = held.reshape((plan.grp - 1, plan.deep * plan.per) + held.shape[1:])
        arrived = [swap(held[d - 1], "grp", plan.grp, d) for d in range(1, plan.grp)]
    else:
        held = held.reshape((plan.deep - 1, plan.per) + held.shape[1:])
        arrived = [swap(held[d - 1], "z", plan.deep, d) for d in range(1, plan.deep)]
    held = functools.reduce(jnp.add, arrived, grams(plan, late, False, near, "near_gram") + mine)
    if plan.split_grp:
        held = held.reshape((plan.deep, plan.per) + held.shape[1:])
        arrived = [swap(held[d], "z", plan.deep, d) for d in range(1, plan.deep)]
        held = functools.reduce(jnp.add, arrived, held[0])
    else:
        held = lax.psum(held, "grp")

    payload = solve(plan, total_rows, held, start)
    payload = jnp.broadcast_to(payload, (plan.chips,) + payload.shape)
    payload = lax.all_to_all(payload, plan.chip_axes, 0, 0, tiled=True)
    far = swap(payload, "core", 2, 1)
    own = modes(plan, coeffs, payload, weights)
    spod_modes, energies = modes(plan, coeffs, far, weights, own)
    return spod_modes, jnp.transpose(energies)


def solution(mesh):
    plan = Plan(mesh.shape["grp"], mesh.shape["row"])
    parted = Mesh(mesh.devices.reshape(plan.grp, plan.deep, 2), ("grp", "z", "core"))
    rows = ("grp", "z", "core")
    in_specs = (P(None, rows), P(rows), P(rows), P())
    out_specs = (P(None, None, rows), P())
    return jax.shard_map(
        functools.partial(shards, plan),
        mesh=parted,
        in_specs=in_specs,
        out_specs=out_specs,
        check_vma=False,
    )
```
